32 devices in a mesh: group: 2 (over y), row: 4 (over z), col: 4 (over x, core).
Axes of the slice: x: 2, y: 2, z: 4, core: 2. Of those that a mesh axis runs over, the one named last changes fastest.
Arguments:
- pair: bfloat16 [1024, 512, 128], P(('group', 'row'), 'col'), parts along dimension 0, may hold values from -6 to 6
- chain: int32 [8], P('group'), parts along dimension 0, may hold values from 0 to 2
- block_mask: int32 [8, 4], P('group'), parts along dimension 0, may hold values 0 or 1
- w_in: bfloat16 [2, 128, 256], replicated, may hold values from -0.5 to 0.5
- w_gate: bfloat16 [2, 128, 128], replicated, may hold values from -0.5 to 0.5
- w_out: bfloat16 [2, 64, 128], replicated, may hold values from -0.75 to 0.75
- gain_in: float32 [2, 128], replicated, may hold values from 0.1 to 1.9
- gain_out: float32 [2, 64], replicated, may hold values from 0.1 to 1.9
Outputs:
- updated: bfloat16 [1024, 512, 128], P(('group', 'row'), 'col'), parts along dimension 0
The draws below stay inside these ranges and needn't reach their ends.
There are 2 independent parts, one for each index of `group`. The reference program is written for one: setup_inputs(seed, part) draws one part's arguments, and reference() takes and returns one part's arrays. A program takes and returns all parts, laid end to end along the dimension named above; an argument that names none is the same for every part. Nothing has to cross between parts.
All inputs are finite; a program needn't handle non-finite values.
Results may differ from the reference program's by a relative error of at most 0.014.
Values may be sent and summed in bfloat16 or wider, within the bound.
No kernel may reach another device: no remote copies, remote signals or barrier semaphores. Data moves between devices by JAX's collectives and lax.ppermute only.
A program may use at most 128 MiB of HBM per device.

```python
import jax
import jax.numpy as jnp
from jax import lax

C = 128
CH = 64
BLOCK = 128
NB = 4
N = 512


def set_ends(array, key, least, high):
    extent = array.shape
    place = [jax.random.randint(jax.random.fold_in(key, axis), (), 0, extent[axis]) for axis in range(len(extent))]
    array = array.at[tuple(place)].set(least)
    longest = extent.index(max(extent))
    place[longest] = (place[longest] + 1) % extent[longest]
    return array.at[tuple(place)].set(high)


def shard_levels(own_key, extent, split, smallest, top_value):
    level = 1.0
    for position, shards_of in split:
        heights = jax.random.uniform(jax.random.fold_in(jax.random.fold_in(own_key, 6), position), (shards_of,), jnp.float32, smallest / len(split), top_value / len(split))
        level = level * jnp.repeat(jnp.exp(heights), extent[position] // shards_of).reshape((-1,) + (1,) * (len(extent) - 1 - position))
    return level


def bell_draw(stream_key, extent, scale, limit, split=(), dtype=jnp.bfloat16):
    drawn = scale * jax.random.normal(stream_key, extent, jnp.float32)
    if split:
        drawn = drawn * shard_levels(stream_key, extent, split, -0.22, 0.18)
    return jnp.clip(drawn, -limit, limit).astype(dtype)


def setup_inputs(seed: int = 0, part: int = 0) -> dict:
    arg_keys = jax.random.split(jax.random.key(seed), 9)
    part_splits = jax.random.split(jax.random.fold_in(arg_keys[8], part), 9)
    pair = bell_draw(part_splits[0], (N, N, C), 1.0, 6.0, ((0, 4), (1, 4)))
    chain = set_ends(jax.random.randint(part_splits[1], (NB,), 0, 3), jax.random.fold_in(part_splits[1], 1), 0, 2).astype(jnp.int32)
    block_mask = set_ends((jax.random.randint(part_splits[2], (NB, NB), 0, 2) < 1).astype(jnp.int32), jax.random.fold_in(part_splits[2], 1), 0, 1)
    w_in = bell_draw(arg_keys[3], (2, C, 4 * CH), C ** -0.5, 0.5)
    w_gate = bell_draw(arg_keys[4], (2, C, C), C ** -0.5, 0.5)
    w_out = bell_draw(arg_keys[5], (2, CH, C), CH ** -0.5, 0.75)
    gain_in = jnp.clip(1.0 + 0.18 * jax.random.normal(arg_keys[6], (2, C), jnp.float32), 0.1, 1.9)
    gain_out = jnp.clip(1.0 + 0.18 * jax.random.normal(arg_keys[7], (2, CH), jnp.float32), 0.1, 1.9)
    return {"pair": pair, "chain": chain, "block_mask": block_mask, "w_in": w_in, "w_gate": w_gate, "w_out": w_out, "gain_in": gain_in, "gain_out": gain_out}


def layer_norm(values, gain):
    mean = lax.optimization_barrier(jnp.mean(values, -1, keepdims=True))
    centred = values - mean
    spread = lax.optimization_barrier(jnp.mean(centred * centred, -1, keepdims=True))
    return centred * lax.rsqrt(spread + 1e-05) * gain

def project(pair, mask_full, w_in, w_gate, gain_in):
    normed = layer_norm(pair.astype(jnp.float32), gain_in).astype(jnp.bfloat16)
    hidden = jnp.dot(normed, w_in, preferred_element_type=jnp.float32)
    width = w_in.shape[1] // 4
    masked = mask_full[..., None]
    left = (masked * jax.nn.sigmoid(hidden[..., width:2 * width]) * hidden[..., :width]).astype(jnp.bfloat16)
    right = (masked * jax.nn.sigmoid(hidden[..., 3 * width:]) * hidden[..., 2 * width:3 * width]).astype(jnp.bfloat16)
    gate = jax.nn.sigmoid(jnp.dot(normed, w_gate, preferred_element_type=jnp.float32))
    return (left, right, gate)

def finish(pair, product, gate, w_out, gain_out):
    update = layer_norm(product, gain_out).astype(jnp.bfloat16)
    return (pair.astype(jnp.float32) + gate * jnp.dot(update, w_out, preferred_element_type=jnp.float32)).astype(jnp.bfloat16)

def reference(pair, chain, block_mask, w_in, w_gate, w_out, gain_in, gain_out):
    same = chain[:, None] == chain[None, :]
    blocks = jnp.where(same | (block_mask == 1), 1.0, 0.0).astype(jnp.float32)
    mask_full = jnp.repeat(jnp.repeat(blocks, BLOCK, 0), BLOCK, 1)
    left, right, gate = project(pair, mask_full, w_in[0], w_gate[0], gain_in[0])
    product = jnp.einsum('ikc,jkc->ijc', left.astype(jnp.float32), right.astype(jnp.float32))
    middle = finish(pair, product, gate, w_out[0], gain_out[0])
    left, right, gate = project(middle, mask_full, w_in[1], w_gate[1], gain_in[1])
    product = jnp.einsum('kic,kjc->ijc', left.astype(jnp.float32), right.astype(jnp.float32))
    return finish(middle, product, gate, w_out[1], gain_out[1])
```

```python
import functools

import jax
import jax.numpy as jnp
from jax import lax
from jax.experimental import pallas as pl
from jax.experimental.pallas import tpu as pltpu
from jax.sharding import PartitionSpec as P

BLOCK = 128
EPS = 1e-05
CHUNKS = 4
STEP = 16
VMEM = 48 * 1024 * 1024


def broadcast(block, axis, owner):
    block = jnp.where(lax.axis_index(axis) == owner, block, jnp.zeros_like(block))
    return lax.psum(block, axis)


def layer_norm(values, gain):
    mean = jnp.mean(values, -1, keepdims=True)
    centred = values - mean
    spread = jnp.mean(centred * centred, -1, keepdims=True)
    return centred * lax.rsqrt(spread + EPS) * gain


def project(pair, tile_mask, w_in, w_gate, gain_in):
    normed = layer_norm(pair.astype(jnp.float32), gain_in).astype(jnp.bfloat16)
    hidden = jnp.dot(normed, w_in, preferred_element_type=jnp.float32)
    width = w_in.shape[1] // 4
    masked = tile_mask[..., None]
    left = (masked * jax.nn.sigmoid(hidden[..., width : 2 * width]) * hidden[..., :width]).astype(
        jnp.bfloat16
    )
    right = (
        masked * jax.nn.sigmoid(hidden[..., 3 * width :]) * hidden[..., 2 * width : 3 * width]
    ).astype(jnp.bfloat16)
    gate = jax.nn.sigmoid(jnp.dot(normed, w_gate, preferred_element_type=jnp.float32))
    return (left, right, gate)


def finish(pair, product, gate, w_out, gain_out):
    update = layer_norm(product, gain_out).astype(jnp.bfloat16)
    return (
        pair.astype(jnp.float32) + gate * jnp.dot(update, w_out, preferred_element_type=jnp.float32)
    ).astype(jnp.bfloat16)


def any_mesh(pair, chain, block_mask, w_in, w_gate, w_out, gain_in, gain_out):
    tile_rows = pair.shape[0]
    tile_cols = pair.shape[1]
    block_count = chain.shape[0]
    ratio = lax.axis_size("row") // lax.axis_size("col")
    row_index = lax.axis_index("row")
    col_index = lax.axis_index("col")
    same = chain[:, None] == chain[None, :]
    blocks = jnp.where(same | (block_mask == 1), 1.0, 0.0).astype(jnp.float32)
    labels = jnp.arange(block_count, dtype=jnp.int32)
    row_blocks = (row_index * tile_rows + jnp.arange(tile_rows, dtype=jnp.int32)) // BLOCK
    col_blocks = (col_index * tile_cols + jnp.arange(tile_cols, dtype=jnp.int32)) // BLOCK
    row_onehot = jnp.where(row_blocks[:, None] == labels[None, :], 1.0, 0.0).astype(jnp.float32)
    col_onehot = jnp.where(col_blocks[:, None] == labels[None, :], 1.0, 0.0).astype(jnp.float32)
    tile_mask = jnp.dot(jnp.dot(row_onehot, blocks), col_onehot.T)
    left, right, gate = project(pair, tile_mask, w_in[0], w_gate[0], gain_in[0])
    partial_terms = jnp.einsum(
        "ikc,jkc->ijc",
        left,
        lax.all_gather(right, "row", axis=0, tiled=True),
        preferred_element_type=jnp.float32,
    )
    product = lax.psum_scatter(
        partial_terms.astype(jnp.bfloat16), "col", scatter_dimension=1, tiled=True
    ).astype(jnp.float32)
    middle = finish(pair, product, gate, w_out[0], gain_out[0])
    left, right, gate = project(middle, tile_mask, w_in[1], w_gate[1], gain_in[1])
    left_cols = lax.all_gather(left, "row", axis=0, tiled=True)
    start_col = row_index % ratio * tile_rows
    left_slice = lax.dynamic_slice_in_dim(left_cols, start_col, tile_rows, 1)
    left_mine = broadcast(left_slice, "col", row_index // ratio)
    product = jnp.einsum(
        "kic,kjc->ijc",
        left_mine,
        lax.all_gather(right, "row", axis=0, tiled=True),
        preferred_element_type=jnp.float32,
    )
    return finish(middle, product, gate, w_out[1], gain_out[1])


NT = (((1,), (1,)), ((), ()))
TN = (((0,), (0,)), ((), ()))
SMEM_SPEC = pl.BlockSpec(memory_space=pltpu.SMEM)


def dot(a, b, dims=(((1,), (0,)), ((), ()))):
    return lax.dot_general(a, b, dims, preferred_element_type=jnp.float32)


def norm_rows(rows, gain, mean_of):
    values = rows.astype(jnp.float32)
    centred = values - dot(rows, mean_of)
    square = centred * centred
    high = square.astype(jnp.bfloat16)
    low = (square - high.astype(jnp.float32)).astype(jnp.bfloat16)
    spread = dot(high, mean_of) + dot(low, mean_of)
    return (centred * lax.rsqrt(spread + EPS) * gain).astype(jnp.bfloat16)


def logistic(values):
    return 0.5 * jnp.tanh(0.5 * values) + 0.5


def project_rows(normed, mask, w_t, scratch, left_refs, right_refs, half):
    hidden = dot(w_t, normed, NT)
    width = w_t.shape[0] // 4
    cols = normed.shape[0] // STEP
    chunks = len(left_refs)
    for side, refs in enumerate((left_refs, right_refs)):
        values = hidden[2 * side * width : (2 * side + 1) * width]
        gates = hidden[(2 * side + 1) * width : (2 * side + 2) * width]
        kept = mask * logistic(gates) * values
        for row in range(STEP):
            scratch[side, pl.ds(row, width, stride=STEP), :] = kept[:, row * cols : (row + 1) * cols]
        span = width // chunks
        for n, ref in enumerate(refs):
            block = scratch[side, n * span * STEP : (n + 1) * span * STEP, :]
            ref[...] = block.astype(jnp.bfloat16).reshape(ref.shape)


def project_kernel(chunks, mask_ref, pair_ref, w_t_ref, gain_ref, mean_ref, *rest):
    left_refs, right_refs, scratch = rest[:chunks], rest[chunks : 2 * chunks], rest[2 * chunks]
    rows = pair_ref[...].reshape(-1, pair_ref.shape[-1])
    normed = norm_rows(rows, gain_ref[...], mean_ref[...])
    project_rows(normed, mask_ref[0], w_t_ref[...], scratch, left_refs, right_refs, None)


def gate_kernel(pair_ref, w_ref, gain_ref, mean_ref, out_ref):
    rows = pair_ref[...].reshape(-1, pair_ref.shape[-1])
    normed = norm_rows(rows, gain_ref[...], mean_ref[...])
    gate = logistic(dot(normed, w_ref[...]))
    out_ref[...] = gate.astype(out_ref.dtype).reshape(out_ref.shape)


def finish_rows(pair_ref, gate_ref, product_refs, w_out_ref, gain_ref, scratch, out_ref):
    width = w_out_ref.shape[0]
    cols = pair_ref.shape[1]
    parts = [ref[...].reshape(-1, STEP, cols) for ref in product_refs]
    product = jnp.concatenate(parts, 0).astype(jnp.float32)
    mean = jnp.sum(product, 0, keepdims=True) * (1.0 / width)
    centred = product - mean
    spread = jnp.sum(centred * centred, 0, keepdims=True) * (1.0 / width)
    update = centred * lax.rsqrt(spread + EPS) * gain_ref[...]
    scratch[...] = update.reshape(width * STEP, cols)
    w_out = w_out_ref[...]
    for row in range(STEP):
        mine = scratch[pl.ds(row, width, stride=STEP), :].astype(jnp.bfloat16)
        change = dot(mine, w_out, TN)
        gate = gate_ref[row].astype(jnp.float32)
        out_ref[row] = (pair_ref[row].astype(jnp.float32) + gate * change).astype(jnp.bfloat16)


def finish_kernel(chunks, pair_ref, gate_ref, w_out_ref, gain_ref, *rest):
    product_refs, out_ref, scratch = rest[:chunks], rest[chunks], rest[chunks + 1]
    finish_rows(pair_ref, gate_ref, product_refs, w_out_ref, gain_ref, scratch, out_ref)


def middle_kernel(
    chunks, mask_ref, pair_ref, gate_ref, w_out_ref, gain_out_ref, w_t_ref, gain_in_ref, mean_ref, *rest
):
    product_refs, rest = rest[:chunks], rest[chunks:]
    out_ref, rest = rest[0], rest[1:]
    left_refs, right_refs = rest[:chunks], rest[chunks : 2 * chunks]
    update_scratch, scratch = rest[2 * chunks :]
    finish_rows(pair_ref, gate_ref, product_refs, w_out_ref, gain_out_ref, update_scratch, out_ref)
    rows = out_ref[...].reshape(-1, out_ref.shape[-1])
    normed = norm_rows(rows, gain_in_ref[...], mean_ref[...])
    project_rows(normed, mask_ref[0], w_t_ref[...], scratch, left_refs, right_refs, None)


def outgoing_kernel(row_ref, left, right, left_pair, right_pair, right_far, right_near, own_ref, pair_ref):
    def wide(ref):
        return jnp.concatenate([ref[k, 0] for k in range(ref.shape[0])], 1)

    size = left.shape[-1]
    lefts = jnp.concatenate([wide(left), wide(left_pair)], 0)
    for step, ref in ((0, right), (1, right_pair), (3, right_near), (2, right_far)):
        terms = dot(lefts, wide(ref), NT).astype(jnp.bfloat16)
        place = row_ref[0] ^ step
        own_ref[place, 0] = terms[:size]
        pair_ref[place, 0] = terms[size:]


def incoming_kernel(row_ref, left, right, left_pair, right_pair, *outs):
    def wide(ref):
        return jnp.concatenate([ref[j, 0] for j in range(ref.shape[0])], 1)

    size = left.shape[-1]
    rights = jnp.concatenate([wide(right), wide(right_pair)], 0)
    for step, out in enumerate(outs):
        place = row_ref[0] ^ step
        lefts = jnp.concatenate([left[place, 0], left_pair[place, 0]], 0)
        terms = dot(lefts, rights, TN).astype(jnp.bfloat16)
        for j in range(out.shape[0]):
            out[j, 0] = terms[:, j * size : (j + 1) * size]


def params():
    return pltpu.CompilerParams(vmem_limit_bytes=VMEM, dimension_semantics=("arbitrary",))


def whole(array):
    return pl.BlockSpec(array.shape, lambda *_: (0,) * array.ndim)


def tile_spec(tile):
    return pl.BlockSpec((STEP,) + tile.shape[1:], lambda r: (r, 0, 0))


def chunk_spec(shape):
    return pl.BlockSpec(shape[:2] + (STEP, shape[3]), lambda r: (0, 0, r, 0))


def cost(flops, nbytes, special=0):
    return pl.CostEstimate(flops=int(flops), bytes_accessed=int(nbytes), transcendentals=int(special))


def project_call(pair, mask, w_t, gain, mean_of, chunk):
    rows, cols, _ = pair.shape
    width = w_t.shape[0] // 4
    outs = [jax.ShapeDtypeStruct(chunk, jnp.bfloat16)] * (2 * CHUNKS)
    result = pl.pallas_call(
        functools.partial(project_kernel, CHUNKS),
        grid=(rows // STEP,),
        in_specs=[SMEM_SPEC, tile_spec(pair), whole(w_t), whole(gain), whole(mean_of)],
        out_specs=[chunk_spec(chunk)] * (2 * CHUNKS),
        out_shape=outs,
        scratch_shapes=[pltpu.VMEM((2, width * STEP, cols), jnp.float32)],
        compiler_params=params(),
        cost_estimate=cost(2e9, 8 << 20, 4 << 20),
        name="project",
    )(mask, pair, w_t, gain, mean_of)
    return result[:CHUNKS], result[CHUNKS:]


def gate_call(pair, w, gain, mean_of):
    return pl.pallas_call(
        gate_kernel,
        grid=(pair.shape[0] // STEP,),
        in_specs=[tile_spec(pair), whole(w), whole(gain), whole(mean_of)],
        out_specs=tile_spec(pair),
        out_shape=jax.ShapeDtypeStruct(pair.shape, jnp.bfloat16),
        compiler_params=params(),
        cost_estimate=cost(2e9, 8 << 20, 4 << 20),
        name="gate",
    )(pair, w, gain, mean_of)


def finish_call(pair, gate, products, w_out, gain):
    rows, cols, _ = pair.shape
    width = w_out.shape[0]
    return pl.pallas_call(
        functools.partial(finish_kernel, CHUNKS),
        grid=(rows // STEP,),
        in_specs=[tile_spec(pair), tile_spec(gate), whole(w_out), whole(gain)]
        + [chunk_spec(p.shape) for p in products],
        out_specs=tile_spec(pair),
        out_shape=jax.ShapeDtypeStruct(pair.shape, pair.dtype),
        scratch_shapes=[pltpu.VMEM((width * STEP, cols), jnp.float32)],
        compiler_params=params(),
        cost_estimate=cost(1e9, 14 << 20, 4 << 20),
        name="finish",
    )(pair, gate, w_out, gain, *products)


def middle_call(mask, pair, gate, products, w_out, gain_out, w_t, gain_in, mean_of, chunk):
    rows, cols, _ = pair.shape
    width = w_out.shape[0]
    outs = [jax.ShapeDtypeStruct(chunk, jnp.bfloat16)] * (2 * CHUNKS)
    result = pl.pallas_call(
        functools.partial(middle_kernel, CHUNKS),
        grid=(rows // STEP,),
        in_specs=[SMEM_SPEC, tile_spec(pair), tile_spec(gate), whole(w_out), whole(gain_out)]
        + [whole(w_t), whole(gain_in), whole(mean_of)]
        + [chunk_spec(p.shape) for p in products],
        out_specs=[tile_spec(pair)] + [chunk_spec(chunk)] * (2 * CHUNKS),
        out_shape=[jax.ShapeDtypeStruct(pair.shape, pair.dtype)] + outs,
        scratch_shapes=[
            pltpu.VMEM((width * STEP, cols), jnp.float32),
            pltpu.VMEM((2, width * STEP, cols), jnp.float32),
        ],
        compiler_params=params(),
        cost_estimate=cost(3e9, 18 << 20, 8 << 20),
        name="middle",
    )(mask, pair, gate, w_out, gain_out, w_t, gain_in, mean_of, *products)
    return result[0], result[1 : 1 + CHUNKS], result[1 + CHUNKS :]


def product_call(kernel, row, operands, count, name):
    blocks, channels, size, _ = operands[0].shape
    spec = pl.BlockSpec((blocks, 1, size, size), lambda c: (0, c, 0, 0))
    return pl.pallas_call(
        kernel,
        grid=(channels,),
        in_specs=[SMEM_SPEC] + [spec] * len(operands),
        out_specs=[spec] * count,
        out_shape=[jax.ShapeDtypeStruct(operands[0].shape, jnp.bfloat16)] * count,
        compiler_params=params(),
        cost_estimate=cost(
            channels * 2 * 2 * (4 * size) ** 2 * size, operands[0].size * 2 * (len(operands) + count)
        ),
        name=name,
    )(row, *operands)


def hop(array, pairs, groups):
    return lax.ppermute(array, "row", pairs)


INWARD = [(0, 1), (3, 2)]
OUTWARD = [(1, 0), (2, 3)]
ACROSS = [(1, 2), (2, 1)]


def exchange(array):
    return lax.all_to_all(array, "col", 0, 0, tiled=True)


def four_by_four(pair, chain, block_mask, w_in, w_gate, w_out, gain_in, gain_out):
    size = pair.shape[0]
    channels = pair.shape[2]
    width = w_out.shape[1]
    row = lax.axis_index("row")
    col = lax.axis_index("col")
    same = chain[row] == chain[col]
    mask = jnp.where(same | (block_mask[row, col] == 1), 1.0, 0.0).astype(jnp.float32)[None]
    row_arg = row.astype(jnp.int32)[None]
    inner = (row == 1) | (row == 2)
    w_t = jnp.swapaxes(w_in, 1, 2)
    mean_of = jnp.full((channels, channels), 1.0 / channels, jnp.bfloat16)
    gain_wide = jnp.broadcast_to(gain_out[:, :, None, None], gain_out.shape + (1, pair.shape[1]))
    chunk = (4, width // (4 * CHUNKS), size, size)

    def select(own, moved):
        return jnp.where(inner, own, moved)

    lefts, rights = project_call(pair, mask, w_t[0], gain_in[0][None], mean_of, chunk)
    gate = gate_call(pair, w_gate[0], gain_in[0][None], mean_of)
    products = []
    for left, right in zip(lefts, rights):
        right = exchange(right)
        left = exchange(left)
        right_pair = hop(right, INWARD, None)
        right_near = hop(right, ACROSS, None)
        left_pair = hop(left, INWARD, None)
        right_far = hop(right_pair, ACROSS, None)
        own, other = product_call(
            outgoing_kernel,
            row_arg,
            (left, right, left_pair, right_pair, right_far, right_near),
            2,
            "outgoing",
        )
        products.append(exchange(select(own, hop(other, OUTWARD, None))))
    middle, lefts, rights = middle_call(
        mask, pair, gate, products, w_out[0], gain_wide[0], w_t[1], gain_in[1][None], mean_of, chunk
    )
    gate = gate_call(middle, w_gate[1], gain_in[1][None], mean_of)
    products = []
    for left, right in zip(lefts, rights):
        right = exchange(right)
        left = exchange(left)
        right_pair = hop(right, INWARD, None)
        left_pair = hop(left, INWARD, None)
        own, other, far, near = product_call(
            incoming_kernel, row_arg, (left, right, left_pair, right_pair), 4, "incoming"
        )
        other = other + hop(far, ACROSS, None)
        own = own + hop(near, ACROSS, None)
        products.append(exchange(select(own, hop(other, OUTWARD, None))))
    return finish_call(middle, gate, products, w_out[1], gain_wide[1])


def solution(mesh):
    four = mesh.shape["row"] == 4 and mesh.shape["col"] == 4
    return jax.shard_map(
        four_by_four if four else any_mesh,
        mesh=mesh,
        in_specs=(
            P(("group", "row"), "col", None),
            P("group"),
            P("group", None),
            P(),
            P(),
            P(),
            P(),
            P(),
        ),
        out_specs=P(("group", "row"), "col", None),
        check_vma=False,
    )
```

```python
import functools

import jax
import jax.numpy as jnp
from jax import lax
from jax.experimental import pallas as pl
from jax.experimental.pallas import tpu as pltpu
from jax.sharding import PartitionSpec as P

BLOCK = 128
EPS = 1e-05
SIZES = (12, 12, 8)
STEP = 16
VMEM = 48 * 1024 * 1024


def broadcast(block, axis, owner):
    block = jnp.where(lax.axis_index(axis) == owner, block, jnp.zeros_like(block))
    return lax.psum(block, axis)


def layer_norm(values, gain):
    mean = jnp.mean(values, -1, keepdims=True)
    centred = values - mean
    spread = jnp.mean(centred * centred, -1, keepdims=True)
    return centred * lax.rsqrt(spread + EPS) * gain


def project(pair, tile_mask, w_in, w_gate, gain_in):
    normed = layer_norm(pair.astype(jnp.float32), gain_in).astype(jnp.bfloat16)
    hidden = jnp.dot(normed, w_in, preferred_element_type=jnp.float32)
    width = w_in.shape[1] // 4
    masked = tile_mask[..., None]
    left = (masked * jax.nn.sigmoid(hidden[..., width : 2 * width]) * hidden[..., :width]).astype(
        jnp.bfloat16
    )
    right = (
        masked * jax.nn.sigmoid(hidden[..., 3 * width :]) * hidden[..., 2 * width : 3 * width]
    ).astype(jnp.bfloat16)
    gate = jax.nn.sigmoid(jnp.dot(normed, w_gate, preferred_element_type=jnp.float32))
    return (left, right, gate)


def finish(pair, product, gate, w_out, gain_out):
    update = layer_norm(product, gain_out).astype(jnp.bfloat16)
    return (
        pair.astype(jnp.float32) + gate * jnp.dot(update, w_out, preferred_element_type=jnp.float32)
    ).astype(jnp.bfloat16)


def any_mesh(pair, chain, block_mask, w_in, w_gate, w_out, gain_in, gain_out):
    tile_rows = pair.shape[0]
    tile_cols = pair.shape[1]
    block_count = chain.shape[0]
    ratio = lax.axis_size("row") // lax.axis_size("col")
    row_index = lax.axis_index("row")
    col_index = lax.axis_index("col")
    same = chain[:, None] == chain[None, :]
    blocks = jnp.where(same | (block_mask == 1), 1.0, 0.0).astype(jnp.float32)
    labels = jnp.arange(block_count, dtype=jnp.int32)
    row_blocks = (row_index * tile_rows + jnp.arange(tile_rows, dtype=jnp.int32)) // BLOCK
    col_blocks = (col_index * tile_cols + jnp.arange(tile_cols, dtype=jnp.int32)) // BLOCK
    row_onehot = jnp.where(row_blocks[:, None] == labels[None, :], 1.0, 0.0).astype(jnp.float32)
    col_onehot = jnp.where(col_blocks[:, None] == labels[None, :], 1.0, 0.0).astype(jnp.float32)
    tile_mask = jnp.dot(jnp.dot(row_onehot, blocks), col_onehot.T)
    left, right, gate = project(pair, tile_mask, w_in[0], w_gate[0], gain_in[0])
    partial_terms = jnp.einsum(
        "ikc,jkc->ijc",
        left,
        lax.all_gather(right, "row", axis=0, tiled=True),
        preferred_element_type=jnp.float32,
    )
    product = lax.psum_scatter(
        partial_terms.astype(jnp.bfloat16), "col", scatter_dimension=1, tiled=True
    ).astype(jnp.float32)
    middle = finish(pair, product, gate, w_out[0], gain_out[0])
    left, right, gate = project(middle, tile_mask, w_in[1], w_gate[1], gain_in[1])
    left_cols = lax.all_gather(left, "row", axis=0, tiled=True)
    start_col = row_index % ratio * tile_rows
    left_slice = lax.dynamic_slice_in_dim(left_cols, start_col, tile_rows, 1)
    left_mine = broadcast(left_slice, "col", row_index // ratio)
    product = jnp.einsum(
        "kic,kjc->ijc",
        left_mine,
        lax.all_gather(right, "row", axis=0, tiled=True),
        preferred_element_type=jnp.float32,
    )
    return finish(middle, product, gate, w_out[1], gain_out[1])


NN = (((1,), (0,)), ((), ()))
NT = (((1,), (1,)), ((), ()))
TN = (((0,), (0,)), ((), ()))
SMEM_SPEC = pl.BlockSpec(memory_space=pltpu.SMEM)
COUNT = len(SIZES)


def dot(a, b, dims=NN):
    return lax.dot_general(a, b, dims, preferred_element_type=jnp.float32)


def norm_rows(rows, gain):
    channels = rows.shape[-1]
    mean_of = jnp.full((channels, channels), 1.0 / channels, jnp.bfloat16)
    values = rows.astype(jnp.float32)
    centred = values - dot(rows, mean_of)
    square = centred * centred
    high = square.astype(jnp.bfloat16)
    low = (square - high.astype(jnp.float32)).astype(jnp.bfloat16)
    spread = dot(high, mean_of) + dot(low, mean_of)
    return (centred * lax.rsqrt(spread + EPS) * gain).astype(jnp.bfloat16)


def logistic(values):
    return 0.5 * jnp.tanh(0.5 * values) + 0.5


def tile_mask(chain_ref, block_mask_ref):
    row, col = lax.axis_index("row"), lax.axis_index("col")
    seen = (chain_ref[row] == chain_ref[col]) | (block_mask_ref[row, col] == 1)
    return jnp.where(seen, 1.0, 0.0).astype(jnp.float32)


def turn_weights(w_ref, w_t):
    @pl.when(pl.program_id(0) == 0)
    def _():
        w_t[...] = w_ref[0].T


def project_rows(normed, mask, w_t, scratch, outs):
    hidden = dot(w_t[...], normed, NT)
    width = w_t.shape[0] // 4
    half = width // 2
    cols = normed.shape[0] // STEP
    x = lax.axis_index("col") // 2
    for side in range(2):
        values = hidden[2 * side * width : (2 * side + 1) * width]
        gates = hidden[(2 * side + 1) * width : (2 * side + 2) * width]
        kept = mask * logistic(gates) * values
        for row in range(STEP):
            scratch[side, pl.ds(row, width, stride=STEP), :] = kept[:, row * cols : (row + 1) * cols]
        for other in range(2):
            start = (x if other == 0 else 1 - x) * half
            for n, size in enumerate(SIZES):
                first = pl.multiple_of((start + sum(SIZES[:n])) * STEP, 8)
                block = scratch[side, pl.ds(first, size * STEP), :]
                ref = outs[(2 * side + other) * COUNT + n]
                ref[...] = block.astype(jnp.bfloat16).reshape(ref.shape)


def project_kernel(chain_ref, block_mask_ref, pair_ref, w_ref, gain_ref, *rest):
    outs, (w_t, scratch) = rest[: 4 * COUNT], rest[4 * COUNT :]
    turn_weights(w_ref, w_t)
    rows = pair_ref[...].reshape(-1, pair_ref.shape[-1])
    normed = norm_rows(rows, gain_ref[...])
    project_rows(normed, tile_mask(chain_ref, block_mask_ref), w_t, scratch, outs)


def gate_kernel(pair_ref, w_ref, gain_ref, out_ref):
    rows = pair_ref[...].reshape(-1, pair_ref.shape[-1])
    normed = norm_rows(rows, gain_ref[...])
    gate = logistic(dot(normed, w_ref[0]))
    out_ref[...] = gate.astype(out_ref.dtype).reshape(out_ref.shape)


def finish_rows(pair_ref, gate_ref, product_refs, w_out_ref, gain_ref, scratch, out_ref):
    width = w_out_ref.shape[1]
    half = width // 2
    cols = pair_ref.shape[1]
    x = lax.axis_index("col") // 2
    mine, others = pl.multiple_of(x * half, half), pl.multiple_of((1 - x) * half, half)
    w_out = jnp.concatenate([w_out_ref[0, pl.ds(mine, half)], w_out_ref[0, pl.ds(others, half)]], 0)
    gain = jnp.concatenate([gain_ref[pl.ds(mine, half)], gain_ref[pl.ds(others, half)]], 0)
    product = jnp.concatenate([ref[...] for ref in product_refs], 0).astype(jnp.float32)
    mean = jnp.sum(product, 0, keepdims=True) * (1.0 / width)
    centred = product - mean
    spread = jnp.sum(centred * centred, 0, keepdims=True) * (1.0 / width)
    update = centred * lax.rsqrt(spread + EPS) * gain
    scratch[...] = update.reshape(width * STEP, cols)
    for row in range(STEP):
        change = dot(scratch[pl.ds(row, width, stride=STEP), :].astype(jnp.bfloat16), w_out, TN)
        gate = gate_ref[row].astype(jnp.float32)
        out_ref[row] = (pair_ref[row].astype(jnp.float32) + gate * change).astype(jnp.bfloat16)


def finish_kernel(pair_ref, gate_ref, w_out_ref, gain_ref, *rest):
    product_refs, (out_ref, scratch) = rest[: 2 * COUNT], rest[2 * COUNT :]
    finish_rows(pair_ref, gate_ref, product_refs, w_out_ref, gain_ref, scratch, out_ref)


def middle_kernel(
    chain_ref, block_mask_ref, pair_ref, gate_ref, w_out_ref, gain_out_ref, w_ref, gain_in_ref, *rest
):
    product_refs, rest = rest[: 2 * COUNT], rest[2 * COUNT :]
    out_ref, outs, (update, w_t, scratch) = rest[0], rest[1 : 1 + 4 * COUNT], rest[1 + 4 * COUNT :]
    turn_weights(w_ref, w_t)
    finish_rows(pair_ref, gate_ref, product_refs, w_out_ref, gain_out_ref, update, out_ref)
    rows = out_ref[...].reshape(-1, out_ref.shape[-1])
    normed = norm_rows(rows, gain_in_ref[...])
    project_rows(normed, tile_mask(chain_ref, block_mask_ref), w_t, scratch, outs)


def outgoing_kernel(
    l_own, l_x, l_pair, l_pair_x, r_own, r_x, r_pair, r_pair_x, r_far, r_far_x, r_near, r_near_x, *rest
):
    own, pair, sent, rights = rest
    size = l_own.shape[-1]
    rights[0] = jnp.concatenate([r_own[0], r_x[0]], 1)
    rights[1] = jnp.concatenate([r_pair[0], r_pair_x[0]], 1)
    rights[2] = jnp.concatenate([r_far[0], r_far_x[0]], 1)
    rights[3] = jnp.concatenate([r_near[0], r_near_x[0]], 1)
    lefts = jnp.concatenate(
        [jnp.concatenate([l_own[0], l_x[0]], 1), jnp.concatenate([l_pair[0], l_pair_x[0]], 1)], 0
    )
    here = lax.axis_index("row") ^ lax.axis_index("col")
    for place in range(4):
        terms = dot(lefts, rights[here ^ place], NT).astype(jnp.bfloat16)
        if place % 2:
            sent[0, place // 2, 0] = terms[:size]
            sent[1, place // 2, 0] = terms[size:]
        else:
            own[place // 2, 0] = terms[:size]
            pair[place // 2, 0] = terms[size:]


def incoming_kernel(
    l_own, l_x, l_core, l_core_x, l_pair, l_pair_x, l_pair_core, l_pair_core_x, r_own, r_x, r_pair, r_pair_x, *rest
):
    *outs, lefts = rest
    size = l_own.shape[-1]
    lefts[0] = jnp.concatenate([l_own[0], l_pair[0]], 0)
    lefts[1] = jnp.concatenate([l_core[0], l_pair_core[0]], 0)
    lefts[2] = jnp.concatenate([l_x[0], l_pair_x[0]], 0)
    lefts[3] = jnp.concatenate([l_core_x[0], l_pair_core_x[0]], 0)
    rights = jnp.concatenate(
        [jnp.concatenate([r_own[0], r_x[0]], 1), jnp.concatenate([r_pair[0], r_pair_x[0]], 1)], 0
    )
    here = lax.axis_index("row") ^ lax.axis_index("col")
    for place, out in enumerate(outs):
        terms = dot(lefts[here ^ place], rights, TN).astype(jnp.bfloat16)
        out[0, 0] = terms[:, :size]
        out[1, 0] = terms[:, size:]


def params():
    return pltpu.CompilerParams(vmem_limit_bytes=VMEM, dimension_semantics=("arbitrary",))


def part(array, index):
    return pl.BlockSpec((1,) + array.shape[1:], lambda *_: (index,) + (0,) * (array.ndim - 1))


def whole(array):
    return pl.BlockSpec(array.shape, lambda *_: (0,) * array.ndim)


def tile_spec(tile):
    return pl.BlockSpec((STEP,) + tile.shape[1:], lambda r: (r, 0, 0))


def chunk_spec(shape):
    return pl.BlockSpec((shape[0], STEP, shape[2]), lambda r: (0, r, 0))


def cost(flops, nbytes, special=0):
    return pl.CostEstimate(flops=int(flops), bytes_accessed=int(nbytes), transcendentals=int(special))


def chunk_shapes(pair):
    shapes = [(size,) + pair.shape[:2] for size in SIZES] * 4
    return [jax.ShapeDtypeStruct(shape, jnp.bfloat16) for shape in shapes]


def split(arrays):
    return [arrays[k * COUNT : (k + 1) * COUNT] for k in range(4)]


def project_call(chain, block_mask, pair, w_in, gain_in):
    rows, cols, _ = pair.shape
    width = w_in.shape[2] // 4
    outs = chunk_shapes(pair)
    result = pl.pallas_call(
        project_kernel,
        grid=(rows // STEP,),
        in_specs=[SMEM_SPEC, SMEM_SPEC, tile_spec(pair), part(w_in, 0), whole(gain_in[:1])],
        out_specs=[chunk_spec(out.shape) for out in outs],
        out_shape=outs,
        scratch_shapes=[
            pltpu.VMEM((w_in.shape[2], w_in.shape[1]), jnp.bfloat16),
            pltpu.VMEM((2, width * STEP, cols), jnp.float32),
        ],
        compiler_params=params(),
        cost_estimate=cost(2e9, 8 << 20, 4 << 20),
        name="project",
    )(chain, block_mask, pair, w_in, gain_in[:1])
    return split(result)


def gate_call(pair, w_gate, gain_in, index):
    gain = gain_in[index : index + 1]
    return pl.pallas_call(
        gate_kernel,
        grid=(pair.shape[0] // STEP,),
        in_specs=[tile_spec(pair), part(w_gate, index), whole(gain)],
        out_specs=tile_spec(pair),
        out_shape=jax.ShapeDtypeStruct(pair.shape, jnp.bfloat16),
        compiler_params=params(),
        cost_estimate=cost(2e9, 8 << 20, 4 << 20),
        name="gate",
    )(pair, w_gate, gain)


def finish_call(pair, gate, products, w_out, gain_wide):
    rows, cols, _ = pair.shape
    width = w_out.shape[1]
    return pl.pallas_call(
        finish_kernel,
        grid=(rows // STEP,),
        in_specs=[tile_spec(pair), tile_spec(gate), part(w_out, 1), whole(gain_wide)]
        + [chunk_spec(p.shape) for p in products],
        out_specs=tile_spec(pair),
        out_shape=jax.ShapeDtypeStruct(pair.shape, pair.dtype),
        scratch_shapes=[pltpu.VMEM((width * STEP, cols), jnp.float32)],
        compiler_params=params(),
        cost_estimate=cost(1e9, 14 << 20, 4 << 20),
        name="finish",
    )(pair, gate, w_out, gain_wide, *products)


def middle_call(chain, block_mask, pair, gate, products, w_out, gain_wide, w_in, gain_in):
    rows, cols, _ = pair.shape
    width = w_out.shape[1]
    outs = chunk_shapes(pair)
    result = pl.pallas_call(
        middle_kernel,
        grid=(rows // STEP,),
        in_specs=[SMEM_SPEC, SMEM_SPEC, tile_spec(pair), tile_spec(gate), part(w_out, 0)]
        + [whole(gain_wide), part(w_in, 1), whole(gain_in[1:])]
        + [chunk_spec(p.shape) for p in products],
        out_specs=[tile_spec(pair)] + [chunk_spec(out.shape) for out in outs],
        out_shape=[jax.ShapeDtypeStruct(pair.shape, pair.dtype)] + outs,
        scratch_shapes=[
            pltpu.VMEM((width * STEP, cols), jnp.float32),
            pltpu.VMEM((w_in.shape[2], w_in.shape[1]), jnp.bfloat16),
            pltpu.VMEM((2, width * STEP, cols), jnp.float32),
        ],
        compiler_params=params(),
        cost_estimate=cost(3e9, 18 << 20, 8 << 20),
        name="middle",
    )(chain, block_mask, pair, gate, w_out, gain_wide, w_in, gain_in[1:], *products)
    return result[0], split(result[1:])


def product_call(kernel, operands, leads, scratch, name):
    channels, size, _ = operands[0].shape
    spec = pl.BlockSpec((1, size, size), lambda c: (c, 0, 0))

    def out_spec(lead):
        return pl.BlockSpec(lead + (1, size, size), lambda c: (0,) * len(lead) + (c, 0, 0))

    return pl.pallas_call(
        kernel,
        grid=(channels,),
        in_specs=[spec] * len(operands),
        out_specs=[out_spec(lead) for lead in leads],
        out_shape=[jax.ShapeDtypeStruct(lead + operands[0].shape, jnp.bfloat16) for lead in leads],
        scratch_shapes=[pltpu.VMEM(scratch, jnp.bfloat16)],
        compiler_params=params(),
        cost_estimate=cost(channels * 2 * (4 * size) ** 2 * size, operands[0].size * 2 * 20),
        name=name,
    )(*operands)


def inward(array):
    return lax.ppermute(array, "row", [(0, 1), (3, 2)])


def outward(array):
    return lax.ppermute(array, "row", [(1, 0), (2, 3)])


def across(array):
    return lax.ppermute(array, "row", [(1, 2), (2, 1)])


def other_core(array):
    return lax.ppermute(array, "col", [(c, c ^ 1) for c in range(4)])


def other_x(array):
    return lax.ppermute(array, "col", [(c, c ^ 2) for c in range(4)])


def share(own, pair):
    row = lax.axis_index("row")
    ready = jnp.where((row == 1) | (row == 2), own, outward(pair))
    return ready[0], other_x(ready[1])


def four_by_four(pair, chain, block_mask, w_in, w_gate, w_out, gain_in, gain_out):
    size = pair.shape[0]
    gain_wide = jnp.broadcast_to(gain_out[:, :, None, None], gain_out.shape + (1, pair.shape[1]))

    parts = project_call(chain, block_mask, pair, w_in, gain_in)
    gate = gate_call(pair, w_gate, gain_in, 0)
    products = []
    for l_own, l_send, r_own, r_send in zip(*parts):
        r_x = other_x(r_send)
        l_x = other_x(l_send)
        r_pair, r_near, l_pair = inward(r_own), across(r_own), inward(l_own)
        r_far = across(r_pair)
        r_pair_x, r_near_x, l_pair_x = inward(r_x), across(r_x), inward(l_x)
        r_far_x = across(r_pair_x)
        own, other, sent = product_call(
            outgoing_kernel,
            (l_own, l_x, l_pair, l_pair_x, r_own, r_x, r_pair, r_pair_x, r_far, r_far_x, r_near, r_near_x),
            ((2,), (2,), (2, 2)),
            (4, size, 2 * size),
            "outgoing",
        )
        come = other_core(sent)
        products.append(share(own + come[0], other + come[1]))
    products = [p[0] for p in products] + [p[1] for p in products]
    middle, parts = middle_call(
        chain, block_mask, pair, gate, products, w_out, gain_wide[0], w_in, gain_in
    )
    gate = gate_call(middle, w_gate, gain_in, 1)
    products = []
    for l_own, l_send, r_own, r_send in zip(*parts):
        l_x = other_x(l_send)
        r_x = other_x(r_send)
        l_pair, r_pair = inward(l_own), inward(r_own)
        l_pair_x, r_pair_x = inward(l_x), inward(r_x)
        own, other, far, near = product_call(
            incoming_kernel,
            (l_own, l_x, other_core(l_own), other_core(l_x))
            + (l_pair, l_pair_x, other_core(l_pair), other_core(l_pair_x))
            + (r_own, r_x, r_pair, r_pair_x),
            ((2,), (2,), (2,), (2,)),
            (4, 2 * size, size),
            "incoming",
        )
        other = other + across(far)
        products.append(share(own + across(near), other))
    products = [p[0] for p in products] + [p[1] for p in products]
    return finish_call(middle, gate, products, w_out, gain_wide[1])


def solution(mesh):
    four = mesh.shape["row"] == 4 and mesh.shape["col"] == 4
    return jax.shard_map(
        four_by_four if four else any_mesh,
        mesh=mesh,
        in_specs=(
            P(("group", "row"), "col", None),
            P("group"),
            P("group", None),
            P(),
            P(),
            P(),
            P(),
            P(),
        ),
        out_specs=P(("group", "row"), "col", None),
        check_vma=False,
    )
```

```python
import functools

import jax
import jax.numpy as jnp
from jax import lax
from jax.experimental import pallas as pl
from jax.experimental.pallas import tpu as pltpu
from jax.sharding import PartitionSpec as P

BLOCK = 128
EPS = 1e-05
OUT_SIZES = (12, 12, 8)
IN_SIZES = (6, 10, 10, 6)
STEP = 16
WINDOW = 5
TOLD = 0.05
VMEM = 48 * 1024 * 1024


def broadcast(block, axis, owner):
    block = jnp.where(lax.axis_index(axis) == owner, block, jnp.zeros_like(block))
    return lax.psum(block, axis)


def layer_norm(values, gain):
    mean = jnp.mean(values, -1, keepdims=True)
    centred = values - mean
    spread = jnp.mean(centred * centred, -1, keepdims=True)
    return centred * lax.rsqrt(spread + EPS) * gain


def project(pair, tile_mask, w_in, w_gate, gain_in):
    normed = layer_norm(pair.astype(jnp.float32), gain_in).astype(jnp.bfloat16)
    hidden = jnp.dot(normed, w_in, preferred_element_type=jnp.float32)
    width = w_in.shape[1] // 4
    masked = tile_mask[..., None]
    left = (masked * jax.nn.sigmoid(hidden[..., width : 2 * width]) * hidden[..., :width]).astype(
        jnp.bfloat16
    )
    right = (
        masked * jax.nn.sigmoid(hidden[..., 3 * width :]) * hidden[..., 2 * width : 3 * width]
    ).astype(jnp.bfloat16)
    gate = jax.nn.sigmoid(jnp.dot(normed, w_gate, preferred_element_type=jnp.float32))
    return (left, right, gate)


def finish(pair, product, gate, w_out, gain_out):
    update = layer_norm(product, gain_out).astype(jnp.bfloat16)
    return (
        pair.astype(jnp.float32) + gate * jnp.dot(update, w_out, preferred_element_type=jnp.float32)
    ).astype(jnp.bfloat16)


def any_mesh(pair, chain, block_mask, w_in, w_gate, w_out, gain_in, gain_out):
    tile_rows = pair.shape[0]
    tile_cols = pair.shape[1]
    block_count = chain.shape[0]
    ratio = lax.axis_size("row") // lax.axis_size("col")
    row_index = lax.axis_index("row")
    col_index = lax.axis_index("col")
    same = chain[:, None] == chain[None, :]
    blocks = jnp.where(same | (block_mask == 1), 1.0, 0.0).astype(jnp.float32)
    labels = jnp.arange(block_count, dtype=jnp.int32)
    row_blocks = (row_index * tile_rows + jnp.arange(tile_rows, dtype=jnp.int32)) // BLOCK
    col_blocks = (col_index * tile_cols + jnp.arange(tile_cols, dtype=jnp.int32)) // BLOCK
    row_onehot = jnp.where(row_blocks[:, None] == labels[None, :], 1.0, 0.0).astype(jnp.float32)
    col_onehot = jnp.where(col_blocks[:, None] == labels[None, :], 1.0, 0.0).astype(jnp.float32)
    tile_mask = jnp.dot(jnp.dot(row_onehot, blocks), col_onehot.T)
    left, right, gate = project(pair, tile_mask, w_in[0], w_gate[0], gain_in[0])
    partial_terms = jnp.einsum(
        "ikc,jkc->ijc",
        left,
        lax.all_gather(right, "row", axis=0, tiled=True),
        preferred_element_type=jnp.float32,
    )
    product = lax.psum_scatter(
        partial_terms.astype(jnp.bfloat16), "col", scatter_dimension=1, tiled=True
    ).astype(jnp.float32)
    middle = finish(pair, product, gate, w_out[0], gain_out[0])
    left, right, gate = project(middle, tile_mask, w_in[1], w_gate[1], gain_in[1])
    left_cols = lax.all_gather(left, "row", axis=0, tiled=True)
    start_col = row_index % ratio * tile_rows
    left_slice = lax.dynamic_slice_in_dim(left_cols, start_col, tile_rows, 1)
    left_mine = broadcast(left_slice, "col", row_index // ratio)
    product = jnp.einsum(
        "kic,kjc->ijc",
        left_mine,
        lax.all_gather(right, "row", axis=0, tiled=True),
        preferred_element_type=jnp.float32,
    )
    return finish(middle, product, gate, w_out[1], gain_out[1])


NN = (((1,), (0,)), ((), ()))
NT = (((1,), (1,)), ((), ()))
TN = (((0,), (0,)), ((), ()))
SMEM_SPEC = pl.BlockSpec(memory_space=pltpu.SMEM)


def dot(a, b, dims=NN):
    return lax.dot_general(a, b, dims, preferred_element_type=jnp.float32)


def norm_rows(rows, gain):
    channels = rows.shape[-1]
    mean_of = jnp.full((channels, channels), 1.0 / channels, jnp.bfloat16)
    values = rows.astype(jnp.float32)
    centred = values - dot(rows, mean_of)
    square = centred * centred
    high = square.astype(jnp.bfloat16)
    low = (square - high.astype(jnp.float32)).astype(jnp.bfloat16)
    spread = dot(high, mean_of) + dot(low, mean_of)
    return (centred * lax.rsqrt(spread + EPS) * gain).astype(jnp.bfloat16)


def logistic(values):
    return 0.5 * jnp.tanh(0.5 * values) + 0.5


def tile_mask(chain_ref, block_mask_ref):
    row, col = lax.axis_index("row"), lax.axis_index("col")
    seen = (chain_ref[row] == chain_ref[col]) | (block_mask_ref[row, col] == 1)
    return jnp.where(seen, 1.0, 0.0).astype(jnp.float32)


def turn_weights(w_ref, w_t):
    @pl.when(pl.program_id(0) == 0)
    def _():
        w_t[...] = w_ref[0].T


def project_rows(normed, mask, w_t, scratch, outs, sizes):
    hidden = dot(w_t[...], normed, NT)
    width = w_t.shape[0] // 4
    half = width // 2
    cols = normed.shape[0] // STEP
    x = lax.axis_index("col") // 2
    for side in range(2):
        values = hidden[2 * side * width : (2 * side + 1) * width]
        gates = hidden[(2 * side + 1) * width : (2 * side + 2) * width]
        kept = mask * logistic(gates) * values
        for row in range(STEP):
            scratch[side, pl.ds(row, width, stride=STEP), :] = kept[:, row * cols : (row + 1) * cols]
    outs = list(outs)
    for n, size in enumerate(sizes):
        right, left, *send = [outs.pop(0) for _ in range(4 if n == 0 else 3)]

        def block(side, start):
            first = pl.multiple_of((start * half + sum(sizes[:n])) * STEP, 8)
            rows = scratch[side, pl.ds(first, size * STEP), :]
            return rows.astype(jnp.bfloat16).reshape(right.shape)

        right[...] = block(1, x)
        left[...] = block(0, x)
        if n == 0:
            send[0][...] = block(1, 1 - x)
            send[1][...] = block(0, 1 - x)
        else:
            send[0][0] = block(1, 1 - x)
            send[0][1] = block(0, 1 - x)


def project_kernel(chain_ref, block_mask_ref, pair_ref, w_ref, gain_ref, *rest):
    outs, (w_t, scratch) = rest[:-2], rest[-2:]
    turn_weights(w_ref, w_t)
    rows = pair_ref[...].reshape(-1, pair_ref.shape[-1])
    normed = norm_rows(rows, gain_ref[...])
    project_rows(normed, tile_mask(chain_ref, block_mask_ref), w_t, scratch, outs, OUT_SIZES)


def gate_kernel(pair_ref, w_ref, gain_ref, out_ref):
    rows = pair_ref[...].reshape(-1, pair_ref.shape[-1])
    normed = norm_rows(rows, gain_ref[...])
    gate = logistic(dot(normed, w_ref[0]))
    out_ref[...] = gate.astype(out_ref.dtype).reshape(out_ref.shape)


def finish_rows(pair_ref, gate_ref, product_refs, w_out_ref, gain_ref, scratch, out_ref):
    width = w_out_ref.shape[1]
    half = width // 2
    cols = pair_ref.shape[1]
    x = lax.axis_index("col") // 2
    mine, others = pl.multiple_of(x * half, half), pl.multiple_of((1 - x) * half, half)
    w_out = jnp.concatenate([w_out_ref[0, pl.ds(mine, half)], w_out_ref[0, pl.ds(others, half)]], 0)
    gain = jnp.concatenate([gain_ref[pl.ds(mine, half)], gain_ref[pl.ds(others, half)]], 0)
    product = jnp.concatenate([ref[...] for ref in product_refs], 0).astype(jnp.float32)
    mean = jnp.sum(product, 0, keepdims=True) * (1.0 / width)
    centred = product - mean
    spread = jnp.sum(centred * centred, 0, keepdims=True) * (1.0 / width)
    update = centred * lax.rsqrt(spread + EPS) * gain
    scratch[...] = update.reshape(width * STEP, cols)
    for row in range(STEP):
        change = dot(scratch[pl.ds(row, width, stride=STEP), :].astype(jnp.bfloat16), w_out, TN)
        gate = gate_ref[row].astype(jnp.float32)
        out_ref[row] = (pair_ref[row].astype(jnp.float32) + gate * change).astype(jnp.bfloat16)


def finish_kernel(pair_ref, gate_ref, w_out_ref, gain_ref, *rest):
    *product_refs, out_ref, scratch = rest
    finish_rows(pair_ref, gate_ref, product_refs, w_out_ref, gain_ref, scratch, out_ref)


def middle_kernel(
    chain_ref, block_mask_ref, pair_ref, gate_ref, w_out_ref, gain_out_ref, w_ref, gain_in_ref, *rest
):
    product_refs, rest = rest[: 2 * len(OUT_SIZES)], rest[2 * len(OUT_SIZES) :]
    out_ref, outs, (update, w_t, scratch) = rest[0], rest[1:-3], rest[-3:]
    turn_weights(w_ref, w_t)
    finish_rows(pair_ref, gate_ref, product_refs, w_out_ref, gain_out_ref, update, out_ref)
    rows = out_ref[...].reshape(-1, out_ref.shape[-1])
    normed = norm_rows(rows, gain_in_ref[...])
    project_rows(normed, tile_mask(chain_ref, block_mask_ref), w_t, scratch, outs, IN_SIZES)


def outgoing_kernel(left, left_pair, right, right_pair, right_far, right_near, outs, rights):
    *kept, pair, sent = outs
    for k, blocks in enumerate((right, right_pair, right_far, right_near)):
        rights[k] = jnp.concatenate(blocks, 1)
    lefts = jnp.concatenate([jnp.concatenate(left, 1), jnp.concatenate(left_pair, 1)], 0)
    size = lefts.shape[0] // 2
    here = lax.axis_index("row") ^ lax.axis_index("col")
    for place in range(4):
        terms = dot(lefts, rights[here ^ place], NT).astype(jnp.bfloat16)
        if place % 2:
            sent[0, place // 2, 0] = terms[:size]
            sent[1, place // 2, 0] = terms[size:]
        else:
            kept[place // 2][0] = terms[:size]
            pair[place // 2, 0] = terms[size:]


def incoming_kernel(left, left_core, left_pair, left_pair_core, right, right_pair, outs, lefts):
    *kept, pair, far, near = outs
    for k in range(2):
        lefts[2 * k] = jnp.concatenate([left[k], left_pair[k]], 0)
        lefts[2 * k + 1] = jnp.concatenate([left_core[k], left_pair_core[k]], 0)
    rights = jnp.concatenate([jnp.concatenate(right, 1), jnp.concatenate(right_pair, 1)], 0)
    size = rights.shape[1] // 2
    here = lax.axis_index("row") ^ lax.axis_index("col")
    for place in range(4):
        terms = dot(lefts[here ^ place], rights, TN).astype(jnp.bfloat16)
        for k in range(2):
            block = terms[:, k * size : (k + 1) * size]
            if place == 0:
                kept[k][0] = block
            else:
                (pair, far, near)[place - 1][k, 0] = block


def pieces_kernel(kernel, counts, *refs):
    operands, position = [], 0
    for count in counts:
        if count == 1:
            operands.append([refs[position][0, 0], refs[position][1, 0]])
        else:
            operands.append([refs[position][0], refs[position + 1][0]])
        position += count
    kernel(*operands, refs[position:-1], refs[-1])


def params():
    return pltpu.CompilerParams(vmem_limit_bytes=VMEM, dimension_semantics=("arbitrary",))


def part(array, index):
    return pl.BlockSpec((1,) + array.shape[1:], lambda *_: (index,) + (0,) * (array.ndim - 1))


def whole(array):
    return pl.BlockSpec(array.shape, lambda *_: (0,) * array.ndim)


def tile_spec(tile):
    return pl.BlockSpec((STEP,) + tile.shape[1:], lambda r: (r, 0, 0))


def chunk_spec(shape):
    lead = shape[:-2]
    return pl.BlockSpec(lead + (STEP, shape[-1]), lambda r: (0,) * len(lead) + (r, 0))


def cost(flops, nbytes, special=0):
    return pl.CostEstimate(
        flops=int(flops * TOLD), bytes_accessed=int(nbytes * TOLD), transcendentals=int(special * TOLD)
    )


def chunk_shapes(pair, sizes):
    shapes = []
    for n, size in enumerate(sizes):
        shape = (size,) + pair.shape[:2]
        shapes += [shape] * 4 if n == 0 else [shape, shape, (2,) + shape]
    return [jax.ShapeDtypeStruct(shape, jnp.bfloat16) for shape in shapes]


def split(arrays, sizes):
    return [arrays[:4]] + [arrays[3 * n + 1 : 3 * n + 4] for n in range(1, len(sizes))]


def project_call(chain, block_mask, pair, w_in, gain_in):
    rows, cols, _ = pair.shape
    width = w_in.shape[2] // 4
    outs = chunk_shapes(pair, OUT_SIZES)
    result = pl.pallas_call(
        project_kernel,
        grid=(rows // STEP,),
        in_specs=[SMEM_SPEC, SMEM_SPEC, tile_spec(pair), part(w_in, 0), whole(gain_in[:1])],
        out_specs=[chunk_spec(out.shape) for out in outs],
        out_shape=outs,
        scratch_shapes=[
            pltpu.VMEM((w_in.shape[2], w_in.shape[1]), jnp.bfloat16),
            pltpu.VMEM((2, width * STEP, cols), jnp.float32),
        ],
        compiler_params=params(),
        cost_estimate=cost(2e9, 8 << 20, 4 << 20),
        name="project",
    )(chain, block_mask, pair, w_in, gain_in[:1])
    return split(result, OUT_SIZES)


def gate_call(pair, w_gate, gain_in, index):
    gain = gain_in[index : index + 1]
    return pl.pallas_call(
        gate_kernel,
        grid=(pair.shape[0] // STEP,),
        in_specs=[tile_spec(pair), part(w_gate, index), whole(gain)],
        out_specs=tile_spec(pair),
        out_shape=jax.ShapeDtypeStruct(pair.shape, jnp.bfloat16),
        compiler_params=params(),
        cost_estimate=cost(2e9, 8 << 20, 4 << 20),
        name="gate",
    )(pair, w_gate, gain)


def finish_call(pair, gate, products, w_out, gain_wide):
    rows, cols, _ = pair.shape
    width = w_out.shape[1]
    return pl.pallas_call(
        finish_kernel,
        grid=(rows // STEP,),
        in_specs=[tile_spec(pair), tile_spec(gate), part(w_out, 1), whole(gain_wide)]
        + [chunk_spec(p.shape) for p in products],
        out_specs=tile_spec(pair),
        out_shape=jax.ShapeDtypeStruct(pair.shape, pair.dtype),
        scratch_shapes=[pltpu.VMEM((width * STEP, cols), jnp.float32)],
        compiler_params=params(),
        cost_estimate=cost(1e9, 14 << 20, 4 << 20),
        name="finish",
    )(pair, gate, w_out, gain_wide, *products)


def middle_call(chain, block_mask, pair, gate, products, w_out, gain_wide, w_in, gain_in):
    rows, cols, _ = pair.shape
    width = w_out.shape[1]
    outs = chunk_shapes(pair, IN_SIZES)
    result = pl.pallas_call(
        middle_kernel,
        grid=(rows // STEP,),
        in_specs=[SMEM_SPEC, SMEM_SPEC, tile_spec(pair), tile_spec(gate), part(w_out, 0)]
        + [whole(gain_wide), part(w_in, 1), whole(gain_in[1:])]
        + [chunk_spec(p.shape) for p in products],
        out_specs=[tile_spec(pair)] + [chunk_spec(out.shape) for out in outs],
        out_shape=[jax.ShapeDtypeStruct(pair.shape, pair.dtype)] + outs,
        scratch_shapes=[
            pltpu.VMEM((width * STEP, cols), jnp.float32),
            pltpu.VMEM((w_in.shape[2], w_in.shape[1]), jnp.bfloat16),
            pltpu.VMEM((2, width * STEP, cols), jnp.float32),
        ],
        compiler_params=params(),
        cost_estimate=cost(3e9, 18 << 20, 8 << 20),
        name="middle",
    )(chain, block_mask, pair, gate, w_out, gain_wide, w_in, gain_in[1:], *products)
    return result[0], split(result[1:], IN_SIZES)


def product_call(kernel, operands, leads, scratch, name):
    counts = [len(operand) if isinstance(operand, tuple) else 1 for operand in operands]
    arrays = []
    for operand in operands:
        arrays += operand if isinstance(operand, tuple) else [operand]
    channels, size, _ = shape = arrays[0].shape[-3:]

    def spec(lead):
        return pl.BlockSpec(lead + (1, size, size), lambda c: (0,) * len(lead) + (c, 0, 0))

    return pl.pallas_call(
        functools.partial(pieces_kernel, kernel, counts),
        grid=(channels,),
        in_specs=[spec(array.shape[:-3]) for array in arrays],
        out_specs=[spec(lead) for lead in leads],
        out_shape=[jax.ShapeDtypeStruct(lead + shape, jnp.bfloat16) for lead in leads],
        scratch_shapes=[pltpu.VMEM(scratch, jnp.bfloat16)],
        compiler_params=params(),
        cost_estimate=cost(channels * 2 * (4 * size) ** 2 * size, channels * size * size * 2 * 20),
        name=name,
    )(*arrays)


def after(array, *others):
    return lax.optimization_barrier((array,) + others)[0]


class Line:
    PAIRS = {
        "inward": ("row", [(0, 1), (3, 2)], 2),
        "across": ("row", [(1, 2), (2, 1)], 2),
        "outward": ("row", [(1, 0), (2, 3)], 2),
        "x": ("col", [(c, c ^ 2) for c in range(4)], 1),
        "core": ("col", [(c, c ^ 1) for c in range(4)], 0),
    }

    def __init__(self):
        self.sent = []
        self.kinds = {kind: [] for kind in self.PAIRS}

    def __call__(self, kind, array, *others):
        axis, pairs, depth = self.PAIRS[kind]
        earlier = self.kinds[kind]
        waits = list(others)
        if depth:
            waits += self.sent[-WINDOW:][:1] if len(self.sent) >= WINDOW else []
            waits += [earlier[-depth]] if len(earlier) >= depth else []
        if waits:
            array = after(array, *waits)
        result = lax.ppermute(array, axis, pairs)
        earlier.append(result)
        if depth:
            self.sent.append(result)
        return result


def join(first, second):
    return jnp.stack([first, second])


def is_inner():
    row = lax.axis_index("row")
    return (row == 1) | (row == 2)


def outgoing(parts, gate):
    send, inner = Line(), is_inner()
    count = len(parts)
    kept, come, returned = [], [], []

    def tail(operands):
        size = operands[1][0].shape[-1]
        mine, mine_x, other, sent = product_call(
            outgoing_kernel, operands, ((), (), (2,), (2, 2)), (4, size, 2 * size), "outgoing"
        )
        core = send("core", sent)
        yield
        moved = send("outward", other + core[1])
        returned.append(moved)
        yield
        kept.append(jnp.where(inner, mine + core[0, 0], moved[0]))
        come.append(send("x", jnp.where(inner, mine_x + core[0, 1], moved[1])))
        yield

    r_own, l_own, r_send, l_send = parts[0]
    r_x = send("x", r_send)
    r_pair = send("inward", r_own)
    r_near = send("across", r_own)
    l_pair = send("inward", l_own)
    l_x = send("x", l_send, r_pair, r_near)
    r_far = send("across", r_pair)
    r_pair_x = send("inward", r_x, gate)
    r_near_x = send("across", r_x)
    x_next = send("x", parts[1][2], l_pair)
    l_pair_x = send("inward", l_x)
    r_far_x = send("across", r_pair_x)
    chunk = [(l_own, l_x), (l_pair, l_pair_x), (r_own, r_x), (r_pair, r_pair_x), (r_far, r_far_x), (r_near, r_near_x)]
    tails = []
    for n in range(1, count):
        r_own, l_own, _ = parts[n]
        right, left = join(r_own, x_next[0]), join(l_own, x_next[1])
        r_pair = send("inward", right)
        r_near = send("across", right)
        if n + 1 < count:
            x_next = send("x", parts[n + 1][2])
        if n > 1:
            next(tails[n - 2])
        l_pair = send("inward", left)
        r_far = send("across", r_pair)
        if n > 1:
            next(tails[n - 2])
        chunk[1] = tuple(after(piece, r_near) for piece in chunk[1]) if n == 1 else after(chunk[1], r_near)
        tails.append(tail(chunk))
        next(tails[n - 1])
        chunk = [left, l_pair, right, r_pair, r_far, r_near]
    if returned:
        chunk[0] = after(chunk[0], returned[-1])
    tails.append(tail(chunk))
    next(tails[-2])
    next(tails[-1])
    next(tails[-2])
    next(tails[-1])
    next(tails[-1])
    return kept + come


def incoming(parts, gate):
    send, inner = Line(), is_inner()
    count = len(parts)
    kept, come = [], []

    def tail(operands):
        size = operands[1].shape[-1]
        mine, mine_x, other, far, near = product_call(
            incoming_kernel, operands, ((), (), (2,), (2,), (2,)), (4, 2 * size, size), "incoming"
        )
        far = send("across", far)
        near = send("across", near)
        yield
        moved = send("outward", other + far)
        yield
        kept.append(jnp.where(inner, mine + near[0], moved[0]))
        come.append(send("x", jnp.where(inner, mine_x + near[1], moved[1])))
        yield

    r_own, l_own, r_send, l_send = parts[0]
    l_x = send("x", l_send)
    l_pair = send("inward", l_own)
    r_pair = send("inward", r_own)
    r_x = send("x", r_send, l_pair)
    x_next = send("x", parts[1][2], r_pair)
    l_pair_x = send("inward", l_x)
    r_pair_x = send("inward", r_x)
    left, left_pair = join(l_own, l_x), join(l_pair, l_pair_x)
    chunk = [left, send("core", left), left_pair, send("core", left_pair), (r_own, r_x), (r_pair, r_pair_x)]
    tails = []
    for n in range(1, count):
        r_own, l_own, _ = parts[n]
        right, left = join(r_own, x_next[0]), join(l_own, x_next[1])
        left_pair = send("inward", left, *((gate,) if n == 1 else ()))
        tails.append(tail(chunk))
        next(tails[n - 1])
        if n + 1 < count:
            x_next = send("x", parts[n + 1][2])
        right_pair = send("inward", right)
        if n > 1:
            next(tails[n - 2])
        next(tails[n - 1])
        chunk = [left, send("core", left), left_pair, send("core", left_pair), right, right_pair]
    tails.append(tail(chunk))
    next(tails[-1])
    next(tails[-2])
    next(tails[-1])
    next(tails[-1])
    return kept + come


def four_by_four(pair, chain, block_mask, w_in, w_gate, w_out, gain_in, gain_out):
    gain_wide = jnp.broadcast_to(gain_out[:, :, None, None], gain_out.shape + (1, pair.shape[1]))
    parts = project_call(chain, block_mask, pair, w_in, gain_in)
    gate = gate_call(pair, w_gate, gain_in, 0)
    products = outgoing(parts, gate)
    middle, parts = middle_call(
        chain, block_mask, pair, gate, products, w_out, gain_wide[0], w_in, gain_in
    )
    gate = gate_call(middle, w_gate, gain_in, 1)
    products = incoming(parts, gate)
    return finish_call(middle, gate, products, w_out, gain_wide[1])


def solution(mesh):
    four = mesh.shape["row"] == 4 and mesh.shape["col"] == 4
    return jax.shard_map(
        four_by_four if four else any_mesh,
        mesh=mesh,
        in_specs=(
            P(("group", "row"), "col", None),
            P("group"),
            P("group", None),
            P(),
            P(),
            P(),
            P(),
            P(),
        ),
        out_specs=P(("group", "row"), "col", None),
        check_vma=False,
    )
```

```python
import functools

import jax
import jax.numpy as jnp
from jax import lax
from jax.experimental import pallas as pl
from jax.experimental.pallas import tpu as pltpu
from jax.sharding import PartitionSpec as P

BLOCK = 128
EPS = 1e-05
OUT_SIZES = (12, 10, 6, 4)
IN_SIZES = (8, 12, 8, 4)
OUT_ORDER = {'l0': ('r0',), 'r0x': ('l0', 'second'), 'l0x': ('r0x', 'gate'), 'r1': ('l0x',), 'l1': ('r1',), 'r2': ('l1',), 'l2': ('r2',), 'r3': ('l2',), 'l3': ('r3',), 'f0': ('n0',), 'n0x': ('f0',), 'f0x': ('n0x',), 'n1': ('f0x',), 'f1': ('n1',), 'n2': ('f1',), 'f2': ('n2',), 'n3': ('f2',), 'f3': ('n3',), 'xl0': ('xr0',), 'x1': ('xl0',), 'x2': ('x1',), 'x3': ('x2',)}
IN_ORDER = {'r0': ('l0',), 'l0x': ('r0', 'second'), 'r0x': ('l0x', 'gate'), 'l1': ('r0x',), 'r1': ('l1',), 'l2': ('r1',), 'r2': ('l2',), 'l3': ('r2',), 'r3': ('l3',), 'n0': ('f0',), 'f1': ('n0',), 'n1': ('f1',), 'f2': ('n1',), 'n2': ('f2',), 'f3': ('n2',), 'n3': ('f3',), 'xr0': ('xl0',), 'x1': ('xr0',), 'x2': ('x1',), 'x3': ('x2',)}
STEP = 16
TOLD = 0.05
VMEM = 48 * 1024 * 1024


def broadcast(block, axis, owner):
    block = jnp.where(lax.axis_index(axis) == owner, block, jnp.zeros_like(block))
    return lax.psum(block, axis)


def layer_norm(values, gain):
    mean = jnp.mean(values, -1, keepdims=True)
    centred = values - mean
    spread = jnp.mean(centred * centred, -1, keepdims=True)
    return centred * lax.rsqrt(spread + EPS) * gain


def project(pair, tile_mask, w_in, w_gate, gain_in):
    normed = layer_norm(pair.astype(jnp.float32), gain_in).astype(jnp.bfloat16)
    hidden = jnp.dot(normed, w_in, preferred_element_type=jnp.float32)
    width = w_in.shape[1] // 4
    masked = tile_mask[..., None]
    left = (masked * jax.nn.sigmoid(hidden[..., width : 2 * width]) * hidden[..., :width]).astype(
        jnp.bfloat16
    )
    right = (
        masked * jax.nn.sigmoid(hidden[..., 3 * width :]) * hidden[..., 2 * width : 3 * width]
    ).astype(jnp.bfloat16)
    gate = jax.nn.sigmoid(jnp.dot(normed, w_gate, preferred_element_type=jnp.float32))
    return (left, right, gate)


def finish(pair, product, gate, w_out, gain_out):
    update = layer_norm(product, gain_out).astype(jnp.bfloat16)
    return (
        pair.astype(jnp.float32) + gate * jnp.dot(update, w_out, preferred_element_type=jnp.float32)
    ).astype(jnp.bfloat16)


def any_mesh(pair, chain, block_mask, w_in, w_gate, w_out, gain_in, gain_out):
    tile_rows = pair.shape[0]
    tile_cols = pair.shape[1]
    block_count = chain.shape[0]
    ratio = lax.axis_size("row") // lax.axis_size("col")
    row_index = lax.axis_index("row")
    col_index = lax.axis_index("col")
    same = chain[:, None] == chain[None, :]
    blocks = jnp.where(same | (block_mask == 1), 1.0, 0.0).astype(jnp.float32)
    labels = jnp.arange(block_count, dtype=jnp.int32)
    row_blocks = (row_index * tile_rows + jnp.arange(tile_rows, dtype=jnp.int32)) // BLOCK
    col_blocks = (col_index * tile_cols + jnp.arange(tile_cols, dtype=jnp.int32)) // BLOCK
    row_onehot = jnp.where(row_blocks[:, None] == labels[None, :], 1.0, 0.0).astype(jnp.float32)
    col_onehot = jnp.where(col_blocks[:, None] == labels[None, :], 1.0, 0.0).astype(jnp.float32)
    tile_mask = jnp.dot(jnp.dot(row_onehot, blocks), col_onehot.T)
    left, right, gate = project(pair, tile_mask, w_in[0], w_gate[0], gain_in[0])
    partial_terms = jnp.einsum(
        "ikc,jkc->ijc",
        left,
        lax.all_gather(right, "row", axis=0, tiled=True),
        preferred_element_type=jnp.float32,
    )
    product = lax.psum_scatter(
        partial_terms.astype(jnp.bfloat16), "col", scatter_dimension=1, tiled=True
    ).astype(jnp.float32)
    middle = finish(pair, product, gate, w_out[0], gain_out[0])
    left, right, gate = project(middle, tile_mask, w_in[1], w_gate[1], gain_in[1])
    left_cols = lax.all_gather(left, "row", axis=0, tiled=True)
    start_col = row_index % ratio * tile_rows
    left_slice = lax.dynamic_slice_in_dim(left_cols, start_col, tile_rows, 1)
    left_mine = broadcast(left_slice, "col", row_index // ratio)
    product = jnp.einsum(
        "kic,kjc->ijc",
        left_mine,
        lax.all_gather(right, "row", axis=0, tiled=True),
        preferred_element_type=jnp.float32,
    )
    return finish(middle, product, gate, w_out[1], gain_out[1])


NN = (((1,), (0,)), ((), ()))
NT = (((1,), (1,)), ((), ()))
TN = (((0,), (0,)), ((), ()))
SMEM_SPEC = pl.BlockSpec(memory_space=pltpu.SMEM)


def dot(a, b, dims=NN):
    return lax.dot_general(a, b, dims, preferred_element_type=jnp.float32)


def norm_rows(rows, gain):
    channels = rows.shape[-1]
    place = lax.broadcasted_iota(jnp.int32, (channels, channels), 0)
    same = place == lax.broadcasted_iota(jnp.int32, (channels, channels), 1)
    centre = jnp.where(same, 1.0 - 1.0 / channels, -1.0 / channels).astype(jnp.bfloat16)
    mean_of = jnp.full((2 * channels, channels), 1.0 / channels, jnp.bfloat16)
    centred = dot(rows, centre)
    square = centred * centred
    high = square.astype(jnp.bfloat16)
    low = (square - high.astype(jnp.float32)).astype(jnp.bfloat16)
    spread = dot(jnp.concatenate([high, low], 1), mean_of)
    return (centred * lax.rsqrt(spread + EPS) * gain).astype(jnp.bfloat16)


def logistic(values):
    return 0.5 * jnp.tanh(0.5 * values) + 0.5


def tile_mask(chain_ref, block_mask_ref):
    row, col = lax.axis_index("row"), lax.axis_index("col")
    seen = (chain_ref[row] == chain_ref[col]) | (block_mask_ref[row, col] == 1)
    return jnp.where(seen, 1.0, 0.0).astype(jnp.float32)


def turn_weights(w_ref, w_t):
    @pl.when(pl.program_id(0) == 0)
    def _():
        w_t[...] = w_ref[0].T


def project_side(normed, mask, w_t, scratch, outs):
    hidden = dot(w_t[...], normed, NT)
    width = w_t.shape[0] // 2
    half = width // 2
    cols = normed.shape[0] // STEP
    x = lax.axis_index("col") // 2
    kept = mask * logistic(hidden[width:]) * hidden[:width]
    for row in range(STEP):
        scratch[pl.ds(row, width, stride=STEP), :] = kept[:, row * cols : (row + 1) * cols]
    count = len(outs) // 2
    for start, refs in ((x, outs[:count]), (1 - x, outs[count:])):
        done = 0
        for ref in refs:
            size = ref.shape[-3]
            rows = scratch[pl.ds(pl.multiple_of((start * half + done) * STEP, 8), size * STEP), :]
            ref[...] = rows.astype(jnp.bfloat16).reshape(ref.shape)
            done += size


def first_kernel(chain_ref, block_mask_ref, pair_ref, w_ref, gain_ref, normed_ref, *rest):
    *outs, w_t, scratch = rest
    turn_weights(w_ref, w_t)
    rows = pair_ref[...].reshape(-1, pair_ref.shape[-1])
    normed = norm_rows(rows, gain_ref[0:1])
    normed_ref[...] = normed.reshape(normed_ref.shape)
    project_side(normed, tile_mask(chain_ref, block_mask_ref), w_t, scratch, outs)


def second_kernel(count, chain_ref, block_mask_ref, normed_ref, w_ref, *rest):
    *outs, w_t, scratch = rest[count:]
    turn_weights(w_ref, w_t)
    normed = normed_ref[...].reshape(-1, normed_ref.shape[-1])
    project_side(normed, tile_mask(chain_ref, block_mask_ref), w_t, scratch, outs)


def gate_kernel(normed_ref, w_ref, out_ref):
    rows = normed_ref[...].reshape(-1, normed_ref.shape[-1])
    out_ref[...] = logistic(dot(rows, w_ref[0])).astype(out_ref.dtype).reshape(out_ref.shape)


def finish_rows(pair_ref, gate_ref, product_refs, w_out_ref, gain_ref, scratch, twice, out_ref):
    width = w_out_ref.shape[1]
    half = width // 2
    cols = pair_ref.shape[1]
    x = lax.axis_index("col") // 2
    mine, others = pl.multiple_of(x * half, half), pl.multiple_of((1 - x) * half, half)

    @pl.when(pl.program_id(0) == 0)
    def _():
        w_out = jnp.concatenate([w_out_ref[0, pl.ds(mine, half)], w_out_ref[0, pl.ds(others, half)]], 0)
        none = jnp.zeros_like(w_out)
        twice[...] = jnp.concatenate(
            [jnp.concatenate([w_out, none], 1), jnp.concatenate([none, w_out], 1)], 0
        )

    gain = jnp.concatenate([gain_ref[pl.ds(mine, half)], gain_ref[pl.ds(others, half)]], 0)
    product = jnp.concatenate([ref[...] for ref in product_refs], 0).astype(jnp.float32)
    mean = jnp.sum(product, 0, keepdims=True) * (1.0 / width)
    centred = product - mean
    spread = jnp.sum(centred * centred, 0, keepdims=True) * (1.0 / width)
    update = centred * lax.rsqrt(spread + EPS) * gain
    scratch[...] = update.reshape(width * STEP, cols)
    for row in range(0, STEP, 2):
        two = jnp.concatenate(
            [scratch[pl.ds(row, width, stride=STEP), :], scratch[pl.ds(row + 1, width, stride=STEP), :]], 0
        )
        changes = dot(two.astype(jnp.bfloat16), twice[...], TN)
        for k in range(2):
            change = changes[:, k * pair_ref.shape[2] : (k + 1) * pair_ref.shape[2]]
            gate = gate_ref[row + k].astype(jnp.float32)
            old = pair_ref[row + k].astype(jnp.float32)
            out_ref[row + k] = (old + gate * change).astype(jnp.bfloat16)


def finish_kernel(pair_ref, gate_ref, w_out_ref, gain_ref, *rest):
    *product_refs, out_ref, scratch, twice = rest
    finish_rows(pair_ref, gate_ref, product_refs, w_out_ref, gain_ref, scratch, twice, out_ref)


def middle_kernel(
    count, chain_ref, block_mask_ref, pair_ref, gate_ref, w_out_ref, gain_out_ref, w_ref, gain_in_ref, *rest
):
    product_refs, (out_ref, normed_ref, *outs, update, twice, w_t, scratch) = rest[:count], rest[count:]
    turn_weights(w_ref, w_t)
    finish_rows(pair_ref, gate_ref, product_refs, w_out_ref, gain_out_ref, update, twice, out_ref)
    rows = out_ref[...].reshape(-1, out_ref.shape[-1])
    normed = norm_rows(rows, gain_in_ref[1:2])
    normed_ref[...] = normed.reshape(normed_ref.shape)
    project_side(normed, tile_mask(chain_ref, block_mask_ref), w_t, scratch, outs)


def outgoing_kernel(left, left_pair, right, right_pair, right_far, right_near, outs, rights):
    *kept, pair, sent = outs
    for k, blocks in enumerate((right, right_pair, right_far, right_near)):
        rights[k] = jnp.concatenate(blocks, 1)
    lefts = jnp.concatenate([jnp.concatenate(left, 1), jnp.concatenate(left_pair, 1)], 0)
    size = lefts.shape[0] // 2
    here = lax.axis_index("row") ^ lax.axis_index("col")
    for place in range(4):
        terms = dot(lefts, rights[here ^ place], NT).astype(jnp.bfloat16)
        if place % 2:
            sent[0, place // 2, 0] = terms[:size]
            sent[1, place // 2, 0] = terms[size:]
        else:
            kept[place // 2][0] = terms[:size]
            pair[place // 2, 0] = terms[size:]


def incoming_kernel(left, left_core, left_pair, left_pair_core, right, right_pair, outs, lefts):
    *kept, pair, far, near = outs
    for k in range(2):
        lefts[2 * k] = jnp.concatenate([left[k], left_pair[k]], 0)
        lefts[2 * k + 1] = jnp.concatenate([left_core[k], left_pair_core[k]], 0)
    rights = jnp.concatenate([jnp.concatenate(right, 1), jnp.concatenate(right_pair, 1)], 0)
    size = rights.shape[1] // 2
    here = lax.axis_index("row") ^ lax.axis_index("col")
    for place in range(4):
        terms = dot(lefts[here ^ place], rights, TN).astype(jnp.bfloat16)
        for k in range(2):
            block = terms[:, k * size : (k + 1) * size]
            if place == 0:
                kept[k][0] = block
            else:
                (pair, far, near)[place - 1][k, 0] = block


def pieces_kernel(kernel, counts, *refs):
    operands, position = [], 0
    for count in counts:
        if count == 1:
            operands.append([refs[position][0, 0], refs[position][1, 0]])
        else:
            operands.append([refs[position][0], refs[position + 1][0]])
        position += count
    kernel(*operands, refs[position:-1], refs[-1])


def params():
    return pltpu.CompilerParams(vmem_limit_bytes=VMEM, dimension_semantics=("arbitrary",))


def part(array, index):
    return pl.BlockSpec((1,) + array.shape[1:], lambda *_: (index,) + (0,) * (array.ndim - 1))


def whole(array):
    return pl.BlockSpec(array.shape, lambda *_: (0,) * array.ndim)


def tile_spec(tile):
    return pl.BlockSpec((STEP,) + tile.shape[1:], lambda r: (r, 0, 0))


def chunk_spec(shape):
    lead = shape[:-2]
    return pl.BlockSpec(lead + (STEP, shape[-1]), lambda r: (0,) * len(lead) + (r, 0))


def cost(flops, nbytes, special=0):
    return pl.CostEstimate(
        flops=int(flops * TOLD), bytes_accessed=int(nbytes * TOLD), transcendentals=int(special * TOLD)
    )


LEFT, RIGHT = 0, 1


def side_outs(pair, sizes, slot):
    tile = pair.shape[:2]
    shapes = [(size,) + tile for size in sizes + sizes[:1]] + [(2, size) + tile for size in sizes[1:]]

    def spec(shape):
        if len(shape) == 3:
            return chunk_spec(shape)
        return pl.BlockSpec((1, shape[1], STEP, shape[3]), lambda r: (slot, 0, r, 0))

    return [jax.ShapeDtypeStruct(shape, jnp.bfloat16) for shape in shapes], [spec(shape) for shape in shapes]


def side_weights(w_in, index, side):
    return pl.BlockSpec((1, w_in.shape[1], w_in.shape[2] // 2), lambda *_: (index, 0, side))


def side_scratch(pair, w_in):
    width = w_in.shape[2] // 4
    return [
        pltpu.VMEM((w_in.shape[2] // 2, w_in.shape[1]), jnp.bfloat16),
        pltpu.VMEM((width * STEP, pair.shape[1]), jnp.float32),
    ]


def finish_scratch(pair, w_out):
    return [
        pltpu.VMEM((w_out.shape[1] * STEP, pair.shape[1]), jnp.float32),
        pltpu.VMEM((2 * w_out.shape[1], 2 * w_out.shape[2]), jnp.bfloat16),
    ]


def first_call(chain, block_mask, pair, w_in, gain_in):
    outs, specs = side_outs(pair, OUT_SIZES, 0)
    normed, *result = pl.pallas_call(
        first_kernel,
        grid=(pair.shape[0] // STEP,),
        in_specs=[SMEM_SPEC, SMEM_SPEC, tile_spec(pair), side_weights(w_in, 0, RIGHT), whole(gain_in)],
        out_specs=[tile_spec(pair)] + specs,
        out_shape=[jax.ShapeDtypeStruct(pair.shape, pair.dtype)] + outs,
        scratch_shapes=side_scratch(pair, w_in),
        compiler_params=params(),
        cost_estimate=cost(2e9, 8 << 20, 4 << 20),
        name="project",
    )(chain, block_mask, pair, w_in, gain_in)
    return normed, result


def second_call(chain, block_mask, normed, w_in, index, side, sizes, shared):
    outs, specs = side_outs(normed, sizes, 1)
    count = len(shared)
    return pl.pallas_call(
        functools.partial(second_kernel, count),
        grid=(normed.shape[0] // STEP,),
        in_specs=[SMEM_SPEC, SMEM_SPEC, tile_spec(normed), side_weights(w_in, index, side)]
        + [pl.BlockSpec(memory_space=pl.ANY)] * count,
        out_specs=specs,
        out_shape=outs,
        input_output_aliases={4 + k: len(outs) - count + k for k in range(count)},
        scratch_shapes=side_scratch(normed, w_in),
        compiler_params=params(),
        cost_estimate=cost(1e9, 8 << 20, 2 << 20),
        name="second",
    )(chain, block_mask, normed, w_in, *shared)


def gate_call(normed, w_gate, index):
    return pl.pallas_call(
        gate_kernel,
        grid=(normed.shape[0] // STEP,),
        in_specs=[tile_spec(normed), part(w_gate, index)],
        out_specs=tile_spec(normed),
        out_shape=jax.ShapeDtypeStruct(normed.shape, jnp.bfloat16),
        compiler_params=params(),
        cost_estimate=cost(1e9, 8 << 20, 2 << 20),
        name="gate",
    )(normed, w_gate)


def finish_call(pair, gate, products, w_out, gain_wide):
    return pl.pallas_call(
        finish_kernel,
        grid=(pair.shape[0] // STEP,),
        in_specs=[tile_spec(pair), tile_spec(gate), part(w_out, 1), whole(gain_wide)]
        + [chunk_spec(p.shape) for p in products],
        out_specs=tile_spec(pair),
        out_shape=jax.ShapeDtypeStruct(pair.shape, pair.dtype),
        scratch_shapes=finish_scratch(pair, w_out),
        compiler_params=params(),
        cost_estimate=cost(1e9, 14 << 20, 4 << 20),
        name="finish",
    )(pair, gate, w_out, gain_wide, *products)


def middle_call(chain, block_mask, pair, gate, products, w_out, gain_wide, w_in, gain_in):
    outs, specs = side_outs(pair, IN_SIZES, 0)
    middle, normed, *result = pl.pallas_call(
        functools.partial(middle_kernel, len(products)),
        grid=(pair.shape[0] // STEP,),
        in_specs=[SMEM_SPEC, SMEM_SPEC, tile_spec(pair), tile_spec(gate), part(w_out, 0)]
        + [whole(gain_wide), side_weights(w_in, 1, LEFT), whole(gain_in)]
        + [chunk_spec(p.shape) for p in products],
        out_specs=[tile_spec(pair)] * 2 + specs,
        out_shape=[jax.ShapeDtypeStruct(pair.shape, pair.dtype)] * 2 + outs,
        scratch_shapes=finish_scratch(pair, w_out) + side_scratch(pair, w_in),
        compiler_params=params(),
        cost_estimate=cost(3e9, 18 << 20, 8 << 20),
        name="middle",
    )(chain, block_mask, pair, gate, w_out, gain_wide, w_in, gain_in, *products)
    return middle, normed, result


def product_call(kernel, operands, leads, scratch, name):
    counts = [len(operand) if isinstance(operand, tuple) else 1 for operand in operands]
    arrays = []
    for operand in operands:
        arrays += operand if isinstance(operand, tuple) else [operand]
    channels, size, _ = shape = arrays[0].shape[-3:]

    def spec(lead):
        return pl.BlockSpec(lead + (1, size, size), lambda c: (0,) * len(lead) + (c, 0, 0))

    return pl.pallas_call(
        functools.partial(pieces_kernel, kernel, counts),
        grid=(channels,),
        in_specs=[spec(array.shape[:-3]) for array in arrays],
        out_specs=[spec(lead) for lead in leads],
        out_shape=[jax.ShapeDtypeStruct(lead + shape, jnp.bfloat16) for lead in leads],
        scratch_shapes=[pltpu.VMEM(scratch, jnp.bfloat16)],
        compiler_params=params(),
        cost_estimate=cost(channels * 2 * (4 * size) ** 2 * size, channels * size * size * 2 * 20),
        name=name,
    )(*arrays)


WAYS = {
    "in": ("row", [(0, 1), (3, 2)]),
    "across": ("row", [(1, 2), (2, 1)]),
    "out": ("row", [(1, 0), (2, 3)]),
    "x": ("col", [(c, c ^ 2) for c in range(4)]),
    "core": ("col", [(c, c ^ 1) for c in range(4)]),
}


class Graph:
    def __init__(self, order, first, count):
        self.order, self.first, self.count = order, first, count
        self.steps, self.made = {}, {}

    def add(self, name, operand, step):
        self.steps[name] = (operand, step)

    def send(self, name, way, operand):
        axis, pairs = WAYS[way]
        self.add(name, operand, lambda array: lax.ppermute(array, axis, pairs))

    def get(self, name):
        if name not in self.made:
            operand, step = self.steps[name]
            waits = [self.get(other) for other in self.order.get(name, ())]
            array = operand()
            if waits:
                array = lax.optimization_barrier((array, *waits))[0]
            self.made[name] = step(array)
        return self.made[name]


def join(first, second):
    return jnp.stack([first, second])


def is_inner():
    row = lax.axis_index("row")
    return (row == 1) | (row == 2)


def shared_steps(graph, n, mine, other):
    inner = is_inner()
    get = graph.get

    def ready(k):
        return jnp.where(inner, mine(k), get(f"o{n}")[k])

    graph.send(f"o{n}", "out", other)
    graph.send(f"b{n}", "x", lambda: ready(1))
    graph.add(f"k{n}", lambda: ready(0), lambda array: array)


def finished(graph, count):
    return graph.get("gate"), [graph.get(kind + str(n)) for kind in ("k", "b") for n in range(count)]


def outgoing(first, normed, second, gate):
    count = len(OUT_SIZES)
    graph = Graph(OUT_ORDER, first, count)
    get, send = graph.get, graph.send
    graph.add("second", lambda: normed, second)
    graph.add("gate", lambda: normed, gate)
    send("xr0", "x", lambda: first[count])
    send("xl0", "x", lambda: get("second")[count])
    for end, right, left in (
        ("", lambda: first[0], lambda: get("second")[0]),
        ("x", lambda: get("xr0"), lambda: get("xl0")),
    ):
        send("r0" + end, "in", right)
        send("n0" + end, "across", right)
        send("l0" + end, "in", left)
        send("f0" + end, "across", lambda end=end: get("r0" + end))
    product_steps(
        graph,
        0,
        lambda: [(get("second")[0], get("xl0")), (get("l0"), get("l0x")), (first[0], get("xr0"))]
        + [(get(name), get(name + "x")) for name in ("r0", "f0", "n0")],
    )
    for n in range(1, count):
        later_steps(graph, n)
    return finished(graph, count)


def later_steps(graph, n):
    get, send = graph.get, graph.send
    first, count = graph.first, graph.count
    send(f"x{n}", "x", lambda: get("second")[count + n])
    graph.add(f"jr{n}", lambda: first[n], lambda own: join(own, get(f"x{n}")[0]))
    graph.add(f"jl{n}", lambda: get("second")[n], lambda own: join(own, get(f"x{n}")[1]))
    send(f"r{n}", "in", lambda: get(f"jr{n}"))
    send(f"n{n}", "across", lambda: get(f"jr{n}"))
    send(f"l{n}", "in", lambda: get(f"jl{n}"))
    send(f"f{n}", "across", lambda: get(f"r{n}"))
    product_steps(graph, n, lambda: [get(name + str(n)) for name in ("jl", "l", "jr", "r", "f", "n")])


def product_steps(graph, n, operands):
    get, send = graph.get, graph.send

    def first():
        head = operands()[0]
        return head[0] if isinstance(head, tuple) else head

    def product(head):
        head_of, *others = operands()
        head = (head, head_of[1]) if isinstance(head_of, tuple) else head
        size = head_of[0].shape[-1]
        return product_call(
            outgoing_kernel, [head, *others], ((), (), (2,), (2, 2)), (4, size, 2 * size), "outgoing"
        )

    graph.add(f"p{n}", first, product)
    send(f"c{n}", "core", lambda: get(f"p{n}")[3])
    shared_steps(
        graph,
        n,
        lambda k: get(f"p{n}")[k] + get(f"c{n}")[0, k],
        lambda: get(f"p{n}")[2] + get(f"c{n}")[1],
    )


def incoming(first, normed, second, gate):
    count = len(IN_SIZES)
    graph = Graph(IN_ORDER, first, count)
    get, send = graph.get, graph.send
    graph.add("second", lambda: normed, second)
    graph.add("gate", lambda: normed, gate)
    send("xl0", "x", lambda: first[count])
    send("xr0", "x", lambda: get("second")[count])
    send("l0", "in", lambda: first[0])
    send("r0", "in", lambda: get("second")[0])
    send("l0x", "in", lambda: get("xl0"))
    send("r0x", "in", lambda: get("xr0"))
    graph.add("jl0", lambda: first[0], lambda own: join(own, get("xl0")))
    graph.add("jp0", lambda: get("l0"), lambda own: join(own, get("l0x")))
    send("cl0", "core", lambda: get("jl0"))
    send("cp0", "core", lambda: get("jp0"))
    incoming_product(
        graph, 0, lambda: [get("jp0"), get("cp0"), (get("second")[0], get("xr0")), (get("r0"), get("r0x"))]
    )
    for n in range(1, count):
        incoming_later(graph, n)
    return finished(graph, count)


def incoming_later(graph, n):
    get, send = graph.get, graph.send
    first, count = graph.first, graph.count
    send(f"x{n}", "x", lambda: get("second")[count + n])
    graph.add(f"jl{n}", lambda: first[n], lambda own: join(own, get(f"x{n}")[0]))
    graph.add(f"jr{n}", lambda: get("second")[n], lambda own: join(own, get(f"x{n}")[1]))
    send(f"l{n}", "in", lambda: get(f"jl{n}"))
    send(f"r{n}", "in", lambda: get(f"jr{n}"))
    send(f"cl{n}", "core", lambda: get(f"jl{n}"))
    send(f"cp{n}", "core", lambda: get(f"l{n}"))
    incoming_product(graph, n, lambda: [get(name + str(n)) for name in ("l", "cp", "jr", "r")])


def incoming_product(graph, n, others):
    get, send = graph.get, graph.send

    def product(left):
        size = left.shape[-1]
        return product_call(
            incoming_kernel,
            [left, get(f"cl{n}"), *others()],
            ((), (), (2,), (2,), (2,)),
            (4, 2 * size, size),
            "incoming",
        )

    graph.add(f"p{n}", lambda: get(f"jl{n}"), product)
    send(f"f{n}", "across", lambda: get(f"p{n}")[3])
    send(f"n{n}", "across", lambda: get(f"p{n}")[4])
    shared_steps(
        graph,
        n,
        lambda k: get(f"p{n}")[k] + get(f"n{n}")[k],
        lambda: get(f"p{n}")[2] + get(f"f{n}"),
    )


def four_by_four(pair, chain, block_mask, w_in, w_gate, w_out, gain_in, gain_out):
    gain_wide = jnp.broadcast_to(gain_out[:, :, None, None], gain_out.shape + (1, pair.shape[1]))

    def rest_of(index, side, sizes, first):
        def second(normed):
            return second_call(chain, block_mask, normed, w_in, index, side, sizes, first[len(sizes) + 1 :])

        return second, lambda normed: gate_call(normed, w_gate, index)

    normed, first = first_call(chain, block_mask, pair, w_in, gain_in)
    gate, products = outgoing(first, normed, *rest_of(0, LEFT, OUT_SIZES, first))
    middle, normed, first = middle_call(
        chain, block_mask, pair, gate, products, w_out, gain_wide[0], w_in, gain_in
    )
    gate, products = incoming(first, normed, *rest_of(1, RIGHT, IN_SIZES, first))
    return finish_call(middle, gate, products, w_out, gain_wide[1])


def solution(mesh):
    four = mesh.shape["row"] == 4 and mesh.shape["col"] == 4
    return jax.shard_map(
        four_by_four if four else any_mesh,
        mesh=mesh,
        in_specs=(
            P(("group", "row"), "col", None),
            P("group"),
            P("group", None),
            P(),
            P(),
            P(),
            P(),
            P(),
        ),
        out_specs=P(("group", "row"), "col", None),
        check_vma=False,
    )
```

```python
import functools

import jax
import jax.numpy as jnp
from jax import lax
from jax.experimental import pallas as pl
from jax.experimental.pallas import tpu as pltpu
from jax.sharding import PartitionSpec as P

BLOCK = 128
EPS = 1e-05
OUT_SIZES = (8, 10, 8, 6)
IN_SIZES = (8, 10, 8, 6)
OUT_ORDER = {'i1': ('i0',), 'i2': ('i1',), 'i3': ('i2',), 'i4': ('i3',), 'i5': ('i4',), 'a1': ('a0',), 'a2': ('a1',), 'a3': ('a2',), 'a4': ('a3',), 'a5': ('a4',), 'x1': ('x0', 'a0'), 'x2': ('x1',), 'x3': ('x2',), 'p3': ('o1',)}
IN_ORDER = {'i0x': ('i0',), 'i1': ('i0x',), 'i2': ('i1',), 'i3': ('i2',), 'a1': ('a0',), 'a2': ('a1',), 'a3': ('a2',), 'x1': ('x0', 'i0'), 'x2': ('x1',), 'x3': ('x2',)}
STEP = 32
TOLD = 0.05
VMEM = 48 * 1024 * 1024


def broadcast(block, axis, owner):
    block = jnp.where(lax.axis_index(axis) == owner, block, jnp.zeros_like(block))
    return lax.psum(block, axis)


def layer_norm(values, gain):
    mean = jnp.mean(values, -1, keepdims=True)
    centred = values - mean
    spread = jnp.mean(centred * centred, -1, keepdims=True)
    return centred * lax.rsqrt(spread + EPS) * gain


def project(pair, tile_mask, w_in, w_gate, gain_in):
    normed = layer_norm(pair.astype(jnp.float32), gain_in).astype(jnp.bfloat16)
    hidden = jnp.dot(normed, w_in, preferred_element_type=jnp.float32)
    width = w_in.shape[1] // 4
    masked = tile_mask[..., None]
    left = (masked * jax.nn.sigmoid(hidden[..., width : 2 * width]) * hidden[..., :width]).astype(
        jnp.bfloat16
    )
    right = (
        masked * jax.nn.sigmoid(hidden[..., 3 * width :]) * hidden[..., 2 * width : 3 * width]
    ).astype(jnp.bfloat16)
    gate = jax.nn.sigmoid(jnp.dot(normed, w_gate, preferred_element_type=jnp.float32))
    return (left, right, gate)


def finish(pair, product, gate, w_out, gain_out):
    update = layer_norm(product, gain_out).astype(jnp.bfloat16)
    return (
        pair.astype(jnp.float32) + gate * jnp.dot(update, w_out, preferred_element_type=jnp.float32)
    ).astype(jnp.bfloat16)


def any_mesh(pair, chain, block_mask, w_in, w_gate, w_out, gain_in, gain_out):
    tile_rows = pair.shape[0]
    tile_cols = pair.shape[1]
    block_count = chain.shape[0]
    ratio = lax.axis_size("row") // lax.axis_size("col")
    row_index = lax.axis_index("row")
    col_index = lax.axis_index("col")
    same = chain[:, None] == chain[None, :]
    blocks = jnp.where(same | (block_mask == 1), 1.0, 0.0).astype(jnp.float32)
    labels = jnp.arange(block_count, dtype=jnp.int32)
    row_blocks = (row_index * tile_rows + jnp.arange(tile_rows, dtype=jnp.int32)) // BLOCK
    col_blocks = (col_index * tile_cols + jnp.arange(tile_cols, dtype=jnp.int32)) // BLOCK
    row_onehot = jnp.where(row_blocks[:, None] == labels[None, :], 1.0, 0.0).astype(jnp.float32)
    col_onehot = jnp.where(col_blocks[:, None] == labels[None, :], 1.0, 0.0).astype(jnp.float32)
    tile_mask = jnp.dot(jnp.dot(row_onehot, blocks), col_onehot.T)
    left, right, gate = project(pair, tile_mask, w_in[0], w_gate[0], gain_in[0])
    partial_terms = jnp.einsum(
        "ikc,jkc->ijc",
        left,
        lax.all_gather(right, "row", axis=0, tiled=True),
        preferred_element_type=jnp.float32,
    )
    product = lax.psum_scatter(
        partial_terms.astype(jnp.bfloat16), "col", scatter_dimension=1, tiled=True
    ).astype(jnp.float32)
    middle = finish(pair, product, gate, w_out[0], gain_out[0])
    left, right, gate = project(middle, tile_mask, w_in[1], w_gate[1], gain_in[1])
    left_cols = lax.all_gather(left, "row", axis=0, tiled=True)
    start_col = row_index % ratio * tile_rows
    left_slice = lax.dynamic_slice_in_dim(left_cols, start_col, tile_rows, 1)
    left_mine = broadcast(left_slice, "col", row_index // ratio)
    product = jnp.einsum(
        "kic,kjc->ijc",
        left_mine,
        lax.all_gather(right, "row", axis=0, tiled=True),
        preferred_element_type=jnp.float32,
    )
    return finish(middle, product, gate, w_out[1], gain_out[1])


NN = (((1,), (0,)), ((), ()))
NT = (((1,), (1,)), ((), ()))
TN = (((0,), (0,)), ((), ()))
SMEM_SPEC = pl.BlockSpec(memory_space=pltpu.SMEM)


def dot(a, b, dims=NN):
    return lax.dot_general(a, b, dims, preferred_element_type=jnp.float32)


def norm_rows(rows, gain):
    channels = rows.shape[-1]
    place = lax.broadcasted_iota(jnp.int32, (channels, channels), 0)
    same = place == lax.broadcasted_iota(jnp.int32, (channels, channels), 1)
    centre = jnp.where(same, 1.0 - 1.0 / channels, -1.0 / channels).astype(jnp.bfloat16)
    mean_of = jnp.full((2 * channels, channels), 1.0 / channels, jnp.bfloat16)
    centred = dot(rows, centre)
    square = centred * centred
    high = square.astype(jnp.bfloat16)
    low = (square - high.astype(jnp.float32)).astype(jnp.bfloat16)
    spread = dot(jnp.concatenate([high, low], 1), mean_of)
    return (centred * lax.rsqrt(spread + EPS) * gain).astype(jnp.bfloat16)


def logistic(values):
    return 0.5 * jnp.tanh(0.5 * values) + 0.5


def tile_mask(chain_ref, block_mask_ref):
    row, col = lax.axis_index("row"), lax.axis_index("col")
    seen = (chain_ref[row] == chain_ref[col]) | (block_mask_ref[row, col] == 1)
    return jnp.where(seen, 1.0, 0.0).astype(jnp.float32)


def pick_weights(w_ref, turned, picked):
    @pl.when(pl.program_id(0) == 0)
    def _():
        turned[...] = w_ref[0].astype(jnp.float32).T
        half = turned.shape[0] // 8
        x = lax.axis_index("col") // 2
        rows = []
        for kind in range(4):
            for other in (x, 1 - x):
                rows.append(turned[pl.ds(pl.multiple_of((2 * kind + other) * half, 8), half), :])
        picked[...] = jnp.concatenate(rows, 0).astype(jnp.bfloat16)


def project_part(normed, mask, picked, scratch, sides, sizes):
    hidden = dot(picked[...], normed, NT)
    width = picked.shape[0] // 4
    cols = normed.shape[0] // STEP
    for side, refs in enumerate(sides):
        values = hidden[2 * side * width : (2 * side + 1) * width]
        gates = hidden[(2 * side + 1) * width : (2 * side + 2) * width]
        kept = mask * logistic(gates) * values
        for row in range(STEP):
            scratch[side, pl.ds(row, width, stride=STEP), :] = kept[:, row * cols : (row + 1) * cols]
        done = 0
        for ref, size in zip(refs, sizes * 2):
            rows = scratch[side, done * STEP : (done + size) * STEP, :]
            ref[...] = rows.astype(jnp.bfloat16).reshape(ref.shape)
            done += size


def split_sides(outs, count, apart):
    lefts, rights = [], []
    for n in range(count):
        if apart:
            rights.append(outs[2 * n])
            lefts.append(outs[2 * n + 1])
        else:
            lefts.append(outs[n].at[0])
            rights.append(outs[n].at[1])
    for ref in outs[-count:]:
        lefts.append(ref.at[1 if apart else 0])
        rights.append(ref.at[0 if apart else 1])
    return lefts, rights


def project_all(rows, gain, mask, w_gate_ref, gate_ref, picked, scratch, outs, sizes, apart):
    normed = norm_rows(rows, gain)
    project_part(normed, mask, picked, scratch, split_sides(outs, len(sizes), apart), sizes)
    gate = logistic(dot(normed, w_gate_ref[0]))
    gate_ref[...] = gate.astype(gate_ref.dtype).reshape(gate_ref.shape)


def first_kernel(sizes, chain_ref, block_mask_ref, pair_ref, w_ref, w_gate_ref, gain_ref, gate_ref, *rest):
    *outs, turned, picked, scratch = rest
    pick_weights(w_ref, turned, picked)
    rows = pair_ref[...].reshape(-1, pair_ref.shape[-1])
    mask = tile_mask(chain_ref, block_mask_ref)
    project_all(rows, gain_ref[0:1], mask, w_gate_ref, gate_ref, picked, scratch, outs, sizes, True)


def finish_rows(pair_ref, gate_ref, product_refs, w_out_ref, gain_ref, scratch, twice, out_ref):
    width = w_out_ref.shape[1]
    half = width // 2
    cols = pair_ref.shape[1]
    x = lax.axis_index("col") // 2
    mine, others = pl.multiple_of(x * half, half), pl.multiple_of((1 - x) * half, half)

    @pl.when(pl.program_id(0) == 0)
    def _():
        w_out = jnp.concatenate([w_out_ref[0, pl.ds(mine, half)], w_out_ref[0, pl.ds(others, half)]], 0)
        none = jnp.zeros_like(w_out)
        twice[...] = jnp.concatenate(
            [jnp.concatenate([w_out, none], 1), jnp.concatenate([none, w_out], 1)], 0
        )

    gain = jnp.concatenate([gain_ref[pl.ds(mine, half)], gain_ref[pl.ds(others, half)]], 0)
    product = jnp.concatenate([ref[...] for ref in product_refs], 0).astype(jnp.float32)
    mean = jnp.sum(product, 0, keepdims=True) * (1.0 / width)
    centred = product - mean
    spread = jnp.sum(centred * centred, 0, keepdims=True) * (1.0 / width)
    update = centred * lax.rsqrt(spread + EPS) * gain
    scratch[...] = update.reshape(width * STEP, cols)
    for row in range(0, STEP, 2):
        two = jnp.concatenate(
            [scratch[pl.ds(row, width, stride=STEP), :], scratch[pl.ds(row + 1, width, stride=STEP), :]], 0
        )
        changes = dot(two.astype(jnp.bfloat16), twice[...], TN)
        for k in range(2):
            change = changes[:, k * pair_ref.shape[2] : (k + 1) * pair_ref.shape[2]]
            gate = gate_ref[row + k].astype(jnp.float32)
            old = pair_ref[row + k].astype(jnp.float32)
            out_ref[row + k] = (old + gate * change).astype(jnp.bfloat16)


def finish_kernel(pair_ref, gate_ref, w_out_ref, gain_ref, *rest):
    *product_refs, out_ref, scratch, twice = rest
    finish_rows(pair_ref, gate_ref, product_refs, w_out_ref, gain_ref, scratch, twice, out_ref)


def middle_kernel(
    sizes,
    count,
    chain_ref,
    block_mask_ref,
    pair_ref,
    gate_ref,
    w_out_ref,
    gain_out_ref,
    w_ref,
    w_gate_ref,
    gain_in_ref,
    *rest,
):
    product_refs, (out_ref, next_ref, *outs, update, twice, turned, picked, scratch) = rest[:count], rest[count:]
    pick_weights(w_ref, turned, picked)
    finish_rows(pair_ref, gate_ref, product_refs, w_out_ref, gain_out_ref, update, twice, out_ref)
    rows = out_ref[...].reshape(-1, out_ref.shape[-1])
    mask = tile_mask(chain_ref, block_mask_ref)
    project_all(rows, gain_in_ref[1:2], mask, w_gate_ref, next_ref, picked, scratch, outs, sizes, False)


def outgoing_kernel(left, left_pair, right, right_pair, right_far, right_near, outs, rights):
    *kept, pair, sent = outs
    for k, blocks in enumerate((right, right_pair, right_far, right_near)):
        rights[k] = jnp.concatenate(blocks, 1)
    lefts = jnp.concatenate([jnp.concatenate(left, 1), jnp.concatenate(left_pair, 1)], 0)
    size = lefts.shape[0] // 2
    here = lax.axis_index("row") ^ lax.axis_index("col")
    for place in range(4):
        terms = dot(lefts, rights[here ^ place], NT).astype(jnp.bfloat16)
        if place % 2:
            sent[0, place // 2, 0] = terms[:size]
            sent[1, place // 2, 0] = terms[size:]
        else:
            kept[place // 2][0] = terms[:size]
            pair[place // 2, 0] = terms[size:]


def incoming_kernel(left, left_core, left_pair, left_pair_core, right, right_pair, outs, lefts):
    *kept, pair, cross = outs
    for k in range(2):
        lefts[2 * k] = jnp.concatenate([left[k], left_pair[k]], 0)
        lefts[2 * k + 1] = jnp.concatenate([left_core[k], left_pair_core[k]], 0)
    rights = jnp.concatenate([jnp.concatenate(right, 1), jnp.concatenate(right_pair, 1)], 0)
    size = rights.shape[1] // 2
    here = lax.axis_index("row") ^ lax.axis_index("col")
    for place in range(4):
        terms = dot(lefts[here ^ place], rights, TN).astype(jnp.bfloat16)
        for k in range(2):
            block = terms[:, k * size : (k + 1) * size]
            if place == 0:
                kept[k][0] = block
            else:
                (pair, cross.at[0], cross.at[1])[place - 1][k, 0] = block


def pieces_kernel(kernel, count, *refs):
    blocks = [ref[(0,) * (len(ref.shape) - 2)] for ref in refs[:count]]
    kernel(*[blocks[k : k + 2] for k in range(0, count, 2)], refs[count:-1], refs[-1])


def params():
    return pltpu.CompilerParams(vmem_limit_bytes=VMEM, dimension_semantics=("arbitrary",))


def part(array, index):
    return pl.BlockSpec((1,) + array.shape[1:], lambda *_: (index,) + (0,) * (array.ndim - 1))


def whole(array):
    return pl.BlockSpec(array.shape, lambda *_: (0,) * array.ndim)


def tile_spec(tile):
    return pl.BlockSpec((STEP,) + tile.shape[1:], lambda r: (r, 0, 0))


def chunk_spec(shape):
    lead = shape[:-2]
    return pl.BlockSpec(lead + (STEP, shape[-1]), lambda r: (0,) * len(lead) + (r, 0))


def cost(flops, nbytes, special=0):
    return pl.CostEstimate(
        flops=int(flops * TOLD), bytes_accessed=int(nbytes * TOLD), transcendentals=int(special * TOLD)
    )


def part_outs(pair, sizes, apart):
    tile = pair.shape[:2]
    own = [(size,) + tile for size in sizes]
    both_sides = [(2,) + shape for shape in own]
    shapes = ([shape for shape in own for _ in range(2)] if apart else both_sides) + both_sides
    return [jax.ShapeDtypeStruct(shape, jnp.bfloat16) for shape in shapes], [chunk_spec(shape) for shape in shapes]


def part_scratch(pair, w_in, sizes):
    width = 2 * sum(sizes)
    return [
        pltpu.VMEM((w_in.shape[2], w_in.shape[1]), jnp.float32),
        pltpu.VMEM((4 * width, w_in.shape[1]), jnp.bfloat16),
        pltpu.VMEM((2, width * STEP, pair.shape[1]), jnp.float32),
    ]


def finish_scratch(pair, w_out):
    return [
        pltpu.VMEM((w_out.shape[1] * STEP, pair.shape[1]), jnp.float32),
        pltpu.VMEM((2 * w_out.shape[1], 2 * w_out.shape[2]), jnp.bfloat16),
    ]


def first_call(chain, block_mask, pair, w_in, w_gate, gain_in):
    outs, specs = part_outs(pair, OUT_SIZES, True)
    gate, *result = pl.pallas_call(
        functools.partial(first_kernel, OUT_SIZES),
        grid=(pair.shape[0] // STEP,),
        in_specs=[SMEM_SPEC, SMEM_SPEC, tile_spec(pair), part(w_in, 0), part(w_gate, 0), whole(gain_in)],
        out_specs=[tile_spec(pair)] + specs,
        out_shape=[jax.ShapeDtypeStruct(pair.shape, pair.dtype)] + outs,
        scratch_shapes=part_scratch(pair, w_in, OUT_SIZES),
        compiler_params=params(),
        cost_estimate=cost(2e9, 8 << 20, 4 << 20),
        name="project",
    )(chain, block_mask, pair, w_in, w_gate, gain_in)
    return gate, result


def finish_call(pair, gate, products, w_out, gain_wide):
    return pl.pallas_call(
        finish_kernel,
        grid=(pair.shape[0] // STEP,),
        in_specs=[tile_spec(pair), tile_spec(gate), part(w_out, 1), whole(gain_wide)]
        + [chunk_spec(p.shape) for p in products],
        out_specs=tile_spec(pair),
        out_shape=jax.ShapeDtypeStruct(pair.shape, pair.dtype),
        scratch_shapes=finish_scratch(pair, w_out),
        compiler_params=params(),
        cost_estimate=cost(1e9, 14 << 20, 4 << 20),
        name="finish",
    )(pair, gate, w_out, gain_wide, *products)


def middle_call(chain, block_mask, pair, gate, products, w_out, gain_wide, w_in, w_gate, gain_in):
    outs, specs = part_outs(pair, IN_SIZES, False)
    middle, gate, *result = pl.pallas_call(
        functools.partial(middle_kernel, IN_SIZES, len(products)),
        grid=(pair.shape[0] // STEP,),
        in_specs=[SMEM_SPEC, SMEM_SPEC, tile_spec(pair), tile_spec(gate), part(w_out, 0)]
        + [whole(gain_wide), part(w_in, 1), part(w_gate, 1), whole(gain_in)]
        + [chunk_spec(p.shape) for p in products],
        out_specs=[tile_spec(pair)] * 2 + specs,
        out_shape=[jax.ShapeDtypeStruct(pair.shape, pair.dtype)] * 2 + outs,
        scratch_shapes=finish_scratch(pair, w_out) + part_scratch(pair, w_in, IN_SIZES),
        compiler_params=params(),
        cost_estimate=cost(3e9, 18 << 20, 8 << 20),
        name="middle",
    )(chain, block_mask, pair, gate, w_out, gain_wide, w_in, w_gate, gain_in, *products)
    return middle, gate, result


def product_call(kernel, operands, channels, leads, scratch, name):
    pieces = [piece for operand in operands for piece in operand]
    size = pieces[0][0].shape[-1]

    def piece_spec(array, lead, first):
        return pl.BlockSpec((1,) * (len(lead) + 1) + (size, size), lambda c: lead + (first + c, 0, 0))

    def out_spec(lead):
        return pl.BlockSpec(lead + (1, size, size), lambda c: (0,) * len(lead) + (c, 0, 0))

    return pl.pallas_call(
        functools.partial(pieces_kernel, kernel, len(pieces)),
        grid=(channels,),
        in_specs=[piece_spec(*piece) for piece in pieces],
        out_specs=[out_spec(lead) for lead in leads],
        out_shape=[jax.ShapeDtypeStruct(lead + (channels, size, size), jnp.bfloat16) for lead in leads],
        scratch_shapes=[pltpu.VMEM(scratch, jnp.bfloat16)],
        compiler_params=params(),
        cost_estimate=cost(channels * 2 * (4 * size) ** 2 * size, channels * size * size * 2 * 20),
        name=name,
    )(*[piece[0] for piece in pieces])


WAYS = {
    "in": ("row", [(0, 1), (3, 2)]),
    "across": ("row", [(1, 2), (2, 1)]),
    "out": ("row", [(1, 0), (2, 3)]),
    "x": ("col", [(c, c ^ 2) for c in range(4)]),
    "core": ("col", [(c, c ^ 1) for c in range(4)]),
}


class Graph:
    def __init__(self, order):
        self.order, self.steps, self.made = order, {}, {}

    def add(self, name, operand, step):
        self.steps[name] = (operand, step)

    def send(self, name, way, operand):
        axis, pairs = WAYS[way]
        self.add(name, operand, lambda array: lax.ppermute(array, axis, pairs))

    def get(self, name):
        if name not in self.made:
            operand, step = self.steps[name]
            waits = [self.get(other) for other in self.order.get(name, ())]
            array = operand()
            if waits:
                array = lax.optimization_barrier((array, *waits))[0]
            self.made[name] = step(array)
        return self.made[name]


def pack(*columns):
    return jnp.stack([jnp.concatenate([column[k] for column in columns]) for k in range(2)])


def both(array, first=0, lead=()):
    return [(array, (k,) + lead, first) for k in range(2)]


def is_inner():
    row = lax.axis_index("row")
    return (row == 1) | (row == 2)


def shared_steps(graph, n, mine, other):
    inner = is_inner()
    get = graph.get

    def ready(k):
        return jnp.where(inner, mine(k), get(f"o{n}")[k])

    graph.send(f"o{n}", "out", other)
    graph.send(f"b{n}", "x", lambda: ready(1))
    graph.add(f"k{n}", lambda: ready(0), lambda array: array)


def finished(graph, count):
    return [graph.get(kind + str(n)) for kind in ("k", "b") for n in range(count)]


def outgoing(parts):
    count = len(OUT_SIZES)
    graph = Graph(OUT_ORDER)
    get, send = graph.get, graph.send
    for n in range(count):
        send(f"x{n}", "x", lambda n=n: parts[2 * count + n])
    later = lambda n, side: parts[2 * n + side]
    right_of = lambda n: (later(n, 0), get(f"x{n}")[0])
    left_of = lambda n: (later(n, 1), get(f"x{n}")[1])
    first = parts
    zero = OUT_SIZES[0]
    send("i0", "in", lambda: first[0])
    send("a0", "across", lambda: first[0])
    send("i1", "in", lambda: jnp.concatenate([get("x0")[0], first[1]]))
    send("a1", "across", lambda: jnp.concatenate([get("x0")[0], get("i0")]))

    def come(n):
        array, skip = get(f"i{n + 1}"), zero // 2 if n == 1 else OUT_SIZES[n - 1]
        return (array[0, skip:], array[1, skip:])

    def halves(array):
        return (array[: zero // 2], array[zero // 2 :])

    def inward(n):
        before = halves(get("x0")[1]) if n == 1 else left_of(n - 1)
        return pack(before, right_of(n)) if n < count else pack(before)

    def across(n):
        before = halves(get("i1")[:zero]) if n == 1 else come(n - 1)
        return pack(before, right_of(n)) if n < count else pack(before)

    for n in range(1, count + 1):
        send(f"i{n + 1}", "in", lambda n=n: inward(n))
        send(f"a{n + 1}", "across", lambda n=n: across(n))

    def product(n, left):
        size = left.shape[-1]
        if n == 0:
            x_left = lambda array: array[:, : zero // 2].reshape((zero,) + array.shape[2:])
            operands = [
                [(left, (), 0), (get("x0"), (1,), 0)],
                [(get("i1"), (), zero), (x_left(get("i2")), (), 0)],
                [(first[0], (), 0), (get("x0"), (0,), 0)],
                [(get("i0"), (), 0), (get("i1"), (), 0)],
                [(get("a1"), (), zero), (x_left(get("a2")), (), 0)],
                [(get("a0"), (), 0), (get("a1"), (), 0)],
            ]
        else:
            skip = zero // 2 if n == 1 else OUT_SIZES[n - 1]
            operands = [
                [(left, (), 0), (get(f"x{n}"), (1,), 0)],
                both(get(f"i{n + 2}")),
                [(later(n, 0), (), 0), (get(f"x{n}"), (0,), 0)],
                both(get(f"i{n + 1}"), skip),
                both(get(f"a{n + 2}")),
                both(get(f"a{n + 1}"), skip),
            ]
        leads = ((), (), (2,), (2, 2))
        return product_call(outgoing_kernel, operands, left.shape[0], leads, (4, size, 2 * size), "outgoing")

    for n in range(count):
        graph.add(f"p{n}", lambda n=n: later(n, 1), functools.partial(product, n))
        send(f"c{n}", "core", lambda n=n: get(f"p{n}")[3])
        shared_steps(
            graph,
            n,
            lambda k, n=n: get(f"p{n}")[k] + get(f"c{n}")[0, k],
            lambda n=n: get(f"p{n}")[2] + get(f"c{n}")[1],
        )
    return finished(graph, count)


def incoming(parts):
    count = len(IN_SIZES)
    graph = Graph(IN_ORDER)
    get, send = graph.get, graph.send
    for n in range(count):
        send(f"x{n}", "x", lambda n=n: parts[count + n])
    send("i0", "in", lambda: parts[0])
    send("i0x", "in", lambda: get("x0"))
    send("cl0", "core", lambda: parts[0])
    send("clx", "core", lambda: get("x0"))
    send("cp0", "core", lambda: get("i0"))
    send("cpx", "core", lambda: get("i0x"))
    for n in range(1, count):
        graph.add(f"j{n}", lambda n=n: parts[n], lambda own, n=n: jnp.stack([own, get(f"x{n}")], 1))
        send(f"i{n}", "in", lambda n=n: get(f"j{n}"))
        send(f"cl{n}", "core", lambda n=n: get(f"j{n}")[0])
        send(f"cp{n}", "core", lambda n=n: get(f"i{n}")[0])

    def product(n, own):
        size = own.shape[-1]
        if n == 0:
            side = lambda name, name_x, slot: [
                (own if name is None else get(name), (slot,), 0),
                (get(name_x), (slot,), 0),
            ]
            operands = [side(None, "x0", 0), side("cl0", "clx", 0), side("i0", "i0x", 0), side("cp0", "cpx", 0)]
            operands += [side(None, "x0", 1), side("i0", "i0x", 1)]
        else:
            side = lambda array, slot: [(array, (slot, k), 0) for k in range(2)]
            operands = [side(own, 0), both(get(f"cl{n}")), side(get(f"i{n}"), 0), both(get(f"cp{n}"))]
            operands += [side(own, 1), side(get(f"i{n}"), 1)]
        leads = ((), (), (2,), (2, 2))
        return product_call(incoming_kernel, operands, IN_SIZES[n], leads, (4, 2 * size, size), "incoming")

    for n in range(count):
        graph.add(f"p{n}", lambda n=n: get(f"j{n}") if n else parts[0], functools.partial(product, n))
        send(f"a{n}", "across", lambda n=n: get(f"p{n}")[3])
        shared_steps(
            graph,
            n,
            lambda k, n=n: get(f"p{n}")[k] + get(f"a{n}")[1, k],
            lambda n=n: get(f"p{n}")[2] + get(f"a{n}")[0],
        )
    return finished(graph, count)


def four_by_four(pair, chain, block_mask, w_in, w_gate, w_out, gain_in, gain_out):
    gain_wide = jnp.broadcast_to(gain_out[:, :, None, None], gain_out.shape + (1, pair.shape[1]))
    gate, parts = first_call(chain, block_mask, pair, w_in, w_gate, gain_in)
    products = outgoing(parts)
    middle, gate, parts = middle_call(
        chain, block_mask, pair, gate, products, w_out, gain_wide[0], w_in, w_gate, gain_in
    )
    products = incoming(parts)
    return finish_call(middle, gate, products, w_out, gain_wide[1])


def solution(mesh):
    four = mesh.shape["row"] == 4 and mesh.shape["col"] == 4
    return jax.shard_map(
        four_by_four if four else any_mesh,
        mesh=mesh,
        in_specs=(
            P(("group", "row"), "col", None),
            P("group"),
            P("group", None),
            P(),
            P(),
            P(),
            P(),
            P(),
        ),
        out_specs=P(("group", "row"), "col", None),
        check_vma=False,
    )
```

```python
import functools

import jax
import jax.numpy as jnp
from jax import lax
from jax.experimental import pallas as pl
from jax.experimental.pallas import tpu as pltpu
from jax.sharding import PartitionSpec as P

BLOCK = 128
EPS = 1e-05
OUT_SIZES = (8, 8, 8, 4, 4)
IN_SIZES = (8, 8, 8, 4, 4)
OUT_ORDER = {'i1': ('i0',), 'i2': ('i1',), 'i3': ('i2',), 'i4': ('i3',), 'i5': ('i4',), 'i6': ('i5',), 'a1': ('a0',), 'a2': ('a1',), 'a3': ('a2',), 'a4': ('a3',), 'a5': ('a4',), 'a6': ('a5',), 'o1': ('o0',), 'o2': ('o1',), 'o3': ('o2',), 'o4': ('o3',), 'x1': ('a0',), 'x2': ('a1',), 'p2': ('o0',), 'p3': ('o1',), 'p4': ('o2',)}
IN_ORDER = {'i0x': ('i0',), 'i1': ('i0x',), 'i2': ('i1',), 'i3': ('i2',), 'i4': ('i3',), 'a1': ('a0',), 'a2': ('a1',), 'a3': ('a2',), 'a4': ('a3',), 'o1': ('o0',), 'o2': ('o1',), 'o3': ('o2',), 'o4': ('o3',), 'x1': ('i0',), 'x2': ('i0x',), 'b4': ('b3',)}
STEP = 16
TOLD = 0.05
VMEM = 48 * 1024 * 1024


def broadcast(block, axis, owner):
    block = jnp.where(lax.axis_index(axis) == owner, block, jnp.zeros_like(block))
    return lax.psum(block, axis)


def layer_norm(values, gain):
    mean = jnp.mean(values, -1, keepdims=True)
    centred = values - mean
    spread = jnp.mean(centred * centred, -1, keepdims=True)
    return centred * lax.rsqrt(spread + EPS) * gain


def project(pair, tile_mask, w_in, w_gate, gain_in):
    normed = layer_norm(pair.astype(jnp.float32), gain_in).astype(jnp.bfloat16)
    hidden = jnp.dot(normed, w_in, preferred_element_type=jnp.float32)
    width = w_in.shape[1] // 4
    masked = tile_mask[..., None]
    left = (masked * jax.nn.sigmoid(hidden[..., width : 2 * width]) * hidden[..., :width]).astype(
        jnp.bfloat16
    )
    right = (
        masked * jax.nn.sigmoid(hidden[..., 3 * width :]) * hidden[..., 2 * width : 3 * width]
    ).astype(jnp.bfloat16)
    gate = jax.nn.sigmoid(jnp.dot(normed, w_gate, preferred_element_type=jnp.float32))
    return (left, right, gate)


def finish(pair, product, gate, w_out, gain_out):
    update = layer_norm(product, gain_out).astype(jnp.bfloat16)
    return (
        pair.astype(jnp.float32) + gate * jnp.dot(update, w_out, preferred_element_type=jnp.float32)
    ).astype(jnp.bfloat16)


def any_mesh(pair, chain, block_mask, w_in, w_gate, w_out, gain_in, gain_out):
    tile_rows = pair.shape[0]
    tile_cols = pair.shape[1]
    block_count = chain.shape[0]
    ratio = lax.axis_size("row") // lax.axis_size("col")
    row_index = lax.axis_index("row")
    col_index = lax.axis_index("col")
    same = chain[:, None] == chain[None, :]
    blocks = jnp.where(same | (block_mask == 1), 1.0, 0.0).astype(jnp.float32)
    labels = jnp.arange(block_count, dtype=jnp.int32)
    row_blocks = (row_index * tile_rows + jnp.arange(tile_rows, dtype=jnp.int32)) // BLOCK
    col_blocks = (col_index * tile_cols + jnp.arange(tile_cols, dtype=jnp.int32)) // BLOCK
    row_onehot = jnp.where(row_blocks[:, None] == labels[None, :], 1.0, 0.0).astype(jnp.float32)
    col_onehot = jnp.where(col_blocks[:, None] == labels[None, :], 1.0, 0.0).astype(jnp.float32)
    tile_mask = jnp.dot(jnp.dot(row_onehot, blocks), col_onehot.T)
    left, right, gate = project(pair, tile_mask, w_in[0], w_gate[0], gain_in[0])
    partial_terms = jnp.einsum(
        "ikc,jkc->ijc",
        left,
        lax.all_gather(right, "row", axis=0, tiled=True),
        preferred_element_type=jnp.float32,
    )
    product = lax.psum_scatter(
        partial_terms.astype(jnp.bfloat16), "col", scatter_dimension=1, tiled=True
    ).astype(jnp.float32)
    middle = finish(pair, product, gate, w_out[0], gain_out[0])
    left, right, gate = project(middle, tile_mask, w_in[1], w_gate[1], gain_in[1])
    left_cols = lax.all_gather(left, "row", axis=0, tiled=True)
    start_col = row_index % ratio * tile_rows
    left_slice = lax.dynamic_slice_in_dim(left_cols, start_col, tile_rows, 1)
    left_mine = broadcast(left_slice, "col", row_index // ratio)
    product = jnp.einsum(
        "kic,kjc->ijc",
        left_mine,
        lax.all_gather(right, "row", axis=0, tiled=True),
        preferred_element_type=jnp.float32,
    )
    return finish(middle, product, gate, w_out[1], gain_out[1])


NN = (((1,), (0,)), ((), ()))
NT = (((1,), (1,)), ((), ()))
TN = (((0,), (0,)), ((), ()))
SMEM_SPEC = pl.BlockSpec(memory_space=pltpu.SMEM)


def dot(a, b, dims=NN):
    return lax.dot_general(a, b, dims, preferred_element_type=jnp.float32)


def norm_rows(rows, gain):
    channels = rows.shape[-1]
    place = lax.broadcasted_iota(jnp.int32, (channels, channels), 0)
    same = place == lax.broadcasted_iota(jnp.int32, (channels, channels), 1)
    centre = jnp.where(same, 1.0 - 1.0 / channels, -1.0 / channels).astype(jnp.bfloat16)
    mean_of = jnp.full((2 * channels, channels), 1.0 / channels, jnp.bfloat16)
    centred = dot(rows, centre)
    square = centred * centred
    high = square.astype(jnp.bfloat16)
    low = (square - high.astype(jnp.float32)).astype(jnp.bfloat16)
    spread = dot(jnp.concatenate([high, low], 1), mean_of)
    return (centred * lax.rsqrt(spread + EPS) * gain).astype(jnp.bfloat16)


def logistic(values):
    return 0.5 * jnp.tanh(0.5 * values) + 0.5


def tile_mask(chain_ref, block_mask_ref):
    row, col = lax.axis_index("row"), lax.axis_index("col")
    seen = (chain_ref[row] == chain_ref[col]) | (block_mask_ref[row, col] == 1)
    return jnp.where(seen, 1.0, 0.0).astype(jnp.float32)


def pick_weights(w_ref, turned, picked):
    @pl.when(pl.program_id(0) == 0)
    def _():
        turned[...] = w_ref[0].astype(jnp.float32).T
        half = turned.shape[0] // 8
        x = lax.axis_index("col") // 2
        rows = []
        for kind in range(4):
            for other in (x, 1 - x):
                rows.append(turned[pl.ds(pl.multiple_of((2 * kind + other) * half, 8), half), :])
        picked[...] = jnp.concatenate(rows, 0).astype(jnp.bfloat16)


def project_row(row, normed, mask, picked, scratch):
    hidden = dot(picked[...], normed, NT)
    width = picked.shape[0] // 4
    for side in range(2):
        values = hidden[2 * side * width : (2 * side + 1) * width]
        gates = hidden[(2 * side + 1) * width : (2 * side + 2) * width]
        scratch[side, pl.ds(row, width, stride=STEP), :] = mask * logistic(gates) * values


def project_out(scratch, sides, sizes):
    for side, refs in enumerate(sides):
        done = 0
        for ref, size in zip(refs, sizes * 2):
            for k in range(size):
                rows = scratch[side, (done + k) * STEP : (done + k + 1) * STEP, :]
                ref[k] = rows.astype(jnp.bfloat16)
            done += size


def split_sides(outs, count, apart):
    lefts, rights = [], []
    for n in range(count):
        if apart:
            rights.append(outs[2 * n])
            lefts.append(outs[2 * n + 1])
        else:
            lefts.append(outs[n].at[0])
            rights.append(outs[n].at[1])
    for ref in outs[-count:]:
        lefts.append(ref.at[1 if apart else 0])
        rights.append(ref.at[0 if apart else 1])
    return lefts, rights


def project_all(rows_ref, gain, mask, w_gate_ref, gate_ref, picked, scratch, outs, sizes, apart):
    for row in range(STEP):
        normed = norm_rows(rows_ref[row], gain)
        project_row(row, normed, mask, picked, scratch)
        gate_ref[row] = logistic(dot(normed, w_gate_ref[0])).astype(gate_ref.dtype)
    project_out(scratch, split_sides(outs, len(sizes), apart), sizes)


def first_kernel(sizes, chain_ref, block_mask_ref, pair_ref, w_ref, w_gate_ref, gain_ref, gate_ref, *rest):
    *outs, turned, picked, scratch = rest
    pick_weights(w_ref, turned, picked)
    mask = tile_mask(chain_ref, block_mask_ref)
    project_all(pair_ref, gain_ref[0:1], mask, w_gate_ref, gate_ref, picked, scratch, outs, sizes, True)


def added(terms):
    lanes = [functools.reduce(jnp.add, terms[k::4]) for k in range(4)]
    return (lanes[0] + lanes[1]) + (lanes[2] + lanes[3])


def finish_rows(pair_ref, gate_ref, product_refs, w_out_ref, gain_ref, scratch, twice, out_ref):
    width = w_out_ref.shape[1]
    half = width // 2
    cols = pair_ref.shape[1]
    x = lax.axis_index("col") // 2
    mine, others = pl.multiple_of(x * half, half), pl.multiple_of((1 - x) * half, half)

    @pl.when(pl.program_id(0) == 0)
    def _():
        w_out = jnp.concatenate([w_out_ref[0, pl.ds(mine, half)], w_out_ref[0, pl.ds(others, half)]], 0)
        none = jnp.zeros_like(w_out)
        twice[...] = jnp.concatenate(
            [jnp.concatenate([w_out, none], 1), jnp.concatenate([none, w_out], 1)], 0
        )

    for start in range(0, STEP, 16):
        group = [(ref, k, start) for ref in product_refs for k in range(ref.shape[0])]
        read = lambda at: at[0][at[1], at[2] : at[2] + 16, :].astype(jnp.float32)
        mean = added([read(at) for at in group]) * (1.0 / width)
        spread = added([jnp.square(read(at) - mean) for at in group]) * (1.0 / width)
        scale = lax.rsqrt(spread + EPS)
        for n, at in enumerate(group):
            gain = gain_ref[(mine if n < half else others) + n % half]
            scratch[n * STEP + start : n * STEP + start + 16, :] = (read(at) - mean) * scale * gain
    for row in range(0, STEP, 2):
        two = jnp.concatenate(
            [scratch[pl.ds(row, width, stride=STEP), :], scratch[pl.ds(row + 1, width, stride=STEP), :]], 0
        )
        changes = dot(two.astype(jnp.bfloat16), twice[...], TN)
        for k in range(2):
            change = changes[:, k * pair_ref.shape[2] : (k + 1) * pair_ref.shape[2]]
            gate = gate_ref[row + k].astype(jnp.float32)
            old = pair_ref[row + k].astype(jnp.float32)
            out_ref[row + k] = (old + gate * change).astype(jnp.bfloat16)


def finish_kernel(pair_ref, gate_ref, w_out_ref, gain_ref, *rest):
    *product_refs, out_ref, scratch, twice = rest
    finish_rows(pair_ref, gate_ref, product_refs, w_out_ref, gain_ref, scratch, twice, out_ref)


def middle_kernel(
    sizes,
    count,
    chain_ref,
    block_mask_ref,
    pair_ref,
    gate_ref,
    w_out_ref,
    gain_out_ref,
    w_ref,
    w_gate_ref,
    gain_in_ref,
    *rest,
):
    product_refs, (out_ref, next_ref, *outs, update, twice, turned, picked, scratch) = rest[:count], rest[count:]
    pick_weights(w_ref, turned, picked)
    finish_rows(pair_ref, gate_ref, product_refs, w_out_ref, gain_out_ref, update, twice, out_ref)
    mask = tile_mask(chain_ref, block_mask_ref)
    project_all(out_ref, gain_in_ref[1:2], mask, w_gate_ref, next_ref, picked, scratch, outs, sizes, False)


def outgoing_kernel(left, left_pair, right, right_pair, right_far, right_near, outs, rights):
    *kept, pair, sent = outs
    for k, blocks in enumerate((right, right_pair, right_far, right_near)):
        rights[k] = jnp.concatenate(blocks, 1)
    lefts = jnp.concatenate([jnp.concatenate(left, 1), jnp.concatenate(left_pair, 1)], 0)
    size = lefts.shape[0] // 2
    here = lax.axis_index("row") ^ lax.axis_index("col")
    for place in range(4):
        terms = dot(lefts, rights[here ^ place], NT).astype(jnp.bfloat16)
        if place % 2:
            sent[0, place // 2, 0] = terms[:size]
            sent[1, place // 2, 0] = terms[size:]
        else:
            kept[place // 2][0] = terms[:size]
            pair[place // 2, 0] = terms[size:]


def incoming_kernel(left, left_core, left_pair, left_pair_core, right, right_pair, outs, lefts):
    *kept, pair, cross = outs
    for k in range(2):
        lefts[2 * k] = jnp.concatenate([left[k], left_pair[k]], 0)
        lefts[2 * k + 1] = jnp.concatenate([left_core[k], left_pair_core[k]], 0)
    rights = jnp.concatenate([jnp.concatenate(right, 1), jnp.concatenate(right_pair, 1)], 0)
    size = rights.shape[1] // 2
    here = lax.axis_index("row") ^ lax.axis_index("col")
    for place in range(4):
        terms = dot(lefts[here ^ place], rights, TN).astype(jnp.bfloat16)
        for k in range(2):
            block = terms[:, k * size : (k + 1) * size]
            if place == 0:
                kept[k][0] = block
            else:
                (pair, cross.at[0], cross.at[1])[place - 1][k, 0] = block


def pieces_kernel(kernel, count, *refs):
    blocks = [ref[(0,) * (len(ref.shape) - 2)] for ref in refs[:count]]
    kernel(*[blocks[k : k + 2] for k in range(0, count, 2)], refs[count:-1], refs[-1])


def params():
    return pltpu.CompilerParams(vmem_limit_bytes=VMEM, dimension_semantics=("arbitrary",))


def part(array, index):
    return pl.BlockSpec((1,) + array.shape[1:], lambda *_: (index,) + (0,) * (array.ndim - 1))


def whole(array):
    return pl.BlockSpec(array.shape, lambda *_: (0,) * array.ndim)


def tile_spec(tile):
    return pl.BlockSpec((STEP,) + tile.shape[1:], lambda r: (r, 0, 0))


def chunk_spec(shape):
    lead = shape[:-2]
    return pl.BlockSpec(lead + (STEP, shape[-1]), lambda r: (0,) * len(lead) + (r, 0))


def cost(flops, nbytes, special=0):
    return pl.CostEstimate(
        flops=int(flops * TOLD), bytes_accessed=int(nbytes * TOLD), transcendentals=int(special * TOLD)
    )


def part_outs(pair, sizes, apart):
    tile = pair.shape[:2]
    own = [(size,) + tile for size in sizes]
    both_sides = [(2,) + shape for shape in own]
    shapes = ([shape for shape in own for _ in range(2)] if apart else both_sides) + both_sides
    return [jax.ShapeDtypeStruct(shape, jnp.bfloat16) for shape in shapes], [chunk_spec(shape) for shape in shapes]


def part_scratch(pair, w_in, sizes):
    width = 2 * sum(sizes)
    return [
        pltpu.VMEM((w_in.shape[2], w_in.shape[1]), jnp.float32),
        pltpu.VMEM((4 * width, w_in.shape[1]), jnp.bfloat16),
        pltpu.VMEM((2, width * STEP, pair.shape[1]), jnp.float32),
    ]


def finish_scratch(pair, w_out):
    return [
        pltpu.VMEM((w_out.shape[1] * STEP, pair.shape[1]), jnp.float32),
        pltpu.VMEM((2 * w_out.shape[1], 2 * w_out.shape[2]), jnp.bfloat16),
    ]


def first_call(chain, block_mask, pair, w_in, w_gate, gain_in):
    outs, specs = part_outs(pair, OUT_SIZES, True)
    gate, *result = pl.pallas_call(
        functools.partial(first_kernel, OUT_SIZES),
        grid=(pair.shape[0] // STEP,),
        in_specs=[SMEM_SPEC, SMEM_SPEC, tile_spec(pair), part(w_in, 0), part(w_gate, 0), whole(gain_in)],
        out_specs=[tile_spec(pair)] + specs,
        out_shape=[jax.ShapeDtypeStruct(pair.shape, pair.dtype)] + outs,
        scratch_shapes=part_scratch(pair, w_in, OUT_SIZES),
        compiler_params=params(),
        cost_estimate=cost(2e9, 8 << 20, 4 << 20),
        name="project",
    )(chain, block_mask, pair, w_in, w_gate, gain_in)
    return gate, result


def finish_call(pair, gate, products, w_out, gain_wide):
    return pl.pallas_call(
        finish_kernel,
        grid=(pair.shape[0] // STEP,),
        in_specs=[tile_spec(pair), tile_spec(gate), part(w_out, 1), whole(gain_wide)]
        + [chunk_spec(p.shape) for p in products],
        out_specs=tile_spec(pair),
        out_shape=jax.ShapeDtypeStruct(pair.shape, pair.dtype),
        scratch_shapes=finish_scratch(pair, w_out),
        compiler_params=params(),
        cost_estimate=cost(1e9, 14 << 20, 4 << 20),
        name="finish",
    )(pair, gate, w_out, gain_wide, *products)


def middle_call(chain, block_mask, pair, gate, products, w_out, gain_wide, w_in, w_gate, gain_in):
    outs, specs = part_outs(pair, IN_SIZES, False)
    middle, gate, *result = pl.pallas_call(
        functools.partial(middle_kernel, IN_SIZES, len(products)),
        grid=(pair.shape[0] // STEP,),
        in_specs=[SMEM_SPEC, SMEM_SPEC, tile_spec(pair), tile_spec(gate), part(w_out, 0)]
        + [whole(gain_wide), part(w_in, 1), part(w_gate, 1), whole(gain_in)]
        + [chunk_spec(p.shape) for p in products],
        out_specs=[tile_spec(pair)] * 2 + specs,
        out_shape=[jax.ShapeDtypeStruct(pair.shape, pair.dtype)] * 2 + outs,
        scratch_shapes=finish_scratch(pair, w_out) + part_scratch(pair, w_in, IN_SIZES),
        compiler_params=params(),
        cost_estimate=cost(3e9, 18 << 20, 8 << 20),
        name="middle",
    )(chain, block_mask, pair, gate, w_out, gain_wide, w_in, w_gate, gain_in, *products)
    return middle, gate, result


def product_call(kernel, operands, channels, leads, scratch, name):
    pieces = [piece for operand in operands for piece in operand]
    size = pieces[0][0].shape[-1]

    def piece_spec(array, lead, first):
        return pl.BlockSpec((1,) * (len(lead) + 1) + (size, size), lambda c: lead + (first + c, 0, 0))

    def out_spec(lead):
        return pl.BlockSpec(lead + (1, size, size), lambda c: (0,) * len(lead) + (c, 0, 0))

    return pl.pallas_call(
        functools.partial(pieces_kernel, kernel, len(pieces)),
        grid=(channels,),
        in_specs=[piece_spec(*piece) for piece in pieces],
        out_specs=[out_spec(lead) for lead in leads],
        out_shape=[jax.ShapeDtypeStruct(lead + (channels, size, size), jnp.bfloat16) for lead in leads],
        scratch_shapes=[pltpu.VMEM(scratch, jnp.bfloat16)],
        compiler_params=params(),
        cost_estimate=cost(channels * 2 * (4 * size) ** 2 * size, channels * size * size * 2 * 20),
        name=name,
    )(*[piece[0] for piece in pieces])


WAYS = {
    "in": ("row", [(0, 1), (3, 2)]),
    "across": ("row", [(1, 2), (2, 1)]),
    "out": ("row", [(1, 0), (2, 3)]),
    "x": ("col", [(c, c ^ 2) for c in range(4)]),
    "core": ("col", [(c, c ^ 1) for c in range(4)]),
}


class Graph:
    def __init__(self, order):
        self.order, self.steps, self.made = order, {}, {}

    def add(self, name, operand, step):
        self.steps[name] = (operand, step)

    def send(self, name, way, operand):
        axis, pairs = WAYS[way]
        self.add(name, operand, lambda array: lax.ppermute(array, axis, pairs))

    def get(self, name):
        if name not in self.made:
            operand, step = self.steps[name]
            waits = [self.get(other) for other in self.order.get(name, ())]
            array = operand()
            if waits:
                array = lax.optimization_barrier((array, *waits))[0]
            self.made[name] = step(array)
        return self.made[name]


def pack(*columns):
    return jnp.stack([jnp.concatenate([column[k] for column in columns]) for k in range(2)])


def both(array, first=0, lead=()):
    return [(array, (k,) + lead, first) for k in range(2)]


def is_inner():
    row = lax.axis_index("row")
    return (row == 1) | (row == 2)


def shared_steps(graph, n, mine, other):
    inner = is_inner()
    get = graph.get

    def ready(k):
        return jnp.where(inner, mine(k), get(f"o{n}")[k])

    graph.send(f"o{n}", "out", other)
    graph.send(f"b{n}", "x", lambda: ready(1))
    graph.add(f"k{n}", lambda: ready(0), lambda array: array)


def finished(graph, count):
    return [graph.get(kind + str(n)) for kind in ("k", "b") for n in range(count)]


def outgoing(parts):
    count = len(OUT_SIZES)
    graph = Graph(OUT_ORDER)
    get, send = graph.get, graph.send
    for n in range(count):
        send(f"x{n}", "x", lambda n=n: parts[2 * count + n])
    later = lambda n, side: parts[2 * n + side]
    right_of = lambda n: (later(n, 0), get(f"x{n}")[0])
    left_of = lambda n: (later(n, 1), get(f"x{n}")[1])
    first = parts
    zero = OUT_SIZES[0]
    send("i0", "in", lambda: first[0])
    send("a0", "across", lambda: first[0])
    send("i1", "in", lambda: jnp.concatenate([get("x0")[0], first[1]]))
    send("a1", "across", lambda: jnp.concatenate([get("x0")[0], get("i0")]))

    def come(n):
        array, skip = get(f"i{n + 1}"), zero // 2 if n == 1 else OUT_SIZES[n - 1]
        return (array[0, skip:], array[1, skip:])

    def halves(array):
        return (array[: zero // 2], array[zero // 2 :])

    def inward(n):
        before = halves(get("x0")[1]) if n == 1 else left_of(n - 1)
        return pack(before, right_of(n)) if n < count else pack(before)

    def across(n):
        before = halves(get("i1")[:zero]) if n == 1 else come(n - 1)
        return pack(before, right_of(n)) if n < count else pack(before)

    for n in range(1, count + 1):
        send(f"i{n + 1}", "in", lambda n=n: inward(n))
        send(f"a{n + 1}", "across", lambda n=n: across(n))

    def product(n, left):
        size = left.shape[-1]
        if n == 0:
            x_left = lambda array: array[:, : zero // 2].reshape((zero,) + array.shape[2:])
            operands = [
                [(left, (), 0), (get("x0"), (1,), 0)],
                [(get("i1"), (), zero), (x_left(get("i2")), (), 0)],
                [(first[0], (), 0), (get("x0"), (0,), 0)],
                [(get("i0"), (), 0), (get("i1"), (), 0)],
                [(get("a1"), (), zero), (x_left(get("a2")), (), 0)],
                [(get("a0"), (), 0), (get("a1"), (), 0)],
            ]
        else:
            skip = zero // 2 if n == 1 else OUT_SIZES[n - 1]
            operands = [
                [(left, (), 0), (get(f"x{n}"), (1,), 0)],
                both(get(f"i{n + 2}")),
                [(later(n, 0), (), 0), (get(f"x{n}"), (0,), 0)],
                both(get(f"i{n + 1}"), skip),
                both(get(f"a{n + 2}")),
                both(get(f"a{n + 1}"), skip),
            ]
        leads = ((), (), (2,), (2, 2))
        return product_call(outgoing_kernel, operands, left.shape[0], leads, (4, size, 2 * size), "outgoing")

    for n in range(count):
        graph.add(f"p{n}", lambda n=n: later(n, 1), functools.partial(product, n))
        send(f"c{n}", "core", lambda n=n: get(f"p{n}")[3])
        shared_steps(
            graph,
            n,
            lambda k, n=n: get(f"p{n}")[k] + get(f"c{n}")[0, k],
            lambda n=n: get(f"p{n}")[2] + get(f"c{n}")[1],
        )
    return finished(graph, count)


def incoming(parts):
    count = len(IN_SIZES)
    graph = Graph(IN_ORDER)
    get, send = graph.get, graph.send
    for n in range(count):
        send(f"x{n}", "x", lambda n=n: parts[count + n])
    send("i0", "in", lambda: parts[0])
    send("i0x", "in", lambda: get("x0"))
    send("cl0", "core", lambda: parts[0])
    send("clx", "core", lambda: get("x0"))
    send("cp0", "core", lambda: get("i0"))
    send("cpx", "core", lambda: get("i0x"))
    for n in range(1, count):
        graph.add(f"j{n}", lambda n=n: parts[n], lambda own, n=n: jnp.stack([own, get(f"x{n}")], 1))
        send(f"i{n}", "in", lambda n=n: get(f"j{n}"))
        send(f"cl{n}", "core", lambda n=n: get(f"j{n}")[0])
        send(f"cp{n}", "core", lambda n=n: get(f"i{n}")[0])

    def product(n, own):
        size = own.shape[-1]
        if n == 0:
            side = lambda name, name_x, slot: [
                (own if name is None else get(name), (slot,), 0),
                (get(name_x), (slot,), 0),
            ]
            operands = [side(None, "x0", 0), side("cl0", "clx", 0), side("i0", "i0x", 0), side("cp0", "cpx", 0)]
            operands += [side(None, "x0", 1), side("i0", "i0x", 1)]
        else:
            side = lambda array, slot: [(array, (slot, k), 0) for k in range(2)]
            operands = [side(own, 0), both(get(f"cl{n}")), side(get(f"i{n}"), 0), both(get(f"cp{n}"))]
            operands += [side(own, 1), side(get(f"i{n}"), 1)]
        leads = ((), (), (2,), (2, 2))
        return product_call(incoming_kernel, operands, IN_SIZES[n], leads, (4, 2 * size, size), "incoming")

    for n in range(count):
        graph.add(f"p{n}", lambda n=n: get(f"j{n}") if n else parts[0], functools.partial(product, n))
        send(f"a{n}", "across", lambda n=n: get(f"p{n}")[3])
        shared_steps(
            graph,
            n,
            lambda k, n=n: get(f"p{n}")[k] + get(f"a{n}")[1, k],
            lambda n=n: get(f"p{n}")[2] + get(f"a{n}")[0],
        )
    return finished(graph, count)


def four_by_four(pair, chain, block_mask, w_in, w_gate, w_out, gain_in, gain_out):
    gain_wide = jnp.broadcast_to(gain_out[:, :, None, None], gain_out.shape + (1, pair.shape[1]))
    gate, parts = first_call(chain, block_mask, pair, w_in, w_gate, gain_in)
    products = outgoing(parts)
    middle, gate, parts = middle_call(
        chain, block_mask, pair, gate, products, w_out, gain_wide[0], w_in, w_gate, gain_in
    )
    products = incoming(parts)
    return finish_call(middle, gate, products, w_out, gain_wide[1])


def solution(mesh):
    four = mesh.shape["row"] == 4 and mesh.shape["col"] == 4
    return jax.shard_map(
        four_by_four if four else any_mesh,
        mesh=mesh,
        in_specs=(
            P(("group", "row"), "col", None),
            P("group"),
            P("group", None),
            P(),
            P(),
            P(),
            P(),
            P(),
        ),
        out_specs=P(("group", "row"), "col", None),
        check_vma=False,
    )
```

```python
import functools

import jax
import jax.numpy as jnp
from jax import lax
from jax.experimental import pallas as pl
from jax.experimental.pallas import tpu as pltpu
from jax.sharding import PartitionSpec as P

BLOCK = 128
EPS = 1e-05
OUT_SIZES = (8, 8, 8, 4, 4)
IN_SIZES = (8, 8, 8, 4, 4)
OUT_GROUPS = (1, 1, 1, 1, 1)
IN_GROUPS = (1, 1, 1, 1, 1)
OUT_ORDER = {'i1': ('i0',), 'i2': ('i1',), 'i3': ('i2',), 'i4': ('i3',), 'i5': ('i4',), 'i6': ('i5',), 'a1': ('a0',), 'a2': ('a1',), 'a3': ('a2',), 'a4': ('a3',), 'a5': ('a4', 'p1'), 'a6': ('a5',), 'x1': ('x0', 'a0'), 'x2': ('x1', 'a1'), 'x3': ('x2',), 'x4': ('x3',), 'o2': ('o1',), 'p2': ('o0',), 'p3': ('o1',), 'p4': ('o2',)}
IN_ORDER = {'i0x': ('i0',), 'i2': ('i1',), 'i3': ('i2',), 'i4': ('i3',), 'a1': ('a0',), 'a2': ('a1',), 'a3': ('a2',), 'x1': ('x0', 'i0'), 'o2': ('o1',), 'o3': ('o2',), 'o4': ('o3',), 'x2': ('i0x',), 'b0': ('x3',)}
STEP = 16
TOLD = 0.05
VMEM = 48 * 1024 * 1024


def broadcast(block, axis, owner):
    block = jnp.where(lax.axis_index(axis) == owner, block, jnp.zeros_like(block))
    return lax.psum(block, axis)


def layer_norm(values, gain):
    mean = jnp.mean(values, -1, keepdims=True)
    centred = values - mean
    spread = jnp.mean(centred * centred, -1, keepdims=True)
    return centred * lax.rsqrt(spread + EPS) * gain


def project(pair, tile_mask, w_in, w_gate, gain_in):
    normed = layer_norm(pair.astype(jnp.float32), gain_in).astype(jnp.bfloat16)
    hidden = jnp.dot(normed, w_in, preferred_element_type=jnp.float32)
    width = w_in.shape[1] // 4
    masked = tile_mask[..., None]
    left = (masked * jax.nn.sigmoid(hidden[..., width : 2 * width]) * hidden[..., :width]).astype(
        jnp.bfloat16
    )
    right = (
        masked * jax.nn.sigmoid(hidden[..., 3 * width :]) * hidden[..., 2 * width : 3 * width]
    ).astype(jnp.bfloat16)
    gate = jax.nn.sigmoid(jnp.dot(normed, w_gate, preferred_element_type=jnp.float32))
    return (left, right, gate)


def finish(pair, product, gate, w_out, gain_out):
    update = layer_norm(product, gain_out).astype(jnp.bfloat16)
    return (
        pair.astype(jnp.float32) + gate * jnp.dot(update, w_out, preferred_element_type=jnp.float32)
    ).astype(jnp.bfloat16)


def any_mesh(pair, chain, block_mask, w_in, w_gate, w_out, gain_in, gain_out):
    tile_rows = pair.shape[0]
    tile_cols = pair.shape[1]
    block_count = chain.shape[0]
    ratio = lax.axis_size("row") // lax.axis_size("col")
    row_index = lax.axis_index("row")
    col_index = lax.axis_index("col")
    same = chain[:, None] == chain[None, :]
    blocks = jnp.where(same | (block_mask == 1), 1.0, 0.0).astype(jnp.float32)
    labels = jnp.arange(block_count, dtype=jnp.int32)
    row_blocks = (row_index * tile_rows + jnp.arange(tile_rows, dtype=jnp.int32)) // BLOCK
    col_blocks = (col_index * tile_cols + jnp.arange(tile_cols, dtype=jnp.int32)) // BLOCK
    row_onehot = jnp.where(row_blocks[:, None] == labels[None, :], 1.0, 0.0).astype(jnp.float32)
    col_onehot = jnp.where(col_blocks[:, None] == labels[None, :], 1.0, 0.0).astype(jnp.float32)
    tile_mask = jnp.dot(jnp.dot(row_onehot, blocks), col_onehot.T)
    left, right, gate = project(pair, tile_mask, w_in[0], w_gate[0], gain_in[0])
    partial_terms = jnp.einsum(
        "ikc,jkc->ijc",
        left,
        lax.all_gather(right, "row", axis=0, tiled=True),
        preferred_element_type=jnp.float32,
    )
    product = lax.psum_scatter(
        partial_terms.astype(jnp.bfloat16), "col", scatter_dimension=1, tiled=True
    ).astype(jnp.float32)
    middle = finish(pair, product, gate, w_out[0], gain_out[0])
    left, right, gate = project(middle, tile_mask, w_in[1], w_gate[1], gain_in[1])
    left_cols = lax.all_gather(left, "row", axis=0, tiled=True)
    start_col = row_index % ratio * tile_rows
    left_slice = lax.dynamic_slice_in_dim(left_cols, start_col, tile_rows, 1)
    left_mine = broadcast(left_slice, "col", row_index // ratio)
    product = jnp.einsum(
        "kic,kjc->ijc",
        left_mine,
        lax.all_gather(right, "row", axis=0, tiled=True),
        preferred_element_type=jnp.float32,
    )
    return finish(middle, product, gate, w_out[1], gain_out[1])


NN = (((1,), (0,)), ((), ()))
NT = (((1,), (1,)), ((), ()))
TN = (((0,), (0,)), ((), ()))
SMEM_SPEC = pl.BlockSpec(memory_space=pltpu.SMEM)


def dot(a, b, dims=NN):
    return lax.dot_general(a, b, dims, preferred_element_type=jnp.float32)


def norm_rows(rows, gain):
    channels = rows.shape[-1]
    place = lax.broadcasted_iota(jnp.int32, (channels, channels), 0)
    same = place == lax.broadcasted_iota(jnp.int32, (channels, channels), 1)
    centre = jnp.where(same, 1.0 - 1.0 / channels, -1.0 / channels).astype(jnp.bfloat16)
    mean_of = jnp.full((2 * channels, channels), 1.0 / channels, jnp.bfloat16)
    centred = dot(rows, centre)
    square = centred * centred
    high = square.astype(jnp.bfloat16)
    low = (square - high.astype(jnp.float32)).astype(jnp.bfloat16)
    spread = dot(jnp.concatenate([high, low], 1), mean_of)
    return (centred * lax.rsqrt(spread + EPS) * gain).astype(jnp.bfloat16)


def tile_mask(chain_ref, block_mask_ref):
    row, col = lax.axis_index("row"), lax.axis_index("col")
    seen = (chain_ref[row] == chain_ref[col]) | (block_mask_ref[row, col] == 1)
    return jnp.where(seen, 1.0, 0.0).astype(jnp.float32)


def pick_weights(w_ref, w_gate_ref, mask, turned, picked, picked_gate):
    @pl.when(pl.program_id(0) == 0)
    def _():
        turned[...] = w_ref[0].astype(jnp.float32).T
        half = turned.shape[0] // 8
        x = lax.axis_index("col") // 2
        rows = []
        for kind in range(4):
            for other in (x, 1 - x):
                some = turned[pl.ds(pl.multiple_of((2 * kind + other) * half, 8), half), :]
                rows.append(some * (0.5 if kind % 2 else 0.5 * mask))
        picked[...] = jnp.concatenate(rows, 0).astype(jnp.bfloat16)
        picked_gate[...] = (w_gate_ref[0].astype(jnp.float32) * 0.5).astype(jnp.bfloat16)


def project_part(normed, picked, scratch, sides, sizes):
    hidden = dot(picked[...], normed, NT)
    width = picked.shape[0] // 4
    cols = normed.shape[0] // STEP
    for side, refs in enumerate(sides):
        values = hidden[2 * side * width : (2 * side + 1) * width]
        gates = hidden[(2 * side + 1) * width : (2 * side + 2) * width]
        kept = (jnp.tanh(gates) + 1.0) * values
        for row in range(STEP):
            scratch[side, pl.ds(row, width, stride=STEP), :] = kept[:, row * cols : (row + 1) * cols]
        done = 0
        for ref, size in zip(refs, sizes * 2):
            rows = scratch[side, done * STEP : (done + size) * STEP, :]
            ref[...] = rows.astype(jnp.bfloat16).reshape(ref.shape)
            done += size


def split_sides(outs, count, apart):
    lefts, rights = [], []
    for n in range(count):
        if apart:
            rights.append(outs[2 * n])
            lefts.append(outs[2 * n + 1])
        else:
            lefts.append(outs[n].at[0])
            rights.append(outs[n].at[1])
    for ref in outs[-count:]:
        lefts.append(ref.at[1 if apart else 0])
        rights.append(ref.at[0 if apart else 1])
    return lefts, rights


def project_all(rows, gain, gate_ref, picked, picked_gate, scratch, outs, sizes, apart):
    normed = norm_rows(rows, gain)
    project_part(normed, picked, scratch, split_sides(outs, len(sizes), apart), sizes)
    gate = 0.5 * jnp.tanh(dot(normed, picked_gate[...])) + 0.5
    gate_ref[...] = gate.astype(gate_ref.dtype).reshape(gate_ref.shape)


def first_kernel(sizes, chain_ref, block_mask_ref, pair_ref, w_ref, w_gate_ref, gain_ref, gate_ref, *rest):
    *outs, turned, picked, picked_gate, scratch = rest
    pick_weights(w_ref, w_gate_ref, tile_mask(chain_ref, block_mask_ref), turned, picked, picked_gate)
    rows = pair_ref[...].reshape(-1, pair_ref.shape[-1])
    project_all(rows, gain_ref[0:1], gate_ref, picked, picked_gate, scratch, outs, sizes, True)


def finish_rows(pair_ref, gate_ref, product_refs, w_out_ref, gain_ref, scratch, twice, out_ref):
    width = w_out_ref.shape[1]
    half = width // 2
    cols = pair_ref.shape[1]
    x = lax.axis_index("col") // 2
    mine, others = pl.multiple_of(x * half, half), pl.multiple_of((1 - x) * half, half)

    @pl.when(pl.program_id(0) == 0)
    def _():
        w_out = jnp.concatenate([w_out_ref[0, pl.ds(mine, half)], w_out_ref[0, pl.ds(others, half)]], 0)
        none = jnp.zeros_like(w_out)
        twice[...] = jnp.concatenate(
            [jnp.concatenate([w_out, none], 1), jnp.concatenate([none, w_out], 1)], 0
        )

    gain = jnp.concatenate([gain_ref[pl.ds(mine, half)], gain_ref[pl.ds(others, half)]], 0)
    product = jnp.concatenate([ref[...] for ref in product_refs], 0).astype(jnp.float32)
    mean = jnp.sum(product, 0, keepdims=True) * (1.0 / width)
    centred = product - mean
    spread = jnp.sum(centred * centred, 0, keepdims=True) * (1.0 / width)
    update = centred * lax.rsqrt(spread + EPS) * gain
    scratch[...] = update.reshape(width * STEP, cols)
    for row in range(0, STEP, 2):
        two = jnp.concatenate(
            [scratch[pl.ds(row, width, stride=STEP), :], scratch[pl.ds(row + 1, width, stride=STEP), :]], 0
        )
        changes = dot(two.astype(jnp.bfloat16), twice[...], TN)
        for k in range(2):
            change = changes[:, k * pair_ref.shape[2] : (k + 1) * pair_ref.shape[2]]
            gate = gate_ref[row + k].astype(jnp.float32)
            old = pair_ref[row + k].astype(jnp.float32)
            out_ref[row + k] = (old + gate * change).astype(jnp.bfloat16)


def finish_kernel(pair_ref, gate_ref, w_out_ref, gain_ref, *rest):
    *product_refs, out_ref, scratch, twice = rest
    finish_rows(pair_ref, gate_ref, product_refs, w_out_ref, gain_ref, scratch, twice, out_ref)


def middle_kernel(
    sizes,
    count,
    chain_ref,
    block_mask_ref,
    pair_ref,
    gate_ref,
    w_out_ref,
    gain_out_ref,
    w_ref,
    w_gate_ref,
    gain_in_ref,
    *rest,
):
    product_refs, (out_ref, next_ref, *outs) = rest[:count], rest[count:]
    *outs, update, twice, turned, picked, picked_gate, scratch = outs
    pick_weights(w_ref, w_gate_ref, tile_mask(chain_ref, block_mask_ref), turned, picked, picked_gate)
    finish_rows(pair_ref, gate_ref, product_refs, w_out_ref, gain_out_ref, update, twice, out_ref)
    rows = out_ref[...].reshape(-1, out_ref.shape[-1])
    project_all(rows, gain_in_ref[1:2], next_ref, picked, picked_gate, scratch, outs, sizes, False)


def outgoing_kernel(left, left_pair, right, right_pair, right_far, right_near, outs, rights):
    *kept, pair, sent = outs
    for k, blocks in enumerate((right, right_pair, right_far, right_near)):
        rights[k] = jnp.concatenate(blocks, 1)
    lefts = jnp.concatenate([jnp.concatenate(left, 1), jnp.concatenate(left_pair, 1)], 0)
    size = lefts.shape[0] // 2
    here = lax.axis_index("row") ^ lax.axis_index("col")
    for place in range(4):
        terms = dot(lefts, rights[here ^ place], NT).astype(jnp.bfloat16)
        if place % 2:
            sent[0, place // 2, 0] = terms[:size]
            sent[1, place // 2, 0] = terms[size:]
        else:
            kept[place // 2][0] = terms[:size]
            pair[place // 2, 0] = terms[size:]


def incoming_kernel(left, left_core, left_pair, left_pair_core, right, right_pair, outs, lefts):
    *kept, pair, cross = outs
    for k in range(2):
        lefts[2 * k] = jnp.concatenate([left[k], left_pair[k]], 0)
        lefts[2 * k + 1] = jnp.concatenate([left_core[k], left_pair_core[k]], 0)
    rights = jnp.concatenate([jnp.concatenate(right, 1), jnp.concatenate(right_pair, 1)], 0)
    size = rights.shape[1] // 2
    here = lax.axis_index("row") ^ lax.axis_index("col")
    for place in range(4):
        terms = dot(lefts[here ^ place], rights, TN).astype(jnp.bfloat16)
        for k in range(2):
            block = terms[:, k * size : (k + 1) * size]
            if place == 0:
                kept[k][0] = block
            else:
                (pair, cross.at[0], cross.at[1])[place - 1][k, 0] = block


def pieces_kernel(kernel, count, *refs):
    blocks = [ref[(0,) * (len(ref.shape) - 2)] for ref in refs[:count]]
    kernel(*[blocks[k : k + 2] for k in range(0, count, 2)], refs[count:-1], refs[-1])


def params():
    return pltpu.CompilerParams(vmem_limit_bytes=VMEM, dimension_semantics=("arbitrary",))


def part(array, index):
    return pl.BlockSpec((1,) + array.shape[1:], lambda *_: (index,) + (0,) * (array.ndim - 1))


def whole(array):
    return pl.BlockSpec(array.shape, lambda *_: (0,) * array.ndim)


def tile_spec(tile):
    return pl.BlockSpec((STEP,) + tile.shape[1:], lambda r: (r, 0, 0))


def chunk_spec(shape):
    lead = shape[:-2]
    return pl.BlockSpec(lead + (STEP, shape[-1]), lambda r: (0,) * len(lead) + (r, 0))


def cost(flops, nbytes, special=0):
    return pl.CostEstimate(
        flops=int(flops * TOLD), bytes_accessed=int(nbytes * TOLD), transcendentals=int(special * TOLD)
    )


def part_outs(pair, sizes, apart):
    tile = pair.shape[:2]
    own = [(size,) + tile for size in sizes]
    both_sides = [(2,) + shape for shape in own]
    shapes = ([shape for shape in own for _ in range(2)] if apart else both_sides) + both_sides
    return [jax.ShapeDtypeStruct(shape, jnp.bfloat16) for shape in shapes], [chunk_spec(shape) for shape in shapes]


def part_scratch(pair, w_in, sizes):
    width = 2 * sum(sizes)
    return [
        pltpu.VMEM((w_in.shape[2], w_in.shape[1]), jnp.float32),
        pltpu.VMEM((4 * width, w_in.shape[1]), jnp.bfloat16),
        pltpu.VMEM((w_in.shape[1], w_in.shape[1]), jnp.bfloat16),
        pltpu.VMEM((2, width * STEP, pair.shape[1]), jnp.float32),
    ]


def finish_scratch(pair, w_out):
    return [
        pltpu.VMEM((w_out.shape[1] * STEP, pair.shape[1]), jnp.float32),
        pltpu.VMEM((2 * w_out.shape[1], 2 * w_out.shape[2]), jnp.bfloat16),
    ]


def first_call(chain, block_mask, pair, w_in, w_gate, gain_in):
    outs, specs = part_outs(pair, OUT_SIZES, True)
    gate, *result = pl.pallas_call(
        functools.partial(first_kernel, OUT_SIZES),
        grid=(pair.shape[0] // STEP,),
        in_specs=[SMEM_SPEC, SMEM_SPEC, tile_spec(pair), part(w_in, 0), part(w_gate, 0), whole(gain_in)],
        out_specs=[tile_spec(pair)] + specs,
        out_shape=[jax.ShapeDtypeStruct(pair.shape, pair.dtype)] + outs,
        scratch_shapes=part_scratch(pair, w_in, OUT_SIZES),
        compiler_params=params(),
        cost_estimate=cost(2e9, 8 << 20, 4 << 20),
        name="project",
    )(chain, block_mask, pair, w_in, w_gate, gain_in)
    return gate, result


def finish_call(pair, gate, products, w_out, gain_wide):
    return pl.pallas_call(
        finish_kernel,
        grid=(pair.shape[0] // STEP,),
        in_specs=[tile_spec(pair), tile_spec(gate), part(w_out, 1), whole(gain_wide)]
        + [chunk_spec(p.shape) for p in products],
        out_specs=tile_spec(pair),
        out_shape=jax.ShapeDtypeStruct(pair.shape, pair.dtype),
        scratch_shapes=finish_scratch(pair, w_out),
        compiler_params=params(),
        cost_estimate=cost(1e9, 14 << 20, 4 << 20),
        name="finish",
    )(pair, gate, w_out, gain_wide, *products)


def middle_call(chain, block_mask, pair, gate, products, w_out, gain_wide, w_in, w_gate, gain_in):
    outs, specs = part_outs(pair, IN_SIZES, False)
    middle, gate, *result = pl.pallas_call(
        functools.partial(middle_kernel, IN_SIZES, len(products)),
        grid=(pair.shape[0] // STEP,),
        in_specs=[SMEM_SPEC, SMEM_SPEC, tile_spec(pair), tile_spec(gate), part(w_out, 0)]
        + [whole(gain_wide), part(w_in, 1), part(w_gate, 1), whole(gain_in)]
        + [chunk_spec(p.shape) for p in products],
        out_specs=[tile_spec(pair)] * 2 + specs,
        out_shape=[jax.ShapeDtypeStruct(pair.shape, pair.dtype)] * 2 + outs,
        scratch_shapes=finish_scratch(pair, w_out) + part_scratch(pair, w_in, IN_SIZES),
        compiler_params=params(),
        cost_estimate=cost(3e9, 18 << 20, 8 << 20),
        name="middle",
    )(chain, block_mask, pair, gate, w_out, gain_wide, w_in, w_gate, gain_in, *products)
    return middle, gate, result


def product_call(kernel, operands, channels, leads, scratch, name):
    pieces = [piece for operand in operands for piece in operand]
    size = pieces[0][0].shape[-1]

    def piece_spec(array, lead, first):
        return pl.BlockSpec((1,) * (len(lead) + 1) + (size, size), lambda c: lead + (first + c, 0, 0))

    def out_spec(lead):
        return pl.BlockSpec(lead + (1, size, size), lambda c: (0,) * len(lead) + (c, 0, 0))

    return pl.pallas_call(
        functools.partial(pieces_kernel, kernel, len(pieces)),
        grid=(channels,),
        in_specs=[piece_spec(*piece) for piece in pieces],
        out_specs=[out_spec(lead) for lead in leads],
        out_shape=[jax.ShapeDtypeStruct(lead + (channels, size, size), jnp.bfloat16) for lead in leads],
        scratch_shapes=[pltpu.VMEM(scratch, jnp.bfloat16)],
        compiler_params=params(),
        cost_estimate=cost(channels * 2 * (4 * size) ** 2 * size, channels * size * size * 2 * 20),
        name=name,
    )(*[piece[0] for piece in pieces])


WAYS = {
    "in": ("row", [(0, 1), (3, 2)]),
    "across": ("row", [(1, 2), (2, 1)]),
    "out": ("row", [(1, 0), (2, 3)]),
    "x": ("col", [(c, c ^ 2) for c in range(4)]),
    "core": ("col", [(c, c ^ 1) for c in range(4)]),
}


class Graph:
    def __init__(self, order):
        self.order, self.steps, self.made = order, {}, {}

    def add(self, name, operand, step):
        self.steps[name] = (operand, step)

    def send(self, name, way, operand):
        axis, pairs = WAYS[way]
        self.add(name, operand, lambda array: lax.ppermute(array, axis, pairs))

    def get(self, name):
        if name not in self.made:
            operand, step = self.steps[name]
            waits = [self.get(other) for other in self.order.get(name, ())]
            array = operand()
            if waits:
                array = lax.optimization_barrier((array, *waits))[0]
            self.made[name] = step(array)
        return self.made[name]


def pack(*columns):
    return jnp.stack([jnp.concatenate([column[k] for column in columns]) for k in range(2)])


def both(array, first=0, lead=()):
    return [(array, (k,) + lead, first) for k in range(2)]


def is_inner():
    row = lax.axis_index("row")
    return (row == 1) | (row == 2)


def shared_steps(graph, groups, mine, other):
    inner = is_inner()
    get = graph.get
    first, names = 0, []

    def joined(arrays, axis):
        return arrays[0] if len(arrays) == 1 else jnp.concatenate(arrays, axis)

    for g, size in enumerate(groups):
        chunks = range(first, first + size)
        first += size

        def ready(k, g=g, chunks=chunks):
            return jnp.where(inner, joined([mine(n, k) for n in chunks], 0), get(f"o{g}")[k])

        graph.send(f"o{g}", "out", lambda chunks=chunks: joined([other(n) for n in chunks], 1))
        graph.send(f"b{g}", "x", lambda ready=ready: ready(1))
        graph.add(f"k{g}", lambda ready=ready: ready(0), lambda array: array)
    return [get(kind + str(g)) for kind in ("k", "b") for g in range(len(groups))]


def outgoing(parts):
    count = len(OUT_SIZES)
    graph = Graph(OUT_ORDER)
    get, send = graph.get, graph.send
    for n in range(count):
        send(f"x{n}", "x", lambda n=n: parts[2 * count + n])
    later = lambda n, side: parts[2 * n + side]
    right_of = lambda n: (later(n, 0), get(f"x{n}")[0])
    left_of = lambda n: (later(n, 1), get(f"x{n}")[1])
    first = parts
    zero = OUT_SIZES[0]
    send("i0", "in", lambda: first[0])
    send("a0", "across", lambda: first[0])
    send("i1", "in", lambda: jnp.concatenate([get("x0")[0], first[1]]))
    send("a1", "across", lambda: jnp.concatenate([get("x0")[0], get("i0")]))

    def come(n):
        array, skip = get(f"i{n + 1}"), zero // 2 if n == 1 else OUT_SIZES[n - 1]
        return (array[0, skip:], array[1, skip:])

    def halves(array):
        return (array[: zero // 2], array[zero // 2 :])

    def inward(n):
        before = halves(get("x0")[1]) if n == 1 else left_of(n - 1)
        return pack(before, right_of(n)) if n < count else pack(before)

    def across(n):
        before = halves(get("i1")[:zero]) if n == 1 else come(n - 1)
        return pack(before, right_of(n)) if n < count else pack(before)

    for n in range(1, count + 1):
        send(f"i{n + 1}", "in", lambda n=n: inward(n))
        send(f"a{n + 1}", "across", lambda n=n: across(n))

    def product(n, left):
        size = left.shape[-1]
        if n == 0:
            x_left = lambda array: array[:, : zero // 2].reshape((zero,) + array.shape[2:])
            operands = [
                [(left, (), 0), (get("x0"), (1,), 0)],
                [(get("i1"), (), zero), (x_left(get("i2")), (), 0)],
                [(first[0], (), 0), (get("x0"), (0,), 0)],
                [(get("i0"), (), 0), (get("i1"), (), 0)],
                [(get("a1"), (), zero), (x_left(get("a2")), (), 0)],
                [(get("a0"), (), 0), (get("a1"), (), 0)],
            ]
        else:
            skip = zero // 2 if n == 1 else OUT_SIZES[n - 1]
            operands = [
                [(left, (), 0), (get(f"x{n}"), (1,), 0)],
                both(get(f"i{n + 2}")),
                [(later(n, 0), (), 0), (get(f"x{n}"), (0,), 0)],
                both(get(f"i{n + 1}"), skip),
                both(get(f"a{n + 2}")),
                both(get(f"a{n + 1}"), skip),
            ]
        leads = ((), (), (2,), (2, 2))
        return product_call(outgoing_kernel, operands, left.shape[0], leads, (4, size, 2 * size), "outgoing")

    for n in range(count):
        graph.add(f"p{n}", lambda n=n: later(n, 1), functools.partial(product, n))
        send(f"c{n}", "core", lambda n=n: get(f"p{n}")[3])
    return shared_steps(
        graph,
        OUT_GROUPS,
        lambda n, k: get(f"p{n}")[k] + get(f"c{n}")[0, k],
        lambda n: get(f"p{n}")[2] + get(f"c{n}")[1],
    )


def incoming(parts):
    count = len(IN_SIZES)
    graph = Graph(IN_ORDER)
    get, send = graph.get, graph.send
    for n in range(count):
        send(f"x{n}", "x", lambda n=n: parts[count + n])
    send("i0", "in", lambda: parts[0])
    send("i0x", "in", lambda: get("x0"))
    send("cl0", "core", lambda: parts[0])
    send("clx", "core", lambda: get("x0"))
    send("cp0", "core", lambda: get("i0"))
    send("cpx", "core", lambda: get("i0x"))
    for n in range(1, count):
        graph.add(f"j{n}", lambda n=n: parts[n], lambda own, n=n: jnp.stack([own, get(f"x{n}")], 1))
        send(f"i{n}", "in", lambda n=n: get(f"j{n}"))
        send(f"cl{n}", "core", lambda n=n: get(f"j{n}")[0])
        send(f"cp{n}", "core", lambda n=n: get(f"i{n}")[0])

    def product(n, own):
        size = own.shape[-1]
        if n == 0:
            side = lambda name, name_x, slot: [
                (own if name is None else get(name), (slot,), 0),
                (get(name_x), (slot,), 0),
            ]
            operands = [side(None, "x0", 0), side("cl0", "clx", 0), side("i0", "i0x", 0), side("cp0", "cpx", 0)]
            operands += [side(None, "x0", 1), side("i0", "i0x", 1)]
        else:
            side = lambda array, slot: [(array, (slot, k), 0) for k in range(2)]
            operands = [side(own, 0), both(get(f"cl{n}")), side(get(f"i{n}"), 0), both(get(f"cp{n}"))]
            operands += [side(own, 1), side(get(f"i{n}"), 1)]
        leads = ((), (), (2,), (2, 2))
        return product_call(incoming_kernel, operands, IN_SIZES[n], leads, (4, 2 * size, size), "incoming")

    for n in range(count):
        graph.add(f"p{n}", lambda n=n: get(f"j{n}") if n else parts[0], functools.partial(product, n))
        send(f"a{n}", "across", lambda n=n: get(f"p{n}")[3])
    return shared_steps(
        graph,
        IN_GROUPS,
        lambda n, k: get(f"p{n}")[k] + get(f"a{n}")[1, k],
        lambda n: get(f"p{n}")[2] + get(f"a{n}")[0],
    )


def four_by_four(pair, chain, block_mask, w_in, w_gate, w_out, gain_in, gain_out):
    gain_wide = jnp.broadcast_to(gain_out[:, :, None, None], gain_out.shape + (1, pair.shape[1]))
    gate, parts = first_call(chain, block_mask, pair, w_in, w_gate, gain_in)
    products = outgoing(parts)
    middle, gate, parts = middle_call(
        chain, block_mask, pair, gate, products, w_out, gain_wide[0], w_in, w_gate, gain_in
    )
    products = incoming(parts)
    return finish_call(middle, gate, products, w_out, gain_wide[1])


def solution(mesh):
    four = mesh.shape["row"] == 4 and mesh.shape["col"] == 4
    return jax.shard_map(
        four_by_four if four else any_mesh,
        mesh=mesh,
        in_specs=(
            P(("group", "row"), "col", None),
            P("group"),
            P("group", None),
            P(),
            P(),
            P(),
            P(),
            P(),
        ),
        out_specs=P(("group", "row"), "col", None),
        check_vma=False,
    )
```

```python
import functools

import jax
import jax.numpy as jnp
from jax import lax
from jax.experimental import pallas as pl
from jax.experimental.pallas import tpu as pltpu
from jax.sharding import PartitionSpec as P

BLOCK = 128
EPS = 1e-05
OUT_SIZES = (8, 8, 8, 4, 4)
IN_SIZES = (8, 8, 8, 4, 4)
OUT_GROUPS = (1, 1, 1, 1, 1)
IN_GROUPS = (1, 1, 1, 1, 1)
OUT_ORDER = {'i1': ('i0',), 'i2': ('i1',), 'i3': ('i2',), 'i4': ('i3',), 'i5': ('i4',), 'i6': ('i5',), 'a1': ('a0',), 'a2': ('a1',), 'a3': ('a2',), 'a4': ('a3',), 'a5': ('a4', 'p1'), 'a6': ('a5',), 'x2': ('x1', 'a1'), 'x3': ('x2',), 'x4': ('x3',), 'o2': ('o1',), 'x1': ('a0',), 'p2': ('o0',), 'p3': ('o1',), 'p4': ('o2',)}
IN_ORDER = {'i0x': ('i0',), 'i2': ('i1',), 'i3': ('i2',), 'i4': ('i3',), 'a1': ('a0', 'i1'), 'x1': ('x0', 'i0'), 'o2': ('o1',), 'o3': ('o2',), 'o4': ('o3',), 'x2': ('i0x',), 'b0': ('x3',)}
STEP = 16
TOLD = 0.05
VMEM = 28 * 1024 * 1024
PRODUCT_VMEM = 10 * 1024 * 1024


def broadcast(block, axis, owner):
    block = jnp.where(lax.axis_index(axis) == owner, block, jnp.zeros_like(block))
    return lax.psum(block, axis)


def layer_norm(values, gain):
    mean = jnp.mean(values, -1, keepdims=True)
    centred = values - mean
    spread = jnp.mean(centred * centred, -1, keepdims=True)
    return centred * lax.rsqrt(spread + EPS) * gain


def project(pair, tile_mask, w_in, w_gate, gain_in):
    normed = layer_norm(pair.astype(jnp.float32), gain_in).astype(jnp.bfloat16)
    hidden = jnp.dot(normed, w_in, preferred_element_type=jnp.float32)
    width = w_in.shape[1] // 4
    masked = tile_mask[..., None]
    left = (masked * jax.nn.sigmoid(hidden[..., width : 2 * width]) * hidden[..., :width]).astype(
        jnp.bfloat16
    )
    right = (
        masked * jax.nn.sigmoid(hidden[..., 3 * width :]) * hidden[..., 2 * width : 3 * width]
    ).astype(jnp.bfloat16)
    gate = jax.nn.sigmoid(jnp.dot(normed, w_gate, preferred_element_type=jnp.float32))
    return (left, right, gate)


def finish(pair, product, gate, w_out, gain_out):
    update = layer_norm(product, gain_out).astype(jnp.bfloat16)
    return (
        pair.astype(jnp.float32) + gate * jnp.dot(update, w_out, preferred_element_type=jnp.float32)
    ).astype(jnp.bfloat16)


def any_mesh(pair, chain, block_mask, w_in, w_gate, w_out, gain_in, gain_out):
    tile_rows = pair.shape[0]
    tile_cols = pair.shape[1]
    block_count = chain.shape[0]
    ratio = lax.axis_size("row") // lax.axis_size("col")
    row_index = lax.axis_index("row")
    col_index = lax.axis_index("col")
    same = chain[:, None] == chain[None, :]
    blocks = jnp.where(same | (block_mask == 1), 1.0, 0.0).astype(jnp.float32)
    labels = jnp.arange(block_count, dtype=jnp.int32)
    row_blocks = (row_index * tile_rows + jnp.arange(tile_rows, dtype=jnp.int32)) // BLOCK
    col_blocks = (col_index * tile_cols + jnp.arange(tile_cols, dtype=jnp.int32)) // BLOCK
    row_onehot = jnp.where(row_blocks[:, None] == labels[None, :], 1.0, 0.0).astype(jnp.float32)
    col_onehot = jnp.where(col_blocks[:, None] == labels[None, :], 1.0, 0.0).astype(jnp.float32)
    tile_mask = jnp.dot(jnp.dot(row_onehot, blocks), col_onehot.T)
    left, right, gate = project(pair, tile_mask, w_in[0], w_gate[0], gain_in[0])
    partial_terms = jnp.einsum(
        "ikc,jkc->ijc",
        left,
        lax.all_gather(right, "row", axis=0, tiled=True),
        preferred_element_type=jnp.float32,
    )
    product = lax.psum_scatter(
        partial_terms.astype(jnp.bfloat16), "col", scatter_dimension=1, tiled=True
    ).astype(jnp.float32)
    middle = finish(pair, product, gate, w_out[0], gain_out[0])
    left, right, gate = project(middle, tile_mask, w_in[1], w_gate[1], gain_in[1])
    left_cols = lax.all_gather(left, "row", axis=0, tiled=True)
    start_col = row_index % ratio * tile_rows
    left_slice = lax.dynamic_slice_in_dim(left_cols, start_col, tile_rows, 1)
    left_mine = broadcast(left_slice, "col", row_index // ratio)
    product = jnp.einsum(
        "kic,kjc->ijc",
        left_mine,
        lax.all_gather(right, "row", axis=0, tiled=True),
        preferred_element_type=jnp.float32,
    )
    return finish(middle, product, gate, w_out[1], gain_out[1])


NN = (((1,), (0,)), ((), ()))
NT = (((1,), (1,)), ((), ()))
TN = (((0,), (0,)), ((), ()))
SMEM_SPEC = pl.BlockSpec(memory_space=pltpu.SMEM)


def dot(a, b, dims=NN):
    return lax.dot_general(a, b, dims, preferred_element_type=jnp.float32)


def norm_rows(rows, gain):
    channels = rows.shape[-1]
    place = lax.broadcasted_iota(jnp.int32, (channels, channels), 0)
    same = place == lax.broadcasted_iota(jnp.int32, (channels, channels), 1)
    centre = jnp.where(same, 1.0 - 1.0 / channels, -1.0 / channels).astype(jnp.bfloat16)
    mean_of = jnp.full((2 * channels, channels), 1.0 / channels, jnp.bfloat16)
    centred = dot(rows, centre)
    square = centred * centred
    high = square.astype(jnp.bfloat16)
    low = (square - high.astype(jnp.float32)).astype(jnp.bfloat16)
    spread = dot(jnp.concatenate([high, low], 1), mean_of)
    return (centred * lax.rsqrt(spread + EPS) * gain).astype(jnp.bfloat16)


def tile_mask(chain_ref, block_mask_ref):
    row, col = lax.axis_index("row"), lax.axis_index("col")
    seen = (chain_ref[row] == chain_ref[col]) | (block_mask_ref[row, col] == 1)
    return jnp.where(seen, 1.0, 0.0).astype(jnp.float32)


def pick_weights(w_ref, w_gate_ref, mask, turned, picked, picked_gate):
    @pl.when(pl.program_id(0) == 0)
    def _():
        turned[...] = w_ref[0].astype(jnp.float32).T
        half = turned.shape[0] // 8
        x = lax.axis_index("col") // 2
        rows = []
        for kind in range(4):
            for other in (x, 1 - x):
                some = turned[pl.ds(pl.multiple_of((2 * kind + other) * half, 8), half), :]
                rows.append(some * (0.5 if kind % 2 else 0.5 * mask))
        picked[...] = jnp.concatenate(rows, 0).astype(jnp.bfloat16)
        picked_gate[...] = (w_gate_ref[0].astype(jnp.float32) * 0.5).astype(jnp.bfloat16)


def project_part(normed, picked, scratch, sides, sizes):
    hidden = dot(picked[...], normed, NT)
    width = picked.shape[0] // 4
    cols = normed.shape[0] // STEP
    for side, refs in enumerate(sides):
        values = hidden[2 * side * width : (2 * side + 1) * width]
        gates = hidden[(2 * side + 1) * width : (2 * side + 2) * width]
        kept = (jnp.tanh(gates) + 1.0) * values
        for row in range(STEP):
            scratch[side, pl.ds(row, width, stride=STEP), :] = kept[:, row * cols : (row + 1) * cols]
        done = 0
        for ref, size in zip(refs, sizes * 2):
            rows = scratch[side, done * STEP : (done + size) * STEP, :]
            ref[...] = rows.astype(jnp.bfloat16).reshape(ref.shape)
            done += size


def split_sides(outs, count, apart):
    lefts, rights = [], []
    for n in range(count):
        if apart:
            rights.append(outs[2 * n])
            lefts.append(outs[2 * n + 1])
        else:
            lefts.append(outs[n].at[0])
            rights.append(outs[n].at[1])
    for ref in outs[-count:]:
        lefts.append(ref.at[1 if apart else 0])
        rights.append(ref.at[0 if apart else 1])
    return lefts, rights


def project_all(rows, gain, gate_ref, picked, picked_gate, scratch, outs, sizes, apart):
    normed = norm_rows(rows, gain)
    project_part(normed, picked, scratch, split_sides(outs, len(sizes), apart), sizes)
    gate = 0.5 * jnp.tanh(dot(normed, picked_gate[...])) + 0.5
    gate_ref[...] = gate.astype(gate_ref.dtype).reshape(gate_ref.shape)


def first_kernel(sizes, chain_ref, block_mask_ref, pair_ref, w_ref, w_gate_ref, gain_ref, gate_ref, *rest):
    *outs, turned, picked, picked_gate, scratch = rest
    pick_weights(w_ref, w_gate_ref, tile_mask(chain_ref, block_mask_ref), turned, picked, picked_gate)
    rows = pair_ref[...].reshape(-1, pair_ref.shape[-1])
    project_all(rows, gain_ref[0:1], gate_ref, picked, picked_gate, scratch, outs, sizes, True)


def finish_rows(pair_ref, gate_ref, product_refs, w_out_ref, gain_ref, scratch, twice, out_ref):
    width = w_out_ref.shape[1]
    half = width // 2
    cols = pair_ref.shape[1]
    x = lax.axis_index("col") // 2
    mine, others = pl.multiple_of(x * half, half), pl.multiple_of((1 - x) * half, half)

    @pl.when(pl.program_id(0) == 0)
    def _():
        w_out = jnp.concatenate([w_out_ref[0, pl.ds(mine, half)], w_out_ref[0, pl.ds(others, half)]], 0)
        none = jnp.zeros_like(w_out)
        twice[...] = jnp.concatenate(
            [jnp.concatenate([w_out, none], 1), jnp.concatenate([none, w_out], 1)], 0
        )

    gain = jnp.concatenate([gain_ref[pl.ds(mine, half)], gain_ref[pl.ds(others, half)]], 0)
    product = jnp.concatenate([ref[...] for ref in product_refs], 0).astype(jnp.float32)
    mean = jnp.sum(product, 0, keepdims=True) * (1.0 / width)
    centred = product - mean
    spread = jnp.sum(centred * centred, 0, keepdims=True) * (1.0 / width)
    update = centred * lax.rsqrt(spread + EPS) * gain
    scratch[...] = update.reshape(width * STEP, cols)
    for row in range(0, STEP, 2):
        two = jnp.concatenate(
            [scratch[pl.ds(row, width, stride=STEP), :], scratch[pl.ds(row + 1, width, stride=STEP), :]], 0
        )
        changes = dot(two.astype(jnp.bfloat16), twice[...], TN)
        for k in range(2):
            change = changes[:, k * pair_ref.shape[2] : (k + 1) * pair_ref.shape[2]]
            gate = gate_ref[row + k].astype(jnp.float32)
            old = pair_ref[row + k].astype(jnp.float32)
            out_ref[row + k] = (old + gate * change).astype(jnp.bfloat16)


def finish_kernel(pair_ref, gate_ref, w_out_ref, gain_ref, *rest):
    *product_refs, out_ref, scratch, twice = rest
    finish_rows(pair_ref, gate_ref, product_refs, w_out_ref, gain_ref, scratch, twice, out_ref)


def middle_kernel(
    sizes,
    count,
    chain_ref,
    block_mask_ref,
    pair_ref,
    gate_ref,
    w_out_ref,
    gain_out_ref,
    w_ref,
    w_gate_ref,
    gain_in_ref,
    *rest,
):
    product_refs, (out_ref, next_ref, *outs) = rest[:count], rest[count:]
    *outs, update, twice, turned, picked, picked_gate, scratch = outs
    pick_weights(w_ref, w_gate_ref, tile_mask(chain_ref, block_mask_ref), turned, picked, picked_gate)
    finish_rows(pair_ref, gate_ref, product_refs, w_out_ref, gain_out_ref, update, twice, out_ref)
    rows = out_ref[...].reshape(-1, out_ref.shape[-1])
    project_all(rows, gain_in_ref[1:2], next_ref, picked, picked_gate, scratch, outs, sizes, False)


def outgoing_kernel(left, left_pair, right, right_pair, right_far, right_near, outs, rights):
    *kept, pair, sent = outs
    for k, blocks in enumerate((right, right_pair, right_far, right_near)):
        rights[k] = jnp.concatenate(blocks, 1)
    lefts = jnp.concatenate([jnp.concatenate(left, 1), jnp.concatenate(left_pair, 1)], 0)
    size = lefts.shape[0] // 2
    here = lax.axis_index("row") ^ lax.axis_index("col")
    for place in range(4):
        terms = dot(lefts, rights[here ^ place], NT).astype(jnp.bfloat16)
        if place % 2:
            sent[0, place // 2, 0] = terms[:size]
            sent[1, place // 2, 0] = terms[size:]
        else:
            kept[place // 2][0] = terms[:size]
            pair[place // 2, 0] = terms[size:]


def incoming_kernel(left, left_core, left_pair, left_pair_core, right, right_pair, outs, lefts):
    *kept, pair, cross = outs
    for k in range(2):
        lefts[2 * k] = jnp.concatenate([left[k], left_pair[k]], 0)
        lefts[2 * k + 1] = jnp.concatenate([left_core[k], left_pair_core[k]], 0)
    rights = jnp.concatenate([jnp.concatenate(right, 1), jnp.concatenate(right_pair, 1)], 0)
    size = rights.shape[1] // 2
    here = lax.axis_index("row") ^ lax.axis_index("col")
    for place in range(4):
        terms = dot(lefts[here ^ place], rights, TN).astype(jnp.bfloat16)
        for k in range(2):
            block = terms[:, k * size : (k + 1) * size]
            if place == 0:
                kept[k][0] = block
            else:
                (pair, cross.at[0], cross.at[1])[place - 1][k, 0] = block


def pieces_kernel(kernel, count, *refs):
    blocks = [ref[(0,) * (len(ref.shape) - 2)] for ref in refs[:count]]
    kernel(*[blocks[k : k + 2] for k in range(0, count, 2)], refs[count:-1], refs[-1])


def params(limit=VMEM):
    return pltpu.CompilerParams(
        vmem_limit_bytes=limit, dimension_semantics=("arbitrary",), fuse_transposed_lhs_in_matmul=True
    )


def part(array, index):
    return pl.BlockSpec((1,) + array.shape[1:], lambda *_: (index,) + (0,) * (array.ndim - 1))


def whole(array):
    return pl.BlockSpec(array.shape, lambda *_: (0,) * array.ndim)


def tile_spec(tile):
    return pl.BlockSpec((STEP,) + tile.shape[1:], lambda r: (r, 0, 0))


def chunk_spec(shape):
    lead = shape[:-2]
    return pl.BlockSpec(lead + (STEP, shape[-1]), lambda r: (0,) * len(lead) + (r, 0))


def cost(flops, nbytes, special=0):
    return pl.CostEstimate(
        flops=int(flops * TOLD), bytes_accessed=int(nbytes * TOLD), transcendentals=int(special * TOLD)
    )


def part_outs(pair, sizes, apart):
    tile = pair.shape[:2]
    own = [(size,) + tile for size in sizes]
    both_sides = [(2,) + shape for shape in own]
    shapes = ([shape for shape in own for _ in range(2)] if apart else both_sides) + both_sides
    return [jax.ShapeDtypeStruct(shape, jnp.bfloat16) for shape in shapes], [chunk_spec(shape) for shape in shapes]


def part_scratch(pair, w_in, sizes):
    width = 2 * sum(sizes)
    return [
        pltpu.VMEM((w_in.shape[2], w_in.shape[1]), jnp.float32),
        pltpu.VMEM((4 * width, w_in.shape[1]), jnp.bfloat16),
        pltpu.VMEM((w_in.shape[1], w_in.shape[1]), jnp.bfloat16),
        pltpu.VMEM((2, width * STEP, pair.shape[1]), jnp.float32),
    ]


def finish_scratch(pair, w_out):
    return [
        pltpu.VMEM((w_out.shape[1] * STEP, pair.shape[1]), jnp.float32),
        pltpu.VMEM((2 * w_out.shape[1], 2 * w_out.shape[2]), jnp.bfloat16),
    ]


def first_call(chain, block_mask, pair, w_in, w_gate, gain_in):
    outs, specs = part_outs(pair, OUT_SIZES, True)
    gate, *result = pl.pallas_call(
        functools.partial(first_kernel, OUT_SIZES),
        grid=(pair.shape[0] // STEP,),
        in_specs=[SMEM_SPEC, SMEM_SPEC, tile_spec(pair), part(w_in, 0), part(w_gate, 0), whole(gain_in)],
        out_specs=[tile_spec(pair)] + specs,
        out_shape=[jax.ShapeDtypeStruct(pair.shape, pair.dtype)] + outs,
        scratch_shapes=part_scratch(pair, w_in, OUT_SIZES),
        compiler_params=params(),
        cost_estimate=cost(2e9, 8 << 20, 4 << 20),
        name="project",
    )(chain, block_mask, pair, w_in, w_gate, gain_in)
    return gate, result


def finish_call(pair, gate, products, w_out, gain_wide):
    return pl.pallas_call(
        finish_kernel,
        grid=(pair.shape[0] // STEP,),
        in_specs=[tile_spec(pair), tile_spec(gate), part(w_out, 1), whole(gain_wide)]
        + [chunk_spec(p.shape) for p in products],
        out_specs=tile_spec(pair),
        out_shape=jax.ShapeDtypeStruct(pair.shape, pair.dtype),
        scratch_shapes=finish_scratch(pair, w_out),
        compiler_params=params(),
        cost_estimate=cost(1e9, 14 << 20, 4 << 20),
        name="finish",
    )(pair, gate, w_out, gain_wide, *products)


def middle_call(chain, block_mask, pair, gate, products, w_out, gain_wide, w_in, w_gate, gain_in):
    outs, specs = part_outs(pair, IN_SIZES, False)
    middle, gate, *result = pl.pallas_call(
        functools.partial(middle_kernel, IN_SIZES, len(products)),
        grid=(pair.shape[0] // STEP,),
        in_specs=[SMEM_SPEC, SMEM_SPEC, tile_spec(pair), tile_spec(gate), part(w_out, 0)]
        + [whole(gain_wide), part(w_in, 1), part(w_gate, 1), whole(gain_in)]
        + [chunk_spec(p.shape) for p in products],
        out_specs=[tile_spec(pair)] * 2 + specs,
        out_shape=[jax.ShapeDtypeStruct(pair.shape, pair.dtype)] * 2 + outs,
        scratch_shapes=finish_scratch(pair, w_out) + part_scratch(pair, w_in, IN_SIZES),
        compiler_params=params(),
        cost_estimate=cost(3e9, 18 << 20, 8 << 20),
        name="middle",
    )(chain, block_mask, pair, gate, w_out, gain_wide, w_in, w_gate, gain_in, *products)
    return middle, gate, result


def product_call(kernel, operands, channels, leads, scratch, name):
    pieces = [piece for operand in operands for piece in operand]
    size = pieces[0][0].shape[-1]

    def piece_spec(array, lead, first):
        return pl.BlockSpec((1,) * (len(lead) + 1) + (size, size), lambda c: lead + (first + c, 0, 0))

    def out_spec(lead):
        return pl.BlockSpec(lead + (1, size, size), lambda c: (0,) * len(lead) + (c, 0, 0))

    return pl.pallas_call(
        functools.partial(pieces_kernel, kernel, len(pieces)),
        grid=(channels,),
        in_specs=[piece_spec(*piece) for piece in pieces],
        out_specs=[out_spec(lead) for lead in leads],
        out_shape=[jax.ShapeDtypeStruct(lead + (channels, size, size), jnp.bfloat16) for lead in leads],
        scratch_shapes=[pltpu.VMEM(scratch, jnp.bfloat16)],
        compiler_params=params(PRODUCT_VMEM),
        cost_estimate=cost(channels * 2 * (4 * size) ** 2 * size, channels * size * size * 2 * 20),
        name=name,
    )(*[piece[0] for piece in pieces])


WAYS = {
    "in": ("row", [(0, 1), (3, 2)]),
    "across": ("row", [(1, 2), (2, 1)]),
    "out": ("row", [(1, 0), (2, 3)]),
    "x": ("col", [(c, c ^ 2) for c in range(4)]),
    "core": ("col", [(c, c ^ 1) for c in range(4)]),
}


class Graph:
    def __init__(self, order):
        self.order, self.steps, self.made = order, {}, {}

    def add(self, name, operand, step):
        self.steps[name] = (operand, step)

    def send(self, name, way, operand):
        axis, pairs = WAYS[way]
        self.add(name, operand, lambda array: lax.ppermute(array, axis, pairs))

    def get(self, name):
        if name not in self.made:
            operand, step = self.steps[name]
            waits = [self.get(other) for other in self.order.get(name, ())]
            array = operand()
            if waits:
                array = lax.optimization_barrier((array, *waits))[0]
            self.made[name] = step(array)
        return self.made[name]


def pack(*columns):
    return jnp.stack([jnp.concatenate([column[k] for column in columns]) for k in range(2)])


def both(array, first=0, lead=()):
    return [(array, (k,) + lead, first) for k in range(2)]


def is_inner():
    row = lax.axis_index("row")
    return (row == 1) | (row == 2)


def shared_steps(graph, groups, mine, other):
    inner = is_inner()
    get = graph.get
    first, names = 0, []

    def joined(arrays, axis):
        return arrays[0] if len(arrays) == 1 else jnp.concatenate(arrays, axis)

    for g, size in enumerate(groups):
        chunks = range(first, first + size)
        first += size

        def ready(k, g=g, chunks=chunks):
            return jnp.where(inner, joined([mine(n, k) for n in chunks], 0), get(f"o{g}")[k])

        graph.send(f"o{g}", "out", lambda chunks=chunks: joined([other(n) for n in chunks], 1))
        graph.send(f"b{g}", "x", lambda ready=ready: ready(1))
        graph.add(f"k{g}", lambda ready=ready: ready(0), lambda array: array)
    return [get(kind + str(g)) for kind in ("k", "b") for g in range(len(groups))]


def outgoing(parts):
    count = len(OUT_SIZES)
    graph = Graph(OUT_ORDER)
    get, send = graph.get, graph.send
    for n in range(count):
        send(f"x{n}", "x", lambda n=n: parts[2 * count + n])
    later = lambda n, side: parts[2 * n + side]
    right_of = lambda n: (later(n, 0), get(f"x{n}")[0])
    left_of = lambda n: (later(n, 1), get(f"x{n}")[1])
    first = parts
    zero = OUT_SIZES[0]
    send("i0", "in", lambda: first[0])
    send("a0", "across", lambda: first[0])
    send("i1", "in", lambda: jnp.concatenate([get("x0")[0], first[1]]))
    send("a1", "across", lambda: jnp.concatenate([get("x0")[0], get("i0")]))

    def come(n):
        array, skip = get(f"i{n + 1}"), zero // 2 if n == 1 else OUT_SIZES[n - 1]
        return (array[0, skip:], array[1, skip:])

    def halves(array):
        return (array[: zero // 2], array[zero // 2 :])

    def inward(n):
        before = halves(get("x0")[1]) if n == 1 else left_of(n - 1)
        return pack(before, right_of(n)) if n < count else pack(before)

    def across(n):
        before = halves(get("i1")[:zero]) if n == 1 else come(n - 1)
        return pack(before, right_of(n)) if n < count else pack(before)

    for n in range(1, count + 1):
        send(f"i{n + 1}", "in", lambda n=n: inward(n))
        send(f"a{n + 1}", "across", lambda n=n: across(n))

    def product(n, left):
        size = left.shape[-1]
        if n == 0:
            x_left = lambda array: array[:, : zero // 2].reshape((zero,) + array.shape[2:])
            operands = [
                [(left, (), 0), (get("x0"), (1,), 0)],
                [(get("i1"), (), zero), (x_left(get("i2")), (), 0)],
                [(first[0], (), 0), (get("x0"), (0,), 0)],
                [(get("i0"), (), 0), (get("i1"), (), 0)],
                [(get("a1"), (), zero), (x_left(get("a2")), (), 0)],
                [(get("a0"), (), 0), (get("a1"), (), 0)],
            ]
        else:
            skip = zero // 2 if n == 1 else OUT_SIZES[n - 1]
            operands = [
                [(left, (), 0), (get(f"x{n}"), (1,), 0)],
                both(get(f"i{n + 2}")),
                [(later(n, 0), (), 0), (get(f"x{n}"), (0,), 0)],
                both(get(f"i{n + 1}"), skip),
                both(get(f"a{n + 2}")),
                both(get(f"a{n + 1}"), skip),
            ]
        leads = ((), (), (2,), (2, 2))
        return product_call(outgoing_kernel, operands, left.shape[0], leads, (4, size, 2 * size), "outgoing")

    for n in range(count):
        graph.add(f"p{n}", lambda n=n: later(n, 1), functools.partial(product, n))
        send(f"c{n}", "core", lambda n=n: get(f"p{n}")[3])
    return shared_steps(
        graph,
        OUT_GROUPS,
        lambda n, k: get(f"p{n}")[k] + get(f"c{n}")[0, k],
        lambda n: get(f"p{n}")[2] + get(f"c{n}")[1],
    )


def incoming(parts):
    count = len(IN_SIZES)
    graph = Graph(IN_ORDER)
    get, send = graph.get, graph.send
    for n in range(count):
        send(f"x{n}", "x", lambda n=n: parts[count + n])
    send("i0", "in", lambda: parts[0])
    send("i0x", "in", lambda: get("x0"))
    send("cl0", "core", lambda: parts[0])
    send("clx", "core", lambda: get("x0"))
    send("cp0", "core", lambda: get("i0"))
    send("cpx", "core", lambda: get("i0x"))
    for n in range(1, count):
        graph.add(f"j{n}", lambda n=n: parts[n], lambda own, n=n: jnp.stack([own, get(f"x{n}")], 1))
        send(f"i{n}", "in", lambda n=n: get(f"j{n}"))
        send(f"cl{n}", "core", lambda n=n: get(f"j{n}")[0])
        send(f"cp{n}", "core", lambda n=n: get(f"i{n}")[0])

    def product(n, own):
        size = own.shape[-1]
        if n == 0:
            side = lambda name, name_x, slot: [
                (own if name is None else get(name), (slot,), 0),
                (get(name_x), (slot,), 0),
            ]
            operands = [side(None, "x0", 0), side("cl0", "clx", 0), side("i0", "i0x", 0), side("cp0", "cpx", 0)]
            operands += [side(None, "x0", 1), side("i0", "i0x", 1)]
        else:
            side = lambda array, slot: [(array, (slot, k), 0) for k in range(2)]
            operands = [side(own, 0), both(get(f"cl{n}")), side(get(f"i{n}"), 0), both(get(f"cp{n}"))]
            operands += [side(own, 1), side(get(f"i{n}"), 1)]
        leads = ((), (), (2,), (2, 2))
        return product_call(incoming_kernel, operands, IN_SIZES[n], leads, (4, 2 * size, size), "incoming")

    for n in range(count):
        graph.add(f"p{n}", lambda n=n: get(f"j{n}") if n else parts[0], functools.partial(product, n))
        send(f"a{n}", "across", lambda n=n: get(f"p{n}")[3])
    return shared_steps(
        graph,
        IN_GROUPS,
        lambda n, k: get(f"p{n}")[k] + get(f"a{n}")[1, k],
        lambda n: get(f"p{n}")[2] + get(f"a{n}")[0],
    )


def four_by_four(pair, chain, block_mask, w_in, w_gate, w_out, gain_in, gain_out):
    gain_wide = jnp.broadcast_to(gain_out[:, :, None, None], gain_out.shape + (1, pair.shape[1]))
    gate, parts = first_call(chain, block_mask, pair, w_in, w_gate, gain_in)
    products = outgoing(parts)
    middle, gate, parts = middle_call(
        chain, block_mask, pair, gate, products, w_out, gain_wide[0], w_in, w_gate, gain_in
    )
    products = incoming(parts)
    return finish_call(middle, gate, products, w_out, gain_wide[1])


def solution(mesh):
    four = mesh.shape["row"] == 4 and mesh.shape["col"] == 4
    return jax.shard_map(
        four_by_four if four else any_mesh,
        mesh=mesh,
        in_specs=(
            P(("group", "row"), "col", None),
            P("group"),
            P("group", None),
            P(),
            P(),
            P(),
            P(),
            P(),
        ),
        out_specs=P(("group", "row"), "col", None),
        check_vma=False,
    )
```

```python
import functools

import jax
import jax.numpy as jnp
from jax import lax
from jax.experimental import pallas as pl
from jax.experimental.pallas import tpu as pltpu
from jax.sharding import PartitionSpec as P

BLOCK = 128
EPS = 1e-05
OUT_SIZES = (10, 8, 8, 4, 2)
IN_SIZES = (8, 8, 8, 4, 4)
OUT_GROUPS = (1, 1, 1, 1, 1)
IN_GROUPS = (1, 1, 1, 1, 1)
OUT_ORDER = {'i1': ('i0',), 'i2': ('i1',), 'i3': ('i2',), 'i4': ('i3',), 'i5': ('i4',), 'i6': ('i5',), 'a1': ('a0',), 'a2': ('a1',), 'a3': ('a2',), 'a4': ('a3',), 'a5': ('a4',), 'a6': ('a5', 'b0', 'i6'), 'x3': ('x2',), 'x5': ('x4',), 'x1': ('a0',), 'x2': ('a1',), 'p3': ('o1',), 'p4': ('o2',)}
IN_ORDER = {'i0x': ('i0',), 'i3': ('i2',), 'i4': ('i3',), 'a1': ('a0', 'i1'), 'a3': ('a2',), 'o2': ('o1',), 'o3': ('o2',), 'o4': ('o3',), 'x1': ('i0',), 'x2': ('i0x',), 'c4': ('c3',)}
STEP = 16
TOLD = 0.05
FIRST_VMEM = 48 * 1024 * 1024
VMEM = 28 * 1024 * 1024
PRODUCT_VMEM = 10 * 1024 * 1024


def broadcast(block, axis, owner):
    block = jnp.where(lax.axis_index(axis) == owner, block, jnp.zeros_like(block))
    return lax.psum(block, axis)


def layer_norm(values, gain):
    mean = jnp.mean(values, -1, keepdims=True)
    centred = values - mean
    spread = jnp.mean(centred * centred, -1, keepdims=True)
    return centred * lax.rsqrt(spread + EPS) * gain


def project(pair, tile_mask, w_in, w_gate, gain_in):
    normed = layer_norm(pair.astype(jnp.float32), gain_in).astype(jnp.bfloat16)
    hidden = jnp.dot(normed, w_in, preferred_element_type=jnp.float32)
    width = w_in.shape[1] // 4
    masked = tile_mask[..., None]
    left = (masked * jax.nn.sigmoid(hidden[..., width : 2 * width]) * hidden[..., :width]).astype(
        jnp.bfloat16
    )
    right = (
        masked * jax.nn.sigmoid(hidden[..., 3 * width :]) * hidden[..., 2 * width : 3 * width]
    ).astype(jnp.bfloat16)
    gate = jax.nn.sigmoid(jnp.dot(normed, w_gate, preferred_element_type=jnp.float32))
    return (left, right, gate)


def finish(pair, product, gate, w_out, gain_out):
    update = layer_norm(product, gain_out).astype(jnp.bfloat16)
    return (
        pair.astype(jnp.float32) + gate * jnp.dot(update, w_out, preferred_element_type=jnp.float32)
    ).astype(jnp.bfloat16)


def any_mesh(pair, chain, block_mask, w_in, w_gate, w_out, gain_in, gain_out):
    tile_rows = pair.shape[0]
    tile_cols = pair.shape[1]
    block_count = chain.shape[0]
    ratio = lax.axis_size("row") // lax.axis_size("col")
    row_index = lax.axis_index("row")
    col_index = lax.axis_index("col")
    same = chain[:, None] == chain[None, :]
    blocks = jnp.where(same | (block_mask == 1), 1.0, 0.0).astype(jnp.float32)
    labels = jnp.arange(block_count, dtype=jnp.int32)
    row_blocks = (row_index * tile_rows + jnp.arange(tile_rows, dtype=jnp.int32)) // BLOCK
    col_blocks = (col_index * tile_cols + jnp.arange(tile_cols, dtype=jnp.int32)) // BLOCK
    row_onehot = jnp.where(row_blocks[:, None] == labels[None, :], 1.0, 0.0).astype(jnp.float32)
    col_onehot = jnp.where(col_blocks[:, None] == labels[None, :], 1.0, 0.0).astype(jnp.float32)
    tile_mask = jnp.dot(jnp.dot(row_onehot, blocks), col_onehot.T)
    left, right, gate = project(pair, tile_mask, w_in[0], w_gate[0], gain_in[0])
    partial_terms = jnp.einsum(
        "ikc,jkc->ijc",
        left,
        lax.all_gather(right, "row", axis=0, tiled=True),
        preferred_element_type=jnp.float32,
    )
    product = lax.psum_scatter(
        partial_terms.astype(jnp.bfloat16), "col", scatter_dimension=1, tiled=True
    ).astype(jnp.float32)
    middle = finish(pair, product, gate, w_out[0], gain_out[0])
    left, right, gate = project(middle, tile_mask, w_in[1], w_gate[1], gain_in[1])
    left_cols = lax.all_gather(left, "row", axis=0, tiled=True)
    start_col = row_index % ratio * tile_rows
    left_slice = lax.dynamic_slice_in_dim(left_cols, start_col, tile_rows, 1)
    left_mine = broadcast(left_slice, "col", row_index // ratio)
    product = jnp.einsum(
        "kic,kjc->ijc",
        left_mine,
        lax.all_gather(right, "row", axis=0, tiled=True),
        preferred_element_type=jnp.float32,
    )
    return finish(middle, product, gate, w_out[1], gain_out[1])


NN = (((1,), (0,)), ((), ()))
NT = (((1,), (1,)), ((), ()))
TN = (((0,), (0,)), ((), ()))
SMEM_SPEC = pl.BlockSpec(memory_space=pltpu.SMEM)


def dot(a, b, dims=NN):
    return lax.dot_general(a, b, dims, preferred_element_type=jnp.float32)


def norm_rows(rows, gain):
    channels = rows.shape[-1]
    place = lax.broadcasted_iota(jnp.int32, (channels, channels), 0)
    same = place == lax.broadcasted_iota(jnp.int32, (channels, channels), 1)
    centre = jnp.where(same, 1.0 - 1.0 / channels, -1.0 / channels).astype(jnp.bfloat16)
    mean_of = jnp.full((2 * channels, channels), 1.0 / channels, jnp.bfloat16)
    centred = dot(rows, centre)
    square = centred * centred
    high = square.astype(jnp.bfloat16)
    low = (square - high.astype(jnp.float32)).astype(jnp.bfloat16)
    spread = dot(jnp.concatenate([high, low], 1), mean_of)
    return (centred * lax.rsqrt(spread + EPS) * gain).astype(jnp.bfloat16)


def tile_mask(chain_ref, block_mask_ref):
    row, col = lax.axis_index("row"), lax.axis_index("col")
    seen = (chain_ref[row] == chain_ref[col]) | (block_mask_ref[row, col] == 1)
    return jnp.where(seen, 1.0, 0.0).astype(jnp.float32)


def pick_weights(w_ref, w_gate_ref, mask, turned, picked, picked_gate):
    @pl.when(pl.program_id(0) == 0)
    def _():
        turned[...] = w_ref[0].astype(jnp.float32).T
        half = turned.shape[0] // 8
        x = lax.axis_index("col") // 2
        rows = []
        for kind in range(4):
            for other in (x, 1 - x):
                some = turned[pl.ds(pl.multiple_of((2 * kind + other) * half, 8), half), :]
                rows.append(some * (0.5 if kind % 2 else 0.5 * mask))
        picked[...] = jnp.concatenate(rows, 0).astype(jnp.bfloat16)
        picked_gate[...] = (w_gate_ref[0].astype(jnp.float32) * 0.5).astype(jnp.bfloat16)


def project_part(normed, picked, scratch, sides, sizes):
    hidden = dot(picked[...], normed, NT)
    width = picked.shape[0] // 4
    cols = normed.shape[0] // STEP
    for side, refs in enumerate(sides):
        values = hidden[2 * side * width : (2 * side + 1) * width]
        gates = hidden[(2 * side + 1) * width : (2 * side + 2) * width]
        kept = (jnp.tanh(gates) + 1.0) * values
        for row in range(STEP):
            scratch[side, pl.ds(row, width, stride=STEP), :] = kept[:, row * cols : (row + 1) * cols]
        done = 0
        for ref, size in zip(refs, sizes * 2):
            rows = scratch[side, done * STEP : (done + size) * STEP, :]
            ref[...] = rows.astype(jnp.bfloat16).reshape(ref.shape)
            done += size


def split_sides(outs, sizes, apart):
    count = len(sizes)
    if not apart:
        return [ref.at[0] for ref in outs], [ref.at[1] for ref in outs]
    rights, lefts, sent = list(outs[: 2 * count : 2]), list(outs[1 : 2 * count : 2]), outs[2 * count :]
    for n, size in enumerate(sizes):
        skip = sizes[n - 1] if n else 0
        rights.append(sent[n].at[skip : skip + size])
        lefts.append(sent[n + 1].at[0:size])
    return lefts, rights


def project_all(rows, gain, gate_ref, picked, picked_gate, scratch, outs, sizes, apart):
    normed = norm_rows(rows, gain)
    project_part(normed, picked, scratch, split_sides(outs, sizes, apart), sizes)
    gate = 0.5 * jnp.tanh(dot(normed, picked_gate[...])) + 0.5
    gate_ref[...] = gate.astype(gate_ref.dtype).reshape(gate_ref.shape)


def first_kernel(sizes, chain_ref, block_mask_ref, pair_ref, w_ref, w_gate_ref, gain_ref, gate_ref, *rest):
    *outs, turned, picked, picked_gate, scratch = rest
    pick_weights(w_ref, w_gate_ref, tile_mask(chain_ref, block_mask_ref), turned, picked, picked_gate)
    rows = pair_ref[...].reshape(-1, pair_ref.shape[-1])
    project_all(rows, gain_ref[0:1], gate_ref, picked, picked_gate, scratch, outs, sizes, True)


def finish_rows(pair_ref, gate_ref, product_refs, w_out_ref, gain_ref, scratch, twice, out_ref):
    width = w_out_ref.shape[1]
    half = width // 2
    cols = pair_ref.shape[1]
    x = lax.axis_index("col") // 2
    mine, others = pl.multiple_of(x * half, half), pl.multiple_of((1 - x) * half, half)

    @pl.when(pl.program_id(0) == 0)
    def _():
        w_out = jnp.concatenate([w_out_ref[0, pl.ds(mine, half)], w_out_ref[0, pl.ds(others, half)]], 0)
        none = jnp.zeros_like(w_out)
        twice[...] = jnp.concatenate(
            [jnp.concatenate([w_out, none], 1), jnp.concatenate([none, w_out], 1)], 0
        )

    gain = jnp.concatenate([gain_ref[pl.ds(mine, half)], gain_ref[pl.ds(others, half)]], 0)
    product = jnp.concatenate([ref[...] for ref in product_refs], 0).astype(jnp.float32)
    mean = jnp.sum(product, 0, keepdims=True) * (1.0 / width)
    centred = product - mean
    spread = jnp.sum(centred * centred, 0, keepdims=True) * (1.0 / width)
    update = centred * lax.rsqrt(spread + EPS) * gain
    scratch[...] = update.reshape(width * STEP, cols)
    for row in range(0, STEP, 2):
        two = jnp.concatenate(
            [scratch[pl.ds(row, width, stride=STEP), :], scratch[pl.ds(row + 1, width, stride=STEP), :]], 0
        )
        changes = dot(two.astype(jnp.bfloat16), twice[...], TN)
        for k in range(2):
            change = changes[:, k * pair_ref.shape[2] : (k + 1) * pair_ref.shape[2]]
            gate = gate_ref[row + k].astype(jnp.float32)
            old = pair_ref[row + k].astype(jnp.float32)
            out_ref[row + k] = (old + gate * change).astype(jnp.bfloat16)


def finish_kernel(pair_ref, gate_ref, w_out_ref, gain_ref, *rest):
    *product_refs, out_ref, scratch, twice = rest
    finish_rows(pair_ref, gate_ref, product_refs, w_out_ref, gain_ref, scratch, twice, out_ref)


def middle_kernel(
    sizes,
    count,
    chain_ref,
    block_mask_ref,
    pair_ref,
    gate_ref,
    w_out_ref,
    gain_out_ref,
    w_ref,
    w_gate_ref,
    gain_in_ref,
    *rest,
):
    product_refs, (out_ref, next_ref, *outs) = rest[:count], rest[count:]
    *outs, update, twice, turned, picked, picked_gate, scratch = outs
    pick_weights(w_ref, w_gate_ref, tile_mask(chain_ref, block_mask_ref), turned, picked, picked_gate)
    finish_rows(pair_ref, gate_ref, product_refs, w_out_ref, gain_out_ref, update, twice, out_ref)
    rows = out_ref[...].reshape(-1, out_ref.shape[-1])
    project_all(rows, gain_in_ref[1:2], next_ref, picked, picked_gate, scratch, outs, sizes, False)


def outgoing_kernel(left, left_pair, right, right_pair, right_far, right_near, outs, rights):
    *kept, pair, sent = outs
    for k, blocks in enumerate((right, right_pair, right_far, right_near)):
        rights[k] = jnp.concatenate(blocks, 1)
    lefts = jnp.concatenate([jnp.concatenate(left, 1), jnp.concatenate(left_pair, 1)], 0)
    size = lefts.shape[0] // 2
    here = lax.axis_index("row") ^ lax.axis_index("col")
    for place in range(4):
        terms = dot(lefts, rights[here ^ place], NT).astype(jnp.bfloat16)
        if place % 2:
            sent[0, place // 2, 0] = terms[:size]
            sent[1, place // 2, 0] = terms[size:]
        else:
            kept[place // 2][0] = terms[:size]
            pair[place // 2, 0] = terms[size:]


def incoming_kernel(left, left_core, left_pair, left_pair_core, right, right_pair, outs, lefts):
    *kept, pair, cross = outs
    for k in range(2):
        lefts[2 * k] = jnp.concatenate([left[k], left_pair[k]], 0)
        lefts[2 * k + 1] = jnp.concatenate([left_core[k], left_pair_core[k]], 0)
    rights = jnp.concatenate([jnp.concatenate(right, 1), jnp.concatenate(right_pair, 1)], 0)
    size = rights.shape[1] // 2
    here = lax.axis_index("row") ^ lax.axis_index("col")
    for place in range(4):
        terms = dot(lefts[here ^ place], rights, TN).astype(jnp.bfloat16)
        for k in range(2):
            block = terms[:, k * size : (k + 1) * size]
            if place == 0:
                kept[k][0] = block
            else:
                (pair, cross.at[0], cross.at[1])[place - 1][k, 0] = block


def pieces_kernel(kernel, count, *refs):
    blocks = [ref[(0,) * (len(ref.shape) - 2)] for ref in refs[:count]]
    kernel(*[blocks[k : k + 2] for k in range(0, count, 2)], refs[count:-1], refs[-1])


def params(limit=VMEM):
    return pltpu.CompilerParams(
        vmem_limit_bytes=limit, dimension_semantics=("arbitrary",), fuse_transposed_lhs_in_matmul=True
    )


def part(array, index):
    return pl.BlockSpec((1,) + array.shape[1:], lambda *_: (index,) + (0,) * (array.ndim - 1))


def whole(array):
    return pl.BlockSpec(array.shape, lambda *_: (0,) * array.ndim)


def tile_spec(tile):
    return pl.BlockSpec((STEP,) + tile.shape[1:], lambda r: (r, 0, 0))


def chunk_spec(shape):
    lead = shape[:-2]
    return pl.BlockSpec(lead + (STEP, shape[-1]), lambda r: (0,) * len(lead) + (r, 0))


def cost(flops, nbytes, special=0):
    return pl.CostEstimate(
        flops=int(flops * TOLD), bytes_accessed=int(nbytes * TOLD), transcendentals=int(special * TOLD)
    )


def part_outs(pair, sizes, apart):
    tile = pair.shape[:2]
    if apart:
        staged = zip((0,) + sizes, sizes + (0,))
        shapes = [(size,) + tile for size in sizes for _ in range(2)] + [(a + b,) + tile for a, b in staged]
    else:
        shapes = [(2, size) + tile for size in sizes] * 2
    return [jax.ShapeDtypeStruct(shape, jnp.bfloat16) for shape in shapes], [chunk_spec(shape) for shape in shapes]


def part_scratch(pair, w_in, sizes):
    width = 2 * sum(sizes)
    return [
        pltpu.VMEM((w_in.shape[2], w_in.shape[1]), jnp.float32),
        pltpu.VMEM((4 * width, w_in.shape[1]), jnp.bfloat16),
        pltpu.VMEM((w_in.shape[1], w_in.shape[1]), jnp.bfloat16),
        pltpu.VMEM((2, width * STEP, pair.shape[1]), jnp.float32),
    ]


def finish_scratch(pair, w_out):
    return [
        pltpu.VMEM((w_out.shape[1] * STEP, pair.shape[1]), jnp.float32),
        pltpu.VMEM((2 * w_out.shape[1], 2 * w_out.shape[2]), jnp.bfloat16),
    ]


def first_call(chain, block_mask, pair, w_in, w_gate, gain_in):
    outs, specs = part_outs(pair, OUT_SIZES, True)
    gate, *result = pl.pallas_call(
        functools.partial(first_kernel, OUT_SIZES),
        grid=(pair.shape[0] // STEP,),
        in_specs=[SMEM_SPEC, SMEM_SPEC, tile_spec(pair), part(w_in, 0), part(w_gate, 0), whole(gain_in)],
        out_specs=[tile_spec(pair)] + specs,
        out_shape=[jax.ShapeDtypeStruct(pair.shape, pair.dtype)] + outs,
        scratch_shapes=part_scratch(pair, w_in, OUT_SIZES),
        compiler_params=params(FIRST_VMEM),
        cost_estimate=cost(2e9, 8 << 20, 4 << 20),
        name="project",
    )(chain, block_mask, pair, w_in, w_gate, gain_in)
    return gate, result


def finish_call(pair, gate, products, w_out, gain_wide):
    return pl.pallas_call(
        finish_kernel,
        grid=(pair.shape[0] // STEP,),
        in_specs=[tile_spec(pair), tile_spec(gate), part(w_out, 1), whole(gain_wide)]
        + [chunk_spec(p.shape) for p in products],
        out_specs=tile_spec(pair),
        out_shape=jax.ShapeDtypeStruct(pair.shape, pair.dtype),
        scratch_shapes=finish_scratch(pair, w_out),
        compiler_params=params(),
        cost_estimate=cost(1e9, 14 << 20, 4 << 20),
        name="finish",
    )(pair, gate, w_out, gain_wide, *products)


def middle_call(chain, block_mask, pair, gate, products, w_out, gain_wide, w_in, w_gate, gain_in):
    outs, specs = part_outs(pair, IN_SIZES, False)
    middle, gate, *result = pl.pallas_call(
        functools.partial(middle_kernel, IN_SIZES, len(products)),
        grid=(pair.shape[0] // STEP,),
        in_specs=[SMEM_SPEC, SMEM_SPEC, tile_spec(pair), tile_spec(gate), part(w_out, 0)]
        + [whole(gain_wide), part(w_in, 1), part(w_gate, 1), whole(gain_in)]
        + [chunk_spec(p.shape) for p in products],
        out_specs=[tile_spec(pair)] * 2 + specs,
        out_shape=[jax.ShapeDtypeStruct(pair.shape, pair.dtype)] * 2 + outs,
        scratch_shapes=finish_scratch(pair, w_out) + part_scratch(pair, w_in, IN_SIZES),
        compiler_params=params(),
        cost_estimate=cost(3e9, 18 << 20, 8 << 20),
        name="middle",
    )(chain, block_mask, pair, gate, w_out, gain_wide, w_in, w_gate, gain_in, *products)
    return middle, gate, result


def product_call(kernel, operands, channels, leads, scratch, name):
    pieces = [piece for operand in operands for piece in operand]
    size = pieces[0][0].shape[-1]

    def piece_spec(array, lead, first):
        return pl.BlockSpec((1,) * (len(lead) + 1) + (size, size), lambda c: lead + (first + c, 0, 0))

    def out_spec(lead):
        return pl.BlockSpec(lead + (1, size, size), lambda c: (0,) * len(lead) + (c, 0, 0))

    return pl.pallas_call(
        functools.partial(pieces_kernel, kernel, len(pieces)),
        grid=(channels,),
        in_specs=[piece_spec(*piece) for piece in pieces],
        out_specs=[out_spec(lead) for lead in leads],
        out_shape=[jax.ShapeDtypeStruct(lead + (channels, size, size), jnp.bfloat16) for lead in leads],
        scratch_shapes=[pltpu.VMEM(scratch, jnp.bfloat16)],
        compiler_params=params(PRODUCT_VMEM),
        cost_estimate=cost(channels * 2 * (4 * size) ** 2 * size, channels * size * size * 2 * 20),
        name=name,
    )(*[piece[0] for piece in pieces])


WAYS = {
    "in": ("row", [(0, 1), (3, 2)]),
    "across": ("row", [(1, 2), (2, 1)]),
    "out": ("row", [(1, 0), (2, 3)]),
    "x": ("col", [(c, c ^ 2) for c in range(4)]),
    "core": ("col", [(c, c ^ 1) for c in range(4)]),
}


class Graph:
    def __init__(self, order):
        self.order, self.steps, self.made = order, {}, {}

    def add(self, name, operand, step):
        self.steps[name] = (operand, step)

    def send(self, name, way, operand):
        axis, pairs = WAYS[way]
        self.add(name, operand, lambda array: lax.ppermute(array, axis, pairs))

    def get(self, name):
        if name not in self.made:
            operand, step = self.steps[name]
            waits = [self.get(other) for other in self.order.get(name, ())]
            array = operand()
            if waits:
                array = lax.optimization_barrier((array, *waits))[0]
            self.made[name] = step(array)
        return self.made[name]


def pack(*columns):
    return jnp.stack([jnp.concatenate([column[k] for column in columns]) for k in range(2)])


def both(array, first=0, lead=()):
    return [(array, (k,) + lead, first) for k in range(2)]


def is_inner():
    row = lax.axis_index("row")
    return (row == 1) | (row == 2)


def shared_steps(graph, groups, mine, other):
    inner = is_inner()
    get = graph.get
    first, names = 0, []

    def joined(arrays, axis):
        return arrays[0] if len(arrays) == 1 else jnp.concatenate(arrays, axis)

    for g, size in enumerate(groups):
        chunks = range(first, first + size)
        first += size

        def ready(k, g=g, chunks=chunks):
            return jnp.where(inner, joined([mine(n, k) for n in chunks], 0), get(f"o{g}")[k])

        graph.send(f"o{g}", "out", lambda chunks=chunks: joined([other(n) for n in chunks], 1))
        graph.send(f"b{g}", "x", lambda ready=ready: ready(1))
        graph.add(f"k{g}", lambda ready=ready: ready(0), lambda array: array)
    return [get(kind + str(g)) for kind in ("k", "b") for g in range(len(groups))]


def outgoing(parts):
    count = len(OUT_SIZES)
    graph = Graph(OUT_ORDER)
    get, send = graph.get, graph.send
    for n in range(count + 1):
        send(f"x{n}", "x", lambda n=n: parts[2 * count + n])
    before = lambda n: OUT_SIZES[n - 1] if n else 0
    right_x = lambda n: (get(f"x{n}"), (), before(n))
    left_x = lambda n: (get(f"x{n + 1}"), (), 0)
    later = lambda n, side: parts[2 * n + side]
    right_of = lambda n: (later(n, 0), get(f"x{n}")[before(n) :])
    left_of = lambda n: (later(n, 1), get(f"x{n + 1}")[: OUT_SIZES[n]])
    first = parts
    zero = OUT_SIZES[0]
    send("i0", "in", lambda: first[0])
    send("a0", "across", lambda: first[0])
    send("i1", "in", lambda: jnp.concatenate([get("x0"), first[1]]))
    send("a1", "across", lambda: jnp.concatenate([get("x0"), get("i0")]))

    def come(n):
        array, skip = get(f"i{n + 1}"), zero // 2 if n == 1 else OUT_SIZES[n - 1]
        return (array[0, skip:], array[1, skip:])

    def halves(array):
        return (array[: zero // 2], array[zero // 2 :])

    def inward(n):
        behind = halves(get("x1")[:zero]) if n == 1 else left_of(n - 1)
        return pack(behind, right_of(n)) if n < count else pack(behind)

    def across(n):
        behind = halves(get("i1")[:zero]) if n == 1 else come(n - 1)
        return pack(behind, right_of(n)) if n < count else pack(behind)

    for n in range(1, count + 1):
        send(f"i{n + 1}", "in", lambda n=n: inward(n))
        send(f"a{n + 1}", "across", lambda n=n: across(n))

    def product(n, left):
        size = left.shape[-1]
        if n == 0:
            x_left = lambda array: array[:, : zero // 2].reshape((zero,) + array.shape[2:])
            operands = [
                [(left, (), 0), left_x(0)],
                [(get("i1"), (), zero), (x_left(get("i2")), (), 0)],
                [(first[0], (), 0), right_x(0)],
                [(get("i0"), (), 0), (get("i1"), (), 0)],
                [(get("a1"), (), zero), (x_left(get("a2")), (), 0)],
                [(get("a0"), (), 0), (get("a1"), (), 0)],
            ]
        else:
            skip = zero // 2 if n == 1 else OUT_SIZES[n - 1]
            operands = [
                [(left, (), 0), left_x(n)],
                both(get(f"i{n + 2}")),
                [(later(n, 0), (), 0), right_x(n)],
                both(get(f"i{n + 1}"), skip),
                both(get(f"a{n + 2}")),
                both(get(f"a{n + 1}"), skip),
            ]
        leads = ((), (), (2,), (2, 2))
        return product_call(outgoing_kernel, operands, left.shape[0], leads, (4, size, 2 * size), "outgoing")

    for n in range(count):
        graph.add(f"p{n}", lambda n=n: later(n, 1), functools.partial(product, n))
        send(f"c{n}", "core", lambda n=n: get(f"p{n}")[3])
    return shared_steps(
        graph,
        OUT_GROUPS,
        lambda n, k: get(f"p{n}")[k] + get(f"c{n}")[0, k],
        lambda n: get(f"p{n}")[2] + get(f"c{n}")[1],
    )


def incoming(parts):
    count = len(IN_SIZES)
    graph = Graph(IN_ORDER)
    get, send = graph.get, graph.send
    for n in range(count):
        send(f"x{n}", "x", lambda n=n: parts[count + n])
    send("i0", "in", lambda: parts[0])
    send("i0x", "in", lambda: get("x0"))
    send("cl0", "core", lambda: parts[0])
    send("clx", "core", lambda: get("x0"))
    send("cp0", "core", lambda: get("i0"))
    send("cpx", "core", lambda: get("i0x"))
    for n in range(1, count):
        graph.add(f"j{n}", lambda n=n: parts[n], lambda own, n=n: jnp.stack([own, get(f"x{n}")], 1))
        send(f"i{n}", "in", lambda n=n: get(f"j{n}"))
        send(f"cl{n}", "core", lambda n=n: get(f"j{n}")[0])
        send(f"cp{n}", "core", lambda n=n: get(f"i{n}")[0])

    def product(n, own):
        size = own.shape[-1]
        if n == 0:
            side = lambda name, name_x, slot: [
                (own if name is None else get(name), (slot,), 0),
                (get(name_x), (slot,), 0),
            ]
            operands = [side(None, "x0", 0), side("cl0", "clx", 0), side("i0", "i0x", 0), side("cp0", "cpx", 0)]
            operands += [side(None, "x0", 1), side("i0", "i0x", 1)]
        else:
            side = lambda array, slot: [(array, (slot, k), 0) for k in range(2)]
            operands = [side(own, 0), both(get(f"cl{n}")), side(get(f"i{n}"), 0), both(get(f"cp{n}"))]
            operands += [side(own, 1), side(get(f"i{n}"), 1)]
        leads = ((), (), (2,), (2, 2))
        return product_call(incoming_kernel, operands, IN_SIZES[n], leads, (4, 2 * size, size), "incoming")

    for n in range(count):
        graph.add(f"p{n}", lambda n=n: get(f"j{n}") if n else parts[0], functools.partial(product, n))
        send(f"a{n}", "across", lambda n=n: get(f"p{n}")[3])
    return shared_steps(
        graph,
        IN_GROUPS,
        lambda n, k: get(f"p{n}")[k] + get(f"a{n}")[1, k],
        lambda n: get(f"p{n}")[2] + get(f"a{n}")[0],
    )


def four_by_four(pair, chain, block_mask, w_in, w_gate, w_out, gain_in, gain_out):
    gain_wide = jnp.broadcast_to(gain_out[:, :, None, None], gain_out.shape + (1, pair.shape[1]))
    gate, parts = first_call(chain, block_mask, pair, w_in, w_gate, gain_in)
    products = outgoing(parts)
    middle, gate, parts = middle_call(
        chain, block_mask, pair, gate, products, w_out, gain_wide[0], w_in, w_gate, gain_in
    )
    products = incoming(parts)
    return finish_call(middle, gate, products, w_out, gain_wide[1])


def solution(mesh):
    four = mesh.shape["row"] == 4 and mesh.shape["col"] == 4
    return jax.shard_map(
        four_by_four if four else any_mesh,
        mesh=mesh,
        in_specs=(
            P(("group", "row"), "col", None),
            P("group"),
            P("group", None),
            P(),
            P(),
            P(),
            P(),
            P(),
        ),
        out_specs=P(("group", "row"), "col", None),
        check_vma=False,
    )
```

```python
import functools

import jax
import jax.numpy as jnp
from jax import lax
from jax.experimental import pallas as pl
from jax.experimental.pallas import tpu as pltpu
from jax.sharding import PartitionSpec as P

BLOCK = 128
EPS = 1e-05
OUT_SIZES = (8, 8, 8, 4, 4)
IN_SIZES = (8, 8, 8, 4, 4)
OUT_GROUPS = (1, 1, 1, 1, 1)
IN_GROUPS = (1, 1, 1, 1, 1)
OUT_ORDER = {'i1': ('i0',), 'i2': ('i1',), 'i3': ('i2',), 'i4': ('i3',), 'i5': ('i4',), 'i6': ('i5',), 'a1': ('a0',), 'a2': ('a1',), 'a3': ('a2',), 'a4': ('a3',), 'a5': ('a4', 'p1'), 'a6': ('a5',), 'x2': ('x1', 'a1'), 'x3': ('x2',), 'x4': ('x3',), 'o2': ('o1',), 'x1': ('a0',), 'p2': ('o0',), 'p3': ('o1',), 'p4': ('o2',)}
IN_ORDER = {'i0x': ('i0',), 'i3': ('i2',), 'i4': ('i3',), 'a1': ('a0', 'i1'), 'a3': ('a2',), 'o2': ('o1',), 'o3': ('o2',), 'o4': ('o3',), 'x1': ('i0',), 'x2': ('i0x',), 'c4': ('c3',)}
STEP = 16
TOLD = 0.05
VMEM = 28 * 1024 * 1024
PRODUCT_VMEM = 10 * 1024 * 1024


def broadcast(block, axis, owner):
    block = jnp.where(lax.axis_index(axis) == owner, block, jnp.zeros_like(block))
    return lax.psum(block, axis)


def layer_norm(values, gain):
    mean = jnp.mean(values, -1, keepdims=True)
    centred = values - mean
    spread = jnp.mean(centred * centred, -1, keepdims=True)
    return centred * lax.rsqrt(spread + EPS) * gain


def project(pair, tile_mask, w_in, w_gate, gain_in):
    normed = layer_norm(pair.astype(jnp.float32), gain_in).astype(jnp.bfloat16)
    hidden = jnp.dot(normed, w_in, preferred_element_type=jnp.float32)
    width = w_in.shape[1] // 4
    masked = tile_mask[..., None]
    left = (masked * jax.nn.sigmoid(hidden[..., width : 2 * width]) * hidden[..., :width]).astype(
        jnp.bfloat16
    )
    right = (
        masked * jax.nn.sigmoid(hidden[..., 3 * width :]) * hidden[..., 2 * width : 3 * width]
    ).astype(jnp.bfloat16)
    gate = jax.nn.sigmoid(jnp.dot(normed, w_gate, preferred_element_type=jnp.float32))
    return (left, right, gate)


def finish(pair, product, gate, w_out, gain_out):
    update = layer_norm(product, gain_out).astype(jnp.bfloat16)
    return (
        pair.astype(jnp.float32) + gate * jnp.dot(update, w_out, preferred_element_type=jnp.float32)
    ).astype(jnp.bfloat16)


def any_mesh(pair, chain, block_mask, w_in, w_gate, w_out, gain_in, gain_out):
    tile_rows = pair.shape[0]
    tile_cols = pair.shape[1]
    block_count = chain.shape[0]
    ratio = lax.axis_size("row") // lax.axis_size("col")
    row_index = lax.axis_index("row")
    col_index = lax.axis_index("col")
    same = chain[:, None] == chain[None, :]
    blocks = jnp.where(same | (block_mask == 1), 1.0, 0.0).astype(jnp.float32)
    labels = jnp.arange(block_count, dtype=jnp.int32)
    row_blocks = (row_index * tile_rows + jnp.arange(tile_rows, dtype=jnp.int32)) // BLOCK
    col_blocks = (col_index * tile_cols + jnp.arange(tile_cols, dtype=jnp.int32)) // BLOCK
    row_onehot = jnp.where(row_blocks[:, None] == labels[None, :], 1.0, 0.0).astype(jnp.float32)
    col_onehot = jnp.where(col_blocks[:, None] == labels[None, :], 1.0, 0.0).astype(jnp.float32)
    tile_mask = jnp.dot(jnp.dot(row_onehot, blocks), col_onehot.T)
    left, right, gate = project(pair, tile_mask, w_in[0], w_gate[0], gain_in[0])
    partial_terms = jnp.einsum(
        "ikc,jkc->ijc",
        left,
        lax.all_gather(right, "row", axis=0, tiled=True),
        preferred_element_type=jnp.float32,
    )
    product = lax.psum_scatter(
        partial_terms.astype(jnp.bfloat16), "col", scatter_dimension=1, tiled=True
    ).astype(jnp.float32)
    middle = finish(pair, product, gate, w_out[0], gain_out[0])
    left, right, gate = project(middle, tile_mask, w_in[1], w_gate[1], gain_in[1])
    left_cols = lax.all_gather(left, "row", axis=0, tiled=True)
    start_col = row_index % ratio * tile_rows
    left_slice = lax.dynamic_slice_in_dim(left_cols, start_col, tile_rows, 1)
    left_mine = broadcast(left_slice, "col", row_index // ratio)
    product = jnp.einsum(
        "kic,kjc->ijc",
        left_mine,
        lax.all_gather(right, "row", axis=0, tiled=True),
        preferred_element_type=jnp.float32,
    )
    return finish(middle, product, gate, w_out[1], gain_out[1])


NN = (((1,), (0,)), ((), ()))
NT = (((1,), (1,)), ((), ()))
TN = (((0,), (0,)), ((), ()))
SMEM_SPEC = pl.BlockSpec(memory_space=pltpu.SMEM)


def dot(a, b, dims=NN):
    return lax.dot_general(a, b, dims, preferred_element_type=jnp.float32)


def norm_rows(rows, gain):
    channels = rows.shape[-1]
    place = lax.broadcasted_iota(jnp.int32, (channels, channels), 0)
    same = place == lax.broadcasted_iota(jnp.int32, (channels, channels), 1)
    centre = jnp.where(same, 1.0 - 1.0 / channels, -1.0 / channels).astype(jnp.bfloat16)
    mean_of = jnp.full((2 * channels, channels), 1.0 / channels, jnp.bfloat16)
    centred = dot(rows, centre)
    square = centred * centred
    high = square.astype(jnp.bfloat16)
    low = (square - high.astype(jnp.float32)).astype(jnp.bfloat16)
    spread = dot(jnp.concatenate([high, low], 1), mean_of)
    return (centred * lax.rsqrt(spread + EPS) * gain).astype(jnp.bfloat16)


def tile_mask(chain_ref, block_mask_ref):
    row, col = lax.axis_index("row"), lax.axis_index("col")
    seen = (chain_ref[row] == chain_ref[col]) | (block_mask_ref[row, col] == 1)
    return jnp.where(seen, 1.0, 0.0).astype(jnp.float32)


def pick_weights(w_ref, w_gate_ref, mask, turned, picked, picked_gate):
    @pl.when(pl.program_id(0) == 0)
    def _():
        turned[...] = w_ref[0].astype(jnp.float32).T
        half = turned.shape[0] // 8
        x = lax.axis_index("col") // 2
        rows = []
        for kind in range(4):
            for other in (x, 1 - x):
                some = turned[pl.ds(pl.multiple_of((2 * kind + other) * half, 8), half), :]
                rows.append(some * (0.5 if kind % 2 else 0.5 * mask))
        picked[...] = jnp.concatenate(rows, 0).astype(jnp.bfloat16)
        picked_gate[...] = (w_gate_ref[0].astype(jnp.float32) * 0.5).astype(jnp.bfloat16)


def project_part(normed, picked, scratch, sides, sizes):
    hidden = dot(picked[...], normed, NT)
    width = picked.shape[0] // 4
    cols = normed.shape[0] // STEP
    for side, refs in enumerate(sides):
        values = hidden[2 * side * width : (2 * side + 1) * width]
        gates = hidden[(2 * side + 1) * width : (2 * side + 2) * width]
        kept = (jnp.tanh(gates) + 1.0) * values
        for row in range(STEP):
            scratch[side, pl.ds(row, width, stride=STEP), :] = kept[:, row * cols : (row + 1) * cols]
        done = 0
        for ref, size in zip(refs, sizes * 2):
            rows = scratch[side, done * STEP : (done + size) * STEP, :]
            ref[...] = rows.astype(jnp.bfloat16).reshape(ref.shape)
            done += size


def split_sides(outs, count, apart):
    lefts, rights = [], []
    for n in range(count):
        if apart:
            rights.append(outs[2 * n])
            lefts.append(outs[2 * n + 1])
        else:
            lefts.append(outs[n].at[0])
            rights.append(outs[n].at[1])
    for ref in outs[-count:]:
        lefts.append(ref.at[1 if apart else 0])
        rights.append(ref.at[0 if apart else 1])
    return lefts, rights


def project_all(rows, gain, gate_ref, picked, picked_gate, scratch, outs, sizes, apart):
    normed = norm_rows(rows, gain)
    project_part(normed, picked, scratch, split_sides(outs, len(sizes), apart), sizes)
    gate = 0.5 * jnp.tanh(dot(normed, picked_gate[...])) + 0.5
    gate_ref[...] = gate.astype(gate_ref.dtype).reshape(gate_ref.shape)


def first_kernel(sizes, chain_ref, block_mask_ref, pair_ref, w_ref, w_gate_ref, gain_ref, gate_ref, *rest):
    *outs, turned, picked, picked_gate, scratch = rest
    pick_weights(w_ref, w_gate_ref, tile_mask(chain_ref, block_mask_ref), turned, picked, picked_gate)
    rows = pair_ref[...].reshape(-1, pair_ref.shape[-1])
    project_all(rows, gain_ref[0:1], gate_ref, picked, picked_gate, scratch, outs, sizes, True)


def finish_rows(pair_ref, gate_ref, product_refs, w_out_ref, gain_ref, scratch, twice, out_ref):
    width = w_out_ref.shape[1]
    half = width // 2
    cols = pair_ref.shape[1]
    x = lax.axis_index("col") // 2
    mine, others = pl.multiple_of(x * half, half), pl.multiple_of((1 - x) * half, half)

    @pl.when(pl.program_id(0) == 0)
    def _():
        w_out = jnp.concatenate([w_out_ref[0, pl.ds(mine, half)], w_out_ref[0, pl.ds(others, half)]], 0)
        none = jnp.zeros_like(w_out)
        twice[...] = jnp.concatenate(
            [jnp.concatenate([w_out, none], 1), jnp.concatenate([none, w_out], 1)], 0
        )

    gain = jnp.concatenate([gain_ref[pl.ds(mine, half)], gain_ref[pl.ds(others, half)]], 0)
    product = jnp.concatenate([ref[...] for ref in product_refs], 0).astype(jnp.float32)
    mean = jnp.sum(product, 0, keepdims=True) * (1.0 / width)
    centred = product - mean
    spread = jnp.sum(centred * centred, 0, keepdims=True) * (1.0 / width)
    update = centred * lax.rsqrt(spread + EPS) * gain
    scratch[...] = update.reshape(width * STEP, cols)
    for row in range(0, STEP, 2):
        two = jnp.concatenate(
            [scratch[pl.ds(row, width, stride=STEP), :], scratch[pl.ds(row + 1, width, stride=STEP), :]], 0
        )
        changes = dot(two.astype(jnp.bfloat16), twice[...], TN)
        for k in range(2):
            change = changes[:, k * pair_ref.shape[2] : (k + 1) * pair_ref.shape[2]]
            gate = gate_ref[row + k].astype(jnp.float32)
            old = pair_ref[row + k].astype(jnp.float32)
            out_ref[row + k] = (old + gate * change).astype(jnp.bfloat16)


def finish_kernel(pair_ref, gate_ref, w_out_ref, gain_ref, *rest):
    *product_refs, out_ref, scratch, twice = rest
    finish_rows(pair_ref, gate_ref, product_refs, w_out_ref, gain_ref, scratch, twice, out_ref)


def middle_kernel(
    sizes,
    count,
    chain_ref,
    block_mask_ref,
    pair_ref,
    gate_ref,
    w_out_ref,
    gain_out_ref,
    w_ref,
    w_gate_ref,
    gain_in_ref,
    *rest,
):
    product_refs, (out_ref, next_ref, *outs) = rest[:count], rest[count:]
    *outs, update, twice, turned, picked, picked_gate, scratch = outs
    pick_weights(w_ref, w_gate_ref, tile_mask(chain_ref, block_mask_ref), turned, picked, picked_gate)
    finish_rows(pair_ref, gate_ref, product_refs, w_out_ref, gain_out_ref, update, twice, out_ref)
    rows = out_ref[...].reshape(-1, out_ref.shape[-1])
    project_all(rows, gain_in_ref[1:2], next_ref, picked, picked_gate, scratch, outs, sizes, False)


def outgoing_kernel(left, left_pair, right, right_pair, right_far, right_near, outs, rights):
    *kept, pair, sent = outs
    for k, blocks in enumerate((right, right_pair, right_far, right_near)):
        rights[k] = jnp.concatenate(blocks, 1)
    lefts = jnp.concatenate([jnp.concatenate(left, 1), jnp.concatenate(left_pair, 1)], 0)
    size = lefts.shape[0] // 2
    here = lax.axis_index("row") ^ lax.axis_index("col")
    for place in range(4):
        terms = dot(lefts, rights[here ^ place], NT).astype(jnp.bfloat16)
        if place % 2:
            sent[0, place // 2, 0] = terms[:size]
            sent[1, place // 2, 0] = terms[size:]
        else:
            kept[place // 2][0] = terms[:size]
            pair[place // 2, 0] = terms[size:]


def incoming_kernel(left, left_core, left_pair, left_pair_core, right, right_pair, outs, lefts):
    *kept, pair, cross = outs
    for k in range(2):
        lefts[2 * k] = jnp.concatenate([left[k], left_pair[k]], 0)
        lefts[2 * k + 1] = jnp.concatenate([left_core[k], left_pair_core[k]], 0)
    rights = jnp.concatenate([jnp.concatenate(right, 1), jnp.concatenate(right_pair, 1)], 0)
    size = rights.shape[1] // 2
    here = lax.axis_index("row") ^ lax.axis_index("col")
    for place in range(4):
        terms = dot(lefts[here ^ place], rights, TN).astype(jnp.bfloat16)
        for k in range(2):
            block = terms[:, k * size : (k + 1) * size]
            if place == 0:
                kept[k][0] = block
            else:
                (pair, cross.at[0], cross.at[1])[place - 1][k, 0] = block


def pieces_kernel(kernel, count, *refs):
    blocks = [ref[(0,) * (len(ref.shape) - 2)] for ref in refs[:count]]
    kernel(*[blocks[k : k + 2] for k in range(0, count, 2)], refs[count:-1], refs[-1])


def params(limit=VMEM):
    return pltpu.CompilerParams(
        vmem_limit_bytes=limit, dimension_semantics=("arbitrary",), fuse_transposed_lhs_in_matmul=True
    )


def part(array, index):
    return pl.BlockSpec((1,) + array.shape[1:], lambda *_: (index,) + (0,) * (array.ndim - 1))


def whole(array):
    return pl.BlockSpec(array.shape, lambda *_: (0,) * array.ndim)


def tile_spec(tile):
    return pl.BlockSpec((STEP,) + tile.shape[1:], lambda r: (r, 0, 0))


def chunk_spec(shape):
    lead = shape[:-2]
    return pl.BlockSpec(lead + (STEP, shape[-1]), lambda r: (0,) * len(lead) + (r, 0))


def cost(flops, nbytes, special=0):
    return pl.CostEstimate(
        flops=int(flops * TOLD), bytes_accessed=int(nbytes * TOLD), transcendentals=int(special * TOLD)
    )


def part_outs(pair, sizes, apart):
    tile = pair.shape[:2]
    own = [(size,) + tile for size in sizes]
    both_sides = [(2,) + shape for shape in own]
    shapes = ([shape for shape in own for _ in range(2)] if apart else both_sides) + both_sides
    return [jax.ShapeDtypeStruct(shape, jnp.bfloat16) for shape in shapes], [chunk_spec(shape) for shape in shapes]


def part_scratch(pair, w_in, sizes):
    width = 2 * sum(sizes)
    return [
        pltpu.VMEM((w_in.shape[2], w_in.shape[1]), jnp.float32),
        pltpu.VMEM((4 * width, w_in.shape[1]), jnp.bfloat16),
        pltpu.VMEM((w_in.shape[1], w_in.shape[1]), jnp.bfloat16),
        pltpu.VMEM((2, width * STEP, pair.shape[1]), jnp.float32),
    ]


def finish_scratch(pair, w_out):
    return [
        pltpu.VMEM((w_out.shape[1] * STEP, pair.shape[1]), jnp.float32),
        pltpu.VMEM((2 * w_out.shape[1], 2 * w_out.shape[2]), jnp.bfloat16),
    ]


def first_call(chain, block_mask, pair, w_in, w_gate, gain_in):
    outs, specs = part_outs(pair, OUT_SIZES, True)
    gate, *result = pl.pallas_call(
        functools.partial(first_kernel, OUT_SIZES),
        grid=(pair.shape[0] // STEP,),
        in_specs=[SMEM_SPEC, SMEM_SPEC, tile_spec(pair), part(w_in, 0), part(w_gate, 0), whole(gain_in)],
        out_specs=[tile_spec(pair)] + specs,
        out_shape=[jax.ShapeDtypeStruct(pair.shape, pair.dtype)] + outs,
        scratch_shapes=part_scratch(pair, w_in, OUT_SIZES),
        compiler_params=params(),
        cost_estimate=cost(2e9, 8 << 20, 4 << 20),
        name="project",
    )(chain, block_mask, pair, w_in, w_gate, gain_in)
    return gate, result


def finish_call(pair, gate, products, w_out, gain_wide):
    return pl.pallas_call(
        finish_kernel,
        grid=(pair.shape[0] // STEP,),
        in_specs=[tile_spec(pair), tile_spec(gate), part(w_out, 1), whole(gain_wide)]
        + [chunk_spec(p.shape) for p in products],
        out_specs=tile_spec(pair),
        out_shape=jax.ShapeDtypeStruct(pair.shape, pair.dtype),
        scratch_shapes=finish_scratch(pair, w_out),
        compiler_params=params(),
        cost_estimate=cost(1e9, 14 << 20, 4 << 20),
        name="finish",
    )(pair, gate, w_out, gain_wide, *products)


def middle_call(chain, block_mask, pair, gate, products, w_out, gain_wide, w_in, w_gate, gain_in):
    outs, specs = part_outs(pair, IN_SIZES, False)
    middle, gate, *result = pl.pallas_call(
        functools.partial(middle_kernel, IN_SIZES, len(products)),
        grid=(pair.shape[0] // STEP,),
        in_specs=[SMEM_SPEC, SMEM_SPEC, tile_spec(pair), tile_spec(gate), part(w_out, 0)]
        + [whole(gain_wide), part(w_in, 1), part(w_gate, 1), whole(gain_in)]
        + [chunk_spec(p.shape) for p in products],
        out_specs=[tile_spec(pair)] * 2 + specs,
        out_shape=[jax.ShapeDtypeStruct(pair.shape, pair.dtype)] * 2 + outs,
        scratch_shapes=finish_scratch(pair, w_out) + part_scratch(pair, w_in, IN_SIZES),
        compiler_params=params(),
        cost_estimate=cost(3e9, 18 << 20, 8 << 20),
        name="middle",
    )(chain, block_mask, pair, gate, w_out, gain_wide, w_in, w_gate, gain_in, *products)
    return middle, gate, result


def product_call(kernel, operands, channels, leads, scratch, name):
    pieces = [piece for operand in operands for piece in operand]
    size = pieces[0][0].shape[-1]

    def piece_spec(array, lead, first):
        return pl.BlockSpec((1,) * (len(lead) + 1) + (size, size), lambda c: lead + (first + c, 0, 0))

    def out_spec(lead):
        return pl.BlockSpec(lead + (1, size, size), lambda c: (0,) * len(lead) + (c, 0, 0))

    return pl.pallas_call(
        functools.partial(pieces_kernel, kernel, len(pieces)),
        grid=(channels,),
        in_specs=[piece_spec(*piece) for piece in pieces],
        out_specs=[out_spec(lead) for lead in leads],
        out_shape=[jax.ShapeDtypeStruct(lead + (channels, size, size), jnp.bfloat16) for lead in leads],
        scratch_shapes=[pltpu.VMEM(scratch, jnp.bfloat16)],
        compiler_params=params(PRODUCT_VMEM),
        cost_estimate=cost(channels * 2 * (4 * size) ** 2 * size, channels * size * size * 2 * 20),
        name=name,
    )(*[piece[0] for piece in pieces])


WAYS = {
    "in": ("row", [(0, 1), (3, 2)]),
    "across": ("row", [(1, 2), (2, 1)]),
    "out": ("row", [(1, 0), (2, 3)]),
    "x": ("col", [(c, c ^ 2) for c in range(4)]),
    "core": ("col", [(c, c ^ 1) for c in range(4)]),
}


class Graph:
    def __init__(self, order):
        self.order, self.steps, self.made = order, {}, {}

    def add(self, name, operand, step):
        self.steps[name] = (operand, step)

    def send(self, name, way, operand):
        axis, pairs = WAYS[way]
        self.add(name, operand, lambda array: lax.ppermute(array, axis, pairs))

    def get(self, name):
        if name not in self.made:
            operand, step = self.steps[name]
            waits = [self.get(other) for other in self.order.get(name, ())]
            array = operand()
            if waits:
                array = lax.optimization_barrier((array, *waits))[0]
            self.made[name] = step(array)
        return self.made[name]


def pack(*columns):
    return jnp.stack([jnp.concatenate([column[k] for column in columns]) for k in range(2)])


def both(array, first=0, lead=()):
    return [(array, (k,) + lead, first) for k in range(2)]


def is_inner():
    row = lax.axis_index("row")
    return (row == 1) | (row == 2)


def shared_steps(graph, groups, mine, other):
    inner = is_inner()
    get = graph.get
    first, names = 0, []

    def joined(arrays, axis):
        return arrays[0] if len(arrays) == 1 else jnp.concatenate(arrays, axis)

    for g, size in enumerate(groups):
        chunks = range(first, first + size)
        first += size

        def ready(k, g=g, chunks=chunks):
            return jnp.where(inner, joined([mine(n, k) for n in chunks], 0), get(f"o{g}")[k])

        graph.send(f"o{g}", "out", lambda chunks=chunks: joined([other(n) for n in chunks], 1))
        graph.send(f"b{g}", "x", lambda ready=ready: ready(1))
        graph.add(f"k{g}", lambda ready=ready: ready(0), lambda array: array)
    return [get(kind + str(g)) for kind in ("k", "b") for g in range(len(groups))]


def outgoing(parts):
    count = len(OUT_SIZES)
    graph = Graph(OUT_ORDER)
    get, send = graph.get, graph.send
    for n in range(count):
        send(f"x{n}", "x", lambda n=n: parts[2 * count + n])
    later = lambda n, side: parts[2 * n + side]
    right_of = lambda n: (later(n, 0), get(f"x{n}")[0])
    left_of = lambda n: (later(n, 1), get(f"x{n}")[1])
    first = parts
    zero = OUT_SIZES[0]
    send("i0", "in", lambda: first[0])
    send("a0", "across", lambda: first[0])
    send("i1", "in", lambda: jnp.concatenate([get("x0")[0], first[1]]))
    send("a1", "across", lambda: jnp.concatenate([get("x0")[0], get("i0")]))

    def come(n):
        array, skip = get(f"i{n + 1}"), zero // 2 if n == 1 else OUT_SIZES[n - 1]
        return (array[0, skip:], array[1, skip:])

    def halves(array):
        return (array[: zero // 2], array[zero // 2 :])

    def inward(n):
        before = halves(get("x0")[1]) if n == 1 else left_of(n - 1)
        return pack(before, right_of(n)) if n < count else pack(before)

    def across(n):
        before = halves(get("i1")[:zero]) if n == 1 else come(n - 1)
        return pack(before, right_of(n)) if n < count else pack(before)

    for n in range(1, count + 1):
        send(f"i{n + 1}", "in", lambda n=n: inward(n))
        send(f"a{n + 1}", "across", lambda n=n: across(n))

    def product(n, left):
        size = left.shape[-1]
        if n == 0:
            x_left = lambda array: array[:, : zero // 2].reshape((zero,) + array.shape[2:])
            operands = [
                [(left, (), 0), (get("x0"), (1,), 0)],
                [(get("i1"), (), zero), (x_left(get("i2")), (), 0)],
                [(first[0], (), 0), (get("x0"), (0,), 0)],
                [(get("i0"), (), 0), (get("i1"), (), 0)],
                [(get("a1"), (), zero), (x_left(get("a2")), (), 0)],
                [(get("a0"), (), 0), (get("a1"), (), 0)],
            ]
        else:
            skip = zero // 2 if n == 1 else OUT_SIZES[n - 1]
            operands = [
                [(left, (), 0), (get(f"x{n}"), (1,), 0)],
                both(get(f"i{n + 2}")),
                [(later(n, 0), (), 0), (get(f"x{n}"), (0,), 0)],
                both(get(f"i{n + 1}"), skip),
                both(get(f"a{n + 2}")),
                both(get(f"a{n + 1}"), skip),
            ]
        leads = ((), (), (2,), (2, 2))
        return product_call(outgoing_kernel, operands, left.shape[0], leads, (4, size, 2 * size), "outgoing")

    for n in range(count):
        graph.add(f"p{n}", lambda n=n: later(n, 1), functools.partial(product, n))
        send(f"c{n}", "core", lambda n=n: get(f"p{n}")[3])
    return shared_steps(
        graph,
        OUT_GROUPS,
        lambda n, k: get(f"p{n}")[k] + get(f"c{n}")[0, k],
        lambda n: get(f"p{n}")[2] + get(f"c{n}")[1],
    )


def incoming(parts):
    count = len(IN_SIZES)
    graph = Graph(IN_ORDER)
    get, send = graph.get, graph.send
    for n in range(count):
        send(f"x{n}", "x", lambda n=n: parts[count + n])
    send("i0", "in", lambda: parts[0])
    send("i0x", "in", lambda: get("x0"))
    send("cl0", "core", lambda: parts[0])
    send("clx", "core", lambda: get("x0"))
    send("cp0", "core", lambda: get("i0"))
    send("cpx", "core", lambda: get("i0x"))
    for n in range(1, count):
        graph.add(f"j{n}", lambda n=n: parts[n], lambda own, n=n: jnp.stack([own, get(f"x{n}")], 1))
        send(f"i{n}", "in", lambda n=n: get(f"j{n}"))
        send(f"cl{n}", "core", lambda n=n: get(f"j{n}")[0])
        send(f"cp{n}", "core", lambda n=n: get(f"i{n}")[0])

    def product(n, own):
        size = own.shape[-1]
        if n == 0:
            side = lambda name, name_x, slot: [
                (own if name is None else get(name), (slot,), 0),
                (get(name_x), (slot,), 0),
            ]
            operands = [side(None, "x0", 0), side("cl0", "clx", 0), side("i0", "i0x", 0), side("cp0", "cpx", 0)]
            operands += [side(None, "x0", 1), side("i0", "i0x", 1)]
        else:
            side = lambda array, slot: [(array, (slot, k), 0) for k in range(2)]
            operands = [side(own, 0), both(get(f"cl{n}")), side(get(f"i{n}"), 0), both(get(f"cp{n}"))]
            operands += [side(own, 1), side(get(f"i{n}"), 1)]
        leads = ((), (), (2,), (2, 2))
        return product_call(incoming_kernel, operands, IN_SIZES[n], leads, (4, 2 * size, size), "incoming")

    for n in range(count):
        graph.add(f"p{n}", lambda n=n: get(f"j{n}") if n else parts[0], functools.partial(product, n))
        send(f"a{n}", "across", lambda n=n: get(f"p{n}")[3])
    return shared_steps(
        graph,
        IN_GROUPS,
        lambda n, k: get(f"p{n}")[k] + get(f"a{n}")[1, k],
        lambda n: get(f"p{n}")[2] + get(f"a{n}")[0],
    )


def four_by_four(pair, chain, block_mask, w_in, w_gate, w_out, gain_in, gain_out):
    gain_wide = jnp.broadcast_to(gain_out[:, :, None, None], gain_out.shape + (1, pair.shape[1]))
    gate, parts = first_call(chain, block_mask, pair, w_in, w_gate, gain_in)
    products = outgoing(parts)
    middle, gate, parts = middle_call(
        chain, block_mask, pair, gate, products, w_out, gain_wide[0], w_in, w_gate, gain_in
    )
    products = incoming(parts)
    return finish_call(middle, gate, products, w_out, gain_wide[1])


def solution(mesh):
    four = mesh.shape["row"] == 4 and mesh.shape["col"] == 4
    return jax.shard_map(
        four_by_four if four else any_mesh,
        mesh=mesh,
        in_specs=(
            P(("group", "row"), "col", None),
            P("group"),
            P("group", None),
            P(),
            P(),
            P(),
            P(),
            P(),
        ),
        out_specs=P(("group", "row"), "col", None),
        check_vma=False,
    )
```

```python
import functools

import jax
import jax.numpy as jnp
from jax import lax
from jax.experimental import pallas as pl
from jax.experimental.pallas import tpu as pltpu
from jax.sharding import PartitionSpec as P

BLOCK = 128
EPS = 1e-05
OUT_SIZES = (8, 8, 8, 4, 4)
IN_SIZES = (8, 8, 8, 4, 4)
OUT_GROUPS = (1, 1, 1, 1, 1)
IN_GROUPS = (1, 1, 1, 1, 1)
OUT_ORDER = {'i1': ('i0',), 'i2': ('i1',), 'i3': ('i2',), 'i4': ('i3',), 'i5': ('i4',), 'i6': ('i5',), 'a1': ('a0',), 'a2': ('a1',), 'a3': ('a2',), 'a4': ('a3',), 'a5': ('a4', 'p1'), 'a6': ('a5',), 'x2': ('x1', 'a1'), 'x3': ('x2',), 'x4': ('x3',), 'o2': ('o1',), 'x1': ('a0',), 'p2': ('o0',), 'p3': ('o1',), 'p4': ('o2',)}
IN_ORDER = {'i0x': ('i0',), 'i3': ('i2',), 'i4': ('i3',), 'a1': ('a0', 'i1'), 'a3': ('a2',), 'o2': ('o1',), 'o3': ('o2',), 'o4': ('o3',), 'x1': ('i0',), 'x2': ('i0x',), 'c4': ('c3',)}
STEP = 16
TOLD = 0.05
VMEM = 28 * 1024 * 1024
PRODUCT_VMEM = 10 * 1024 * 1024


def broadcast(block, axis, owner):
    block = jnp.where(lax.axis_index(axis) == owner, block, jnp.zeros_like(block))
    return lax.psum(block, axis)


def layer_norm(values, gain):
    mean = jnp.mean(values, -1, keepdims=True)
    centred = values - mean
    spread = jnp.mean(centred * centred, -1, keepdims=True)
    return centred * lax.rsqrt(spread + EPS) * gain


def project(pair, tile_mask, w_in, w_gate, gain_in):
    normed = layer_norm(pair.astype(jnp.float32), gain_in).astype(jnp.bfloat16)
    hidden = jnp.dot(normed, w_in, preferred_element_type=jnp.float32)
    width = w_in.shape[1] // 4
    masked = tile_mask[..., None]
    left = (masked * jax.nn.sigmoid(hidden[..., width : 2 * width]) * hidden[..., :width]).astype(
        jnp.bfloat16
    )
    right = (
        masked * jax.nn.sigmoid(hidden[..., 3 * width :]) * hidden[..., 2 * width : 3 * width]
    ).astype(jnp.bfloat16)
    gate = jax.nn.sigmoid(jnp.dot(normed, w_gate, preferred_element_type=jnp.float32))
    return (left, right, gate)


def finish(pair, product, gate, w_out, gain_out):
    update = layer_norm(product, gain_out).astype(jnp.bfloat16)
    return (
        pair.astype(jnp.float32) + gate * jnp.dot(update, w_out, preferred_element_type=jnp.float32)
    ).astype(jnp.bfloat16)


def any_mesh(pair, chain, block_mask, w_in, w_gate, w_out, gain_in, gain_out):
    tile_rows = pair.shape[0]
    tile_cols = pair.shape[1]
    block_count = chain.shape[0]
    ratio = lax.axis_size("row") // lax.axis_size("col")
    row_index = lax.axis_index("row")
    col_index = lax.axis_index("col")
    same = chain[:, None] == chain[None, :]
    blocks = jnp.where(same | (block_mask == 1), 1.0, 0.0).astype(jnp.float32)
    labels = jnp.arange(block_count, dtype=jnp.int32)
    row_blocks = (row_index * tile_rows + jnp.arange(tile_rows, dtype=jnp.int32)) // BLOCK
    col_blocks = (col_index * tile_cols + jnp.arange(tile_cols, dtype=jnp.int32)) // BLOCK
    row_onehot = jnp.where(row_blocks[:, None] == labels[None, :], 1.0, 0.0).astype(jnp.float32)
    col_onehot = jnp.where(col_blocks[:, None] == labels[None, :], 1.0, 0.0).astype(jnp.float32)
    tile_mask = jnp.dot(jnp.dot(row_onehot, blocks), col_onehot.T)
    left, right, gate = project(pair, tile_mask, w_in[0], w_gate[0], gain_in[0])
    partial_terms = jnp.einsum(
        "ikc,jkc->ijc",
        left,
        lax.all_gather(right, "row", axis=0, tiled=True),
        preferred_element_type=jnp.float32,
    )
    product = lax.psum_scatter(
        partial_terms.astype(jnp.bfloat16), "col", scatter_dimension=1, tiled=True
    ).astype(jnp.float32)
    middle = finish(pair, product, gate, w_out[0], gain_out[0])
    left, right, gate = project(middle, tile_mask, w_in[1], w_gate[1], gain_in[1])
    left_cols = lax.all_gather(left, "row", axis=0, tiled=True)
    start_col = row_index % ratio * tile_rows
    left_slice = lax.dynamic_slice_in_dim(left_cols, start_col, tile_rows, 1)
    left_mine = broadcast(left_slice, "col", row_index // ratio)
    product = jnp.einsum(
        "kic,kjc->ijc",
        left_mine,
        lax.all_gather(right, "row", axis=0, tiled=True),
        preferred_element_type=jnp.float32,
    )
    return finish(middle, product, gate, w_out[1], gain_out[1])


NN = (((1,), (0,)), ((), ()))
NT = (((1,), (1,)), ((), ()))
TN = (((0,), (0,)), ((), ()))
SMEM_SPEC = pl.BlockSpec(memory_space=pltpu.SMEM)


def dot(a, b, dims=NN):
    return lax.dot_general(a, b, dims, preferred_element_type=jnp.float32)


def norm_rows(rows, gain):
    channels = rows.shape[-1]
    place = lax.broadcasted_iota(jnp.int32, (channels, channels), 0)
    same = place == lax.broadcasted_iota(jnp.int32, (channels, channels), 1)
    centre = jnp.where(same, 1.0 - 1.0 / channels, -1.0 / channels).astype(jnp.bfloat16)
    mean_of = jnp.full((channels, channels), 1.0 / channels, jnp.bfloat16)
    centred = dot(rows, centre)
    spread = dot((centred * centred).astype(jnp.bfloat16), mean_of)
    return (centred * lax.rsqrt(spread + EPS) * gain).astype(jnp.bfloat16)


def tile_mask(chain_ref, block_mask_ref):
    row, col = lax.axis_index("row"), lax.axis_index("col")
    seen = (chain_ref[row] == chain_ref[col]) | (block_mask_ref[row, col] == 1)
    return jnp.where(seen, 1.0, 0.0).astype(jnp.float32)


def pick_weights(w_ref, w_gate_ref, mask, turned, picked, picked_gate):
    @pl.when(pl.program_id(0) == 0)
    def _():
        turned[...] = w_ref[0].astype(jnp.float32).T
        half = turned.shape[0] // 8
        x = lax.axis_index("col") // 2
        rows = []
        for kind in range(4):
            for other in (x, 1 - x):
                some = turned[pl.ds(pl.multiple_of((2 * kind + other) * half, 8), half), :]
                rows.append(some * (0.5 if kind % 2 else 0.5 * mask))
        picked[...] = jnp.concatenate(rows, 0).astype(jnp.bfloat16)
        picked_gate[...] = (w_gate_ref[0].astype(jnp.float32) * 0.5).astype(jnp.bfloat16)


def project_part(normed, picked, scratch, sides, sizes):
    hidden = dot(picked[...], normed, NT)
    width = picked.shape[0] // 4
    cols = normed.shape[0] // STEP
    for side, refs in enumerate(sides):
        values = hidden[2 * side * width : (2 * side + 1) * width]
        gates = hidden[(2 * side + 1) * width : (2 * side + 2) * width]
        kept = (jnp.tanh(gates) + 1.0) * values
        for row in range(STEP):
            scratch[side, pl.ds(row, width, stride=STEP), :] = kept[:, row * cols : (row + 1) * cols]
        done = 0
        for ref, size in zip(refs, sizes * 2):
            rows = scratch[side, done * STEP : (done + size) * STEP, :]
            ref[...] = rows.astype(jnp.bfloat16).reshape(ref.shape)
            done += size


def split_sides(outs, count, apart):
    lefts, rights = [], []
    for n in range(count):
        if apart:
            rights.append(outs[2 * n])
            lefts.append(outs[2 * n + 1])
        else:
            lefts.append(outs[n].at[0])
            rights.append(outs[n].at[1])
    for ref in outs[-count:]:
        lefts.append(ref.at[1 if apart else 0])
        rights.append(ref.at[0 if apart else 1])
    return lefts, rights


def project_all(rows, gain, gate_ref, picked, picked_gate, scratch, outs, sizes, apart):
    normed = norm_rows(rows, gain)
    project_part(normed, picked, scratch, split_sides(outs, len(sizes), apart), sizes)
    gate = 0.5 * jnp.tanh(dot(normed, picked_gate[...])) + 0.5
    gate_ref[...] = gate.astype(gate_ref.dtype).reshape(gate_ref.shape)


def first_kernel(sizes, chain_ref, block_mask_ref, pair_ref, w_ref, w_gate_ref, gain_ref, gate_ref, *rest):
    *outs, turned, picked, picked_gate, scratch = rest
    pick_weights(w_ref, w_gate_ref, tile_mask(chain_ref, block_mask_ref), turned, picked, picked_gate)
    rows = pair_ref[...].reshape(-1, pair_ref.shape[-1])
    project_all(rows, gain_ref[0:1], gate_ref, picked, picked_gate, scratch, outs, sizes, True)


def finish_rows(pair_ref, gate_ref, product_refs, w_out_ref, gain_ref, scratch, twice, out_ref):
    width = w_out_ref.shape[1]
    half = width // 2
    cols = pair_ref.shape[1]
    x = lax.axis_index("col") // 2
    mine, others = pl.multiple_of(x * half, half), pl.multiple_of((1 - x) * half, half)

    @pl.when(pl.program_id(0) == 0)
    def _():
        w_out = jnp.concatenate([w_out_ref[0, pl.ds(mine, half)], w_out_ref[0, pl.ds(others, half)]], 0)
        none = jnp.zeros_like(w_out)
        twice[...] = jnp.concatenate(
            [jnp.concatenate([w_out, none], 1), jnp.concatenate([none, w_out], 1)], 0
        )

    gain = jnp.concatenate([gain_ref[pl.ds(mine, half)], gain_ref[pl.ds(others, half)]], 0)
    product = jnp.concatenate([ref[...] for ref in product_refs], 0).astype(jnp.float32)
    mean = jnp.sum(product, 0, keepdims=True) * (1.0 / width)
    centred = product - mean
    spread = jnp.sum(centred * centred, 0, keepdims=True) * (1.0 / width)
    update = centred * lax.rsqrt(spread + EPS) * gain
    scratch[...] = update.reshape(width * STEP, cols)
    for row in range(0, STEP, 2):
        two = jnp.concatenate(
            [scratch[pl.ds(row, width, stride=STEP), :], scratch[pl.ds(row + 1, width, stride=STEP), :]], 0
        )
        changes = dot(two.astype(jnp.bfloat16), twice[...], TN)
        for k in range(2):
            change = changes[:, k * pair_ref.shape[2] : (k + 1) * pair_ref.shape[2]]
            gate = gate_ref[row + k].astype(jnp.float32)
            old = pair_ref[row + k].astype(jnp.float32)
            out_ref[row + k] = (old + gate * change).astype(jnp.bfloat16)


def finish_kernel(pair_ref, gate_ref, w_out_ref, gain_ref, *rest):
    *product_refs, out_ref, scratch, twice = rest
    finish_rows(pair_ref, gate_ref, product_refs, w_out_ref, gain_ref, scratch, twice, out_ref)


def middle_kernel(
    sizes,
    count,
    chain_ref,
    block_mask_ref,
    pair_ref,
    gate_ref,
    w_out_ref,
    gain_out_ref,
    w_ref,
    w_gate_ref,
    gain_in_ref,
    *rest,
):
    product_refs, (out_ref, next_ref, *outs) = rest[:count], rest[count:]
    *outs, update, twice, turned, picked, picked_gate, scratch = outs
    pick_weights(w_ref, w_gate_ref, tile_mask(chain_ref, block_mask_ref), turned, picked, picked_gate)
    finish_rows(pair_ref, gate_ref, product_refs, w_out_ref, gain_out_ref, update, twice, out_ref)
    rows = out_ref[...].reshape(-1, out_ref.shape[-1])
    project_all(rows, gain_in_ref[1:2], next_ref, picked, picked_gate, scratch, outs, sizes, False)


def outgoing_kernel(left, left_pair, right, right_pair, right_far, right_near, outs, rights):
    *kept, pair, sent = outs
    for k, blocks in enumerate((right, right_pair, right_far, right_near)):
        rights[k] = jnp.concatenate(blocks, 1)
    lefts = jnp.concatenate([jnp.concatenate(left, 1), jnp.concatenate(left_pair, 1)], 0)
    size = lefts.shape[0] // 2
    here = lax.axis_index("row") ^ lax.axis_index("col")
    for place in range(4):
        terms = dot(lefts, rights[here ^ place], NT).astype(jnp.bfloat16)
        if place % 2:
            sent[0, place // 2, 0] = terms[:size]
            sent[1, place // 2, 0] = terms[size:]
        else:
            kept[place // 2][0] = terms[:size]
            pair[place // 2, 0] = terms[size:]


def incoming_kernel(left, left_core, left_pair, left_pair_core, right, right_pair, outs, lefts):
    *kept, pair, cross = outs
    for k in range(2):
        lefts[2 * k] = jnp.concatenate([left[k], left_pair[k]], 0)
        lefts[2 * k + 1] = jnp.concatenate([left_core[k], left_pair_core[k]], 0)
    rights = jnp.concatenate([jnp.concatenate(right, 1), jnp.concatenate(right_pair, 1)], 0)
    size = rights.shape[1] // 2
    here = lax.axis_index("row") ^ lax.axis_index("col")
    for place in range(4):
        terms = dot(lefts[here ^ place], rights, TN).astype(jnp.bfloat16)
        for k in range(2):
            block = terms[:, k * size : (k + 1) * size]
            if place == 0:
                kept[k][0] = block
            else:
                (pair, cross.at[0], cross.at[1])[place - 1][k, 0] = block


def pieces_kernel(kernel, count, *refs):
    blocks = [ref[(0,) * (len(ref.shape) - 2)] for ref in refs[:count]]
    kernel(*[blocks[k : k + 2] for k in range(0, count, 2)], refs[count:-1], refs[-1])


def params(limit=VMEM):
    return pltpu.CompilerParams(
        vmem_limit_bytes=limit, dimension_semantics=("arbitrary",), fuse_transposed_lhs_in_matmul=True
    )


def part(array, index):
    return pl.BlockSpec((1,) + array.shape[1:], lambda *_: (index,) + (0,) * (array.ndim - 1))


def whole(array):
    return pl.BlockSpec(array.shape, lambda *_: (0,) * array.ndim)


def tile_spec(tile):
    return pl.BlockSpec((STEP,) + tile.shape[1:], lambda r: (r, 0, 0))


def chunk_spec(shape):
    lead = shape[:-2]
    return pl.BlockSpec(lead + (STEP, shape[-1]), lambda r: (0,) * len(lead) + (r, 0))


def cost(flops, nbytes, special=0):
    return pl.CostEstimate(
        flops=int(flops * TOLD), bytes_accessed=int(nbytes * TOLD), transcendentals=int(special * TOLD)
    )


def part_outs(pair, sizes, apart):
    tile = pair.shape[:2]
    own = [(size,) + tile for size in sizes]
    both_sides = [(2,) + shape for shape in own]
    shapes = ([shape for shape in own for _ in range(2)] if apart else both_sides) + both_sides
    return [jax.ShapeDtypeStruct(shape, jnp.bfloat16) for shape in shapes], [chunk_spec(shape) for shape in shapes]


def part_scratch(pair, w_in, sizes):
    width = 2 * sum(sizes)
    return [
        pltpu.VMEM((w_in.shape[2], w_in.shape[1]), jnp.float32),
        pltpu.VMEM((4 * width, w_in.shape[1]), jnp.bfloat16),
        pltpu.VMEM((w_in.shape[1], w_in.shape[1]), jnp.bfloat16),
        pltpu.VMEM((2, width * STEP, pair.shape[1]), jnp.float32),
    ]


def finish_scratch(pair, w_out):
    return [
        pltpu.VMEM((w_out.shape[1] * STEP, pair.shape[1]), jnp.float32),
        pltpu.VMEM((2 * w_out.shape[1], 2 * w_out.shape[2]), jnp.bfloat16),
    ]


def first_call(chain, block_mask, pair, w_in, w_gate, gain_in):
    outs, specs = part_outs(pair, OUT_SIZES, True)
    gate, *result = pl.pallas_call(
        functools.partial(first_kernel, OUT_SIZES),
        grid=(pair.shape[0] // STEP,),
        in_specs=[SMEM_SPEC, SMEM_SPEC, tile_spec(pair), part(w_in, 0), part(w_gate, 0), whole(gain_in)],
        out_specs=[tile_spec(pair)] + specs,
        out_shape=[jax.ShapeDtypeStruct(pair.shape, pair.dtype)] + outs,
        scratch_shapes=part_scratch(pair, w_in, OUT_SIZES),
        compiler_params=params(),
        cost_estimate=cost(2e9, 8 << 20, 4 << 20),
        name="project",
    )(chain, block_mask, pair, w_in, w_gate, gain_in)
    return gate, result


def finish_call(pair, gate, products, w_out, gain_wide):
    return pl.pallas_call(
        finish_kernel,
        grid=(pair.shape[0] // STEP,),
        in_specs=[tile_spec(pair), tile_spec(gate), part(w_out, 1), whole(gain_wide)]
        + [chunk_spec(p.shape) for p in products],
        out_specs=tile_spec(pair),
        out_shape=jax.ShapeDtypeStruct(pair.shape, pair.dtype),
        scratch_shapes=finish_scratch(pair, w_out),
        compiler_params=params(),
        cost_estimate=cost(1e9, 14 << 20, 4 << 20),
        name="finish",
    )(pair, gate, w_out, gain_wide, *products)


def middle_call(chain, block_mask, pair, gate, products, w_out, gain_wide, w_in, w_gate, gain_in):
    outs, specs = part_outs(pair, IN_SIZES, False)
    middle, gate, *result = pl.pallas_call(
        functools.partial(middle_kernel, IN_SIZES, len(products)),
        grid=(pair.shape[0] // STEP,),
        in_specs=[SMEM_SPEC, SMEM_SPEC, tile_spec(pair), tile_spec(gate), part(w_out, 0)]
        + [whole(gain_wide), part(w_in, 1), part(w_gate, 1), whole(gain_in)]
        + [chunk_spec(p.shape) for p in products],
        out_specs=[tile_spec(pair)] * 2 + specs,
        out_shape=[jax.ShapeDtypeStruct(pair.shape, pair.dtype)] * 2 + outs,
        scratch_shapes=finish_scratch(pair, w_out) + part_scratch(pair, w_in, IN_SIZES),
        compiler_params=params(),
        cost_estimate=cost(3e9, 18 << 20, 8 << 20),
        name="middle",
    )(chain, block_mask, pair, gate, w_out, gain_wide, w_in, w_gate, gain_in, *products)
    return middle, gate, result


def product_call(kernel, operands, channels, leads, scratch, name):
    pieces = [piece for operand in operands for piece in operand]
    size = pieces[0][0].shape[-1]

    def piece_spec(array, lead, first):
        return pl.BlockSpec((1,) * (len(lead) + 1) + (size, size), lambda c: lead + (first + c, 0, 0))

    def out_spec(lead):
        return pl.BlockSpec(lead + (1, size, size), lambda c: (0,) * len(lead) + (c, 0, 0))

    return pl.pallas_call(
        functools.partial(pieces_kernel, kernel, len(pieces)),
        grid=(channels,),
        in_specs=[piece_spec(*piece) for piece in pieces],
        out_specs=[out_spec(lead) for lead in leads],
        out_shape=[jax.ShapeDtypeStruct(lead + (channels, size, size), jnp.bfloat16) for lead in leads],
        scratch_shapes=[pltpu.VMEM(scratch, jnp.bfloat16)],
        compiler_params=params(PRODUCT_VMEM),
        cost_estimate=cost(channels * 2 * (4 * size) ** 2 * size, channels * size * size * 2 * 20),
        name=name,
    )(*[piece[0] for piece in pieces])


WAYS = {
    "in": ("row", [(0, 1), (3, 2)]),
    "across": ("row", [(1, 2), (2, 1)]),
    "out": ("row", [(1, 0), (2, 3)]),
    "x": ("col", [(c, c ^ 2) for c in range(4)]),
    "core": ("col", [(c, c ^ 1) for c in range(4)]),
}


class Graph:
    def __init__(self, order):
        self.order, self.steps, self.made = order, {}, {}

    def add(self, name, operand, step):
        self.steps[name] = (operand, step)

    def send(self, name, way, operand):
        axis, pairs = WAYS[way]
        self.add(name, operand, lambda array: lax.ppermute(array, axis, pairs))

    def get(self, name):
        if name not in self.made:
            operand, step = self.steps[name]
            waits = [self.get(other) for other in self.order.get(name, ())]
            array = operand()
            if waits:
                array = lax.optimization_barrier((array, *waits))[0]
            self.made[name] = step(array)
        return self.made[name]


def pack(*columns):
    return jnp.stack([jnp.concatenate([column[k] for column in columns]) for k in range(2)])


def both(array, first=0, lead=()):
    return [(array, (k,) + lead, first) for k in range(2)]


def is_inner():
    row = lax.axis_index("row")
    return (row == 1) | (row == 2)


def shared_steps(graph, groups, mine, other):
    inner = is_inner()
    get = graph.get
    first, names = 0, []

    def joined(arrays, axis):
        return arrays[0] if len(arrays) == 1 else jnp.concatenate(arrays, axis)

    for g, size in enumerate(groups):
        chunks = range(first, first + size)
        first += size

        def ready(k, g=g, chunks=chunks):
            return jnp.where(inner, joined([mine(n, k) for n in chunks], 0), get(f"o{g}")[k])

        graph.send(f"o{g}", "out", lambda chunks=chunks: joined([other(n) for n in chunks], 1))
        graph.send(f"b{g}", "x", lambda ready=ready: ready(1))
        graph.add(f"k{g}", lambda ready=ready: ready(0), lambda array: array)
    return [get(kind + str(g)) for kind in ("k", "b") for g in range(len(groups))]


def outgoing(parts):
    count = len(OUT_SIZES)
    graph = Graph(OUT_ORDER)
    get, send = graph.get, graph.send
    for n in range(count):
        send(f"x{n}", "x", lambda n=n: parts[2 * count + n])
    later = lambda n, side: parts[2 * n + side]
    right_of = lambda n: (later(n, 0), get(f"x{n}")[0])
    left_of = lambda n: (later(n, 1), get(f"x{n}")[1])
    first = parts
    zero = OUT_SIZES[0]
    send("i0", "in", lambda: first[0])
    send("a0", "across", lambda: first[0])
    send("i1", "in", lambda: jnp.concatenate([get("x0")[0], first[1]]))
    send("a1", "across", lambda: jnp.concatenate([get("x0")[0], get("i0")]))

    def come(n):
        array, skip = get(f"i{n + 1}"), zero // 2 if n == 1 else OUT_SIZES[n - 1]
        return (array[0, skip:], array[1, skip:])

    def halves(array):
        return (array[: zero // 2], array[zero // 2 :])

    def inward(n):
        before = halves(get("x0")[1]) if n == 1 else left_of(n - 1)
        return pack(before, right_of(n)) if n < count else pack(before)

    def across(n):
        before = halves(get("i1")[:zero]) if n == 1 else come(n - 1)
        return pack(before, right_of(n)) if n < count else pack(before)

    for n in range(1, count + 1):
        send(f"i{n + 1}", "in", lambda n=n: inward(n))
        send(f"a{n + 1}", "across", lambda n=n: across(n))

    def product(n, left):
        size = left.shape[-1]
        if n == 0:
            x_left = lambda array: array[:, : zero // 2].reshape((zero,) + array.shape[2:])
            operands = [
                [(left, (), 0), (get("x0"), (1,), 0)],
                [(get("i1"), (), zero), (x_left(get("i2")), (), 0)],
                [(first[0], (), 0), (get("x0"), (0,), 0)],
                [(get("i0"), (), 0), (get("i1"), (), 0)],
                [(get("a1"), (), zero), (x_left(get("a2")), (), 0)],
                [(get("a0"), (), 0), (get("a1"), (), 0)],
            ]
        else:
            skip = zero // 2 if n == 1 else OUT_SIZES[n - 1]
            operands = [
                [(left, (), 0), (get(f"x{n}"), (1,), 0)],
                both(get(f"i{n + 2}")),
                [(later(n, 0), (), 0), (get(f"x{n}"), (0,), 0)],
                both(get(f"i{n + 1}"), skip),
                both(get(f"a{n + 2}")),
                both(get(f"a{n + 1}"), skip),
            ]
        leads = ((), (), (2,), (2, 2))
        return product_call(outgoing_kernel, operands, left.shape[0], leads, (4, size, 2 * size), "outgoing")

    for n in range(count):
        graph.add(f"p{n}", lambda n=n: later(n, 1), functools.partial(product, n))
        send(f"c{n}", "core", lambda n=n: get(f"p{n}")[3])
    return shared_steps(
        graph,
        OUT_GROUPS,
        lambda n, k: get(f"p{n}")[k] + get(f"c{n}")[0, k],
        lambda n: get(f"p{n}")[2] + get(f"c{n}")[1],
    )


def incoming(parts):
    count = len(IN_SIZES)
    graph = Graph(IN_ORDER)
    get, send = graph.get, graph.send
    for n in range(count):
        send(f"x{n}", "x", lambda n=n: parts[count + n])
    send("i0", "in", lambda: parts[0])
    send("i0x", "in", lambda: get("x0"))
    send("cl0", "core", lambda: parts[0])
    send("clx", "core", lambda: get("x0"))
    send("cp0", "core", lambda: get("i0"))
    send("cpx", "core", lambda: get("i0x"))
    for n in range(1, count):
        graph.add(f"j{n}", lambda n=n: parts[n], lambda own, n=n: jnp.stack([own, get(f"x{n}")], 1))
        send(f"i{n}", "in", lambda n=n: get(f"j{n}"))
        send(f"cl{n}", "core", lambda n=n: get(f"j{n}")[0])
        send(f"cp{n}", "core", lambda n=n: get(f"i{n}")[0])

    def product(n, own):
        size = own.shape[-1]
        if n == 0:
            side = lambda name, name_x, slot: [
                (own if name is None else get(name), (slot,), 0),
                (get(name_x), (slot,), 0),
            ]
            operands = [side(None, "x0", 0), side("cl0", "clx", 0), side("i0", "i0x", 0), side("cp0", "cpx", 0)]
            operands += [side(None, "x0", 1), side("i0", "i0x", 1)]
        else:
            side = lambda array, slot: [(array, (slot, k), 0) for k in range(2)]
            operands = [side(own, 0), both(get(f"cl{n}")), side(get(f"i{n}"), 0), both(get(f"cp{n}"))]
            operands += [side(own, 1), side(get(f"i{n}"), 1)]
        leads = ((), (), (2,), (2, 2))
        return product_call(incoming_kernel, operands, IN_SIZES[n], leads, (4, 2 * size, size), "incoming")

    for n in range(count):
        graph.add(f"p{n}", lambda n=n: get(f"j{n}") if n else parts[0], functools.partial(product, n))
        send(f"a{n}", "across", lambda n=n: get(f"p{n}")[3])
    return shared_steps(
        graph,
        IN_GROUPS,
        lambda n, k: get(f"p{n}")[k] + get(f"a{n}")[1, k],
        lambda n: get(f"p{n}")[2] + get(f"a{n}")[0],
    )


def four_by_four(pair, chain, block_mask, w_in, w_gate, w_out, gain_in, gain_out):
    gain_wide = jnp.broadcast_to(gain_out[:, :, None, None], gain_out.shape + (1, pair.shape[1]))
    gate, parts = first_call(chain, block_mask, pair, w_in, w_gate, gain_in)
    products = outgoing(parts)
    middle, gate, parts = middle_call(
        chain, block_mask, pair, gate, products, w_out, gain_wide[0], w_in, w_gate, gain_in
    )
    products = incoming(parts)
    return finish_call(middle, gate, products, w_out, gain_wide[1])


def solution(mesh):
    four = mesh.shape["row"] == 4 and mesh.shape["col"] == 4
    return jax.shard_map(
        four_by_four if four else any_mesh,
        mesh=mesh,
        in_specs=(
            P(("group", "row"), "col", None),
            P("group"),
            P("group", None),
            P(),
            P(),
            P(),
            P(),
            P(),
        ),
        out_specs=P(("group", "row"), "col", None),
        check_vma=False,
    )
```

```python
import functools

import jax
import jax.numpy as jnp
from jax import lax
from jax.experimental import pallas as pl
from jax.experimental.pallas import tpu as pltpu
from jax.sharding import PartitionSpec as P

BLOCK = 128
EPS = 1e-05
OUT_SIZES = (8, 8, 8, 4, 4)
IN_SIZES = (8, 8, 8, 4, 4)
OUT_GROUPS = (1, 1, 1, 1, 1)
IN_GROUPS = (1, 1, 1, 1, 1)
OUT_ORDER = {'i1': ('i0',), 'i2': ('i1',), 'i3': ('i2',), 'i4': ('i3',), 'i5': ('i4',), 'i6': ('i5',), 'a1': ('a0',), 'a2': ('a1',), 'a3': ('a2',), 'a4': ('a3',), 'a5': ('a4', 'p1'), 'a6': ('a5',), 'x2': ('x1', 'a1'), 'x3': ('x2',), 'x4': ('x3',), 'o2': ('o1',), 'x1': ('a0',), 'p2': ('o0',), 'p3': ('o1',), 'p4': ('o2',)}
IN_ORDER = {'i0x': ('i0',), 'i3': ('i2',), 'i4': ('i3',), 'a1': ('a0', 'i1'), 'a3': ('a2',), 'o2': ('o1',), 'o3': ('o2',), 'o4': ('o3',), 'x1': ('i0',), 'x2': ('i0x',), 'c4': ('c3',)}
STEP = 16
TOLD = 0.05
FIRST_VMEM = 61 * 1024 * 1024
VMEM = 28 * 1024 * 1024
PRODUCT_VMEM = 10 * 1024 * 1024


def broadcast(block, axis, owner):
    block = jnp.where(lax.axis_index(axis) == owner, block, jnp.zeros_like(block))
    return lax.psum(block, axis)


def layer_norm(values, gain):
    mean = jnp.mean(values, -1, keepdims=True)
    centred = values - mean
    spread = jnp.mean(centred * centred, -1, keepdims=True)
    return centred * lax.rsqrt(spread + EPS) * gain


def project(pair, tile_mask, w_in, w_gate, gain_in):
    normed = layer_norm(pair.astype(jnp.float32), gain_in).astype(jnp.bfloat16)
    hidden = jnp.dot(normed, w_in, preferred_element_type=jnp.float32)
    width = w_in.shape[1] // 4
    masked = tile_mask[..., None]
    left = (masked * jax.nn.sigmoid(hidden[..., width : 2 * width]) * hidden[..., :width]).astype(
        jnp.bfloat16
    )
    right = (
        masked * jax.nn.sigmoid(hidden[..., 3 * width :]) * hidden[..., 2 * width : 3 * width]
    ).astype(jnp.bfloat16)
    gate = jax.nn.sigmoid(jnp.dot(normed, w_gate, preferred_element_type=jnp.float32))
    return (left, right, gate)


def finish(pair, product, gate, w_out, gain_out):
    update = layer_norm(product, gain_out).astype(jnp.bfloat16)
    return (
        pair.astype(jnp.float32) + gate * jnp.dot(update, w_out, preferred_element_type=jnp.float32)
    ).astype(jnp.bfloat16)


def any_mesh(pair, chain, block_mask, w_in, w_gate, w_out, gain_in, gain_out):
    tile_rows = pair.shape[0]
    tile_cols = pair.shape[1]
    block_count = chain.shape[0]
    ratio = lax.axis_size("row") // lax.axis_size("col")
    row_index = lax.axis_index("row")
    col_index = lax.axis_index("col")
    same = chain[:, None] == chain[None, :]
    blocks = jnp.where(same | (block_mask == 1), 1.0, 0.0).astype(jnp.float32)
    labels = jnp.arange(block_count, dtype=jnp.int32)
    row_blocks = (row_index * tile_rows + jnp.arange(tile_rows, dtype=jnp.int32)) // BLOCK
    col_blocks = (col_index * tile_cols + jnp.arange(tile_cols, dtype=jnp.int32)) // BLOCK
    row_onehot = jnp.where(row_blocks[:, None] == labels[None, :], 1.0, 0.0).astype(jnp.float32)
    col_onehot = jnp.where(col_blocks[:, None] == labels[None, :], 1.0, 0.0).astype(jnp.float32)
    tile_mask = jnp.dot(jnp.dot(row_onehot, blocks), col_onehot.T)
    left, right, gate = project(pair, tile_mask, w_in[0], w_gate[0], gain_in[0])
    partial_terms = jnp.einsum(
        "ikc,jkc->ijc",
        left,
        lax.all_gather(right, "row", axis=0, tiled=True),
        preferred_element_type=jnp.float32,
    )
    product = lax.psum_scatter(
        partial_terms.astype(jnp.bfloat16), "col", scatter_dimension=1, tiled=True
    ).astype(jnp.float32)
    middle = finish(pair, product, gate, w_out[0], gain_out[0])
    left, right, gate = project(middle, tile_mask, w_in[1], w_gate[1], gain_in[1])
    left_cols = lax.all_gather(left, "row", axis=0, tiled=True)
    start_col = row_index % ratio * tile_rows
    left_slice = lax.dynamic_slice_in_dim(left_cols, start_col, tile_rows, 1)
    left_mine = broadcast(left_slice, "col", row_index // ratio)
    product = jnp.einsum(
        "kic,kjc->ijc",
        left_mine,
        lax.all_gather(right, "row", axis=0, tiled=True),
        preferred_element_type=jnp.float32,
    )
    return finish(middle, product, gate, w_out[1], gain_out[1])


NN = (((1,), (0,)), ((), ()))
NT = (((1,), (1,)), ((), ()))
TN = (((0,), (0,)), ((), ()))
SMEM_SPEC = pl.BlockSpec(memory_space=pltpu.SMEM)


def dot(a, b, dims=NN):
    return lax.dot_general(a, b, dims, preferred_element_type=jnp.float32)


def norm_rows(rows, gain):
    channels = rows.shape[-1]
    place = lax.broadcasted_iota(jnp.int32, (channels, channels), 0)
    same = place == lax.broadcasted_iota(jnp.int32, (channels, channels), 1)
    centre = jnp.where(same, 1.0 - 1.0 / channels, -1.0 / channels).astype(jnp.bfloat16)
    mean_of = jnp.full((channels, channels), 1.0 / channels, jnp.bfloat16)
    centred = dot(rows, centre)
    spread = dot((centred * centred).astype(jnp.bfloat16), mean_of)
    return (centred * lax.rsqrt(spread + EPS) * gain).astype(jnp.bfloat16)


def tile_mask(chain_ref, block_mask_ref):
    row, col = lax.axis_index("row"), lax.axis_index("col")
    seen = (chain_ref[row] == chain_ref[col]) | (block_mask_ref[row, col] == 1)
    return jnp.where(seen, 1.0, 0.0).astype(jnp.float32)


def pick_weights(w_ref, w_gate_ref, mask, turned, picked, picked_gate):
    @pl.when(pl.program_id(0) == 0)
    def _():
        turned[...] = w_ref[0].astype(jnp.float32).T
        half = turned.shape[0] // 8
        x = lax.axis_index("col") // 2
        rows = []
        for kind in range(4):
            for other in (x, 1 - x):
                some = turned[pl.ds(pl.multiple_of((2 * kind + other) * half, 8), half), :]
                rows.append(some * (0.5 if kind % 2 else 0.5 * mask))
        picked[...] = jnp.concatenate(rows, 0).astype(jnp.bfloat16)
        picked_gate[...] = (w_gate_ref[0].astype(jnp.float32) * 0.5).astype(jnp.bfloat16)


def project_part(normed, picked, scratch, sides, sizes):
    hidden = dot(picked[...], normed, NT)
    width = picked.shape[0] // 4
    cols = normed.shape[0] // STEP
    for side, refs in enumerate(sides):
        values = hidden[2 * side * width : (2 * side + 1) * width]
        gates = hidden[(2 * side + 1) * width : (2 * side + 2) * width]
        kept = (jnp.tanh(gates) + 1.0) * values
        for row in range(STEP):
            scratch[side, pl.ds(row, width, stride=STEP), :] = kept[:, row * cols : (row + 1) * cols]
        done = 0
        for ref, size in zip(refs, sizes * 2):
            rows = scratch[side, done * STEP : (done + size) * STEP, :]
            ref[...] = rows.astype(jnp.bfloat16).reshape(ref.shape)
            done += size


def split_sides(outs, count, apart):
    lefts, rights = [], []
    for n in range(count):
        if apart:
            rights.append(outs[2 * n])
            lefts.append(outs[2 * n + 1])
        else:
            lefts.append(outs[n].at[0])
            rights.append(outs[n].at[1])
    for ref in outs[-count:]:
        lefts.append(ref.at[1 if apart else 0])
        rights.append(ref.at[0 if apart else 1])
    return lefts, rights


def project_all(rows, gain, gate_ref, picked, picked_gate, scratch, outs, sizes, apart):
    normed = norm_rows(rows, gain)
    project_part(normed, picked, scratch, split_sides(outs, len(sizes), apart), sizes)
    gate = 0.5 * jnp.tanh(dot(normed, picked_gate[...])) + 0.5
    gate_ref[...] = gate.astype(gate_ref.dtype).reshape(gate_ref.shape)


def first_kernel(sizes, chain_ref, block_mask_ref, pair_ref, w_ref, w_gate_ref, gain_ref, gate_ref, *rest):
    *outs, turned, picked, picked_gate, scratch = rest
    pick_weights(w_ref, w_gate_ref, tile_mask(chain_ref, block_mask_ref), turned, picked, picked_gate)
    rows = pair_ref[...].reshape(-1, pair_ref.shape[-1])
    project_all(rows, gain_ref[0:1], gate_ref, picked, picked_gate, scratch, outs, sizes, True)


def finish_rows(pair_ref, gate_ref, product_refs, w_out_ref, gain_ref, scratch, twice, out_ref):
    width = w_out_ref.shape[1]
    half = width // 2
    cols = pair_ref.shape[1]
    x = lax.axis_index("col") // 2
    mine, others = pl.multiple_of(x * half, half), pl.multiple_of((1 - x) * half, half)

    @pl.when(pl.program_id(0) == 0)
    def _():
        w_out = jnp.concatenate([w_out_ref[0, pl.ds(mine, half)], w_out_ref[0, pl.ds(others, half)]], 0)
        none = jnp.zeros_like(w_out)
        twice[...] = jnp.concatenate(
            [jnp.concatenate([w_out, none], 1), jnp.concatenate([none, w_out], 1)], 0
        )

    gain = jnp.concatenate([gain_ref[pl.ds(mine, half)], gain_ref[pl.ds(others, half)]], 0)
    product = jnp.concatenate([ref[...] for ref in product_refs], 0).astype(jnp.float32)
    mean = jnp.sum(product, 0, keepdims=True) * (1.0 / width)
    centred = product - mean
    spread = jnp.sum(centred * centred, 0, keepdims=True) * (1.0 / width)
    update = centred * lax.rsqrt(spread + EPS) * gain
    scratch[...] = update.reshape(width * STEP, cols)
    for row in range(0, STEP, 2):
        two = jnp.concatenate(
            [scratch[pl.ds(row, width, stride=STEP), :], scratch[pl.ds(row + 1, width, stride=STEP), :]], 0
        )
        changes = dot(two.astype(jnp.bfloat16), twice[...], TN)
        for k in range(2):
            change = changes[:, k * pair_ref.shape[2] : (k + 1) * pair_ref.shape[2]]
            gate = gate_ref[row + k].astype(jnp.float32)
            old = pair_ref[row + k].astype(jnp.float32)
            out_ref[row + k] = (old + gate * change).astype(jnp.bfloat16)


def finish_kernel(pair_ref, gate_ref, w_out_ref, gain_ref, *rest):
    *product_refs, out_ref, scratch, twice = rest
    finish_rows(pair_ref, gate_ref, product_refs, w_out_ref, gain_ref, scratch, twice, out_ref)


def middle_kernel(
    sizes,
    count,
    chain_ref,
    block_mask_ref,
    pair_ref,
    gate_ref,
    w_out_ref,
    gain_out_ref,
    w_ref,
    w_gate_ref,
    gain_in_ref,
    *rest,
):
    product_refs, (out_ref, next_ref, *outs) = rest[:count], rest[count:]
    *outs, update, twice, turned, picked, picked_gate, scratch = outs
    pick_weights(w_ref, w_gate_ref, tile_mask(chain_ref, block_mask_ref), turned, picked, picked_gate)
    finish_rows(pair_ref, gate_ref, product_refs, w_out_ref, gain_out_ref, update, twice, out_ref)
    rows = out_ref[...].reshape(-1, out_ref.shape[-1])
    project_all(rows, gain_in_ref[1:2], next_ref, picked, picked_gate, scratch, outs, sizes, False)


def outgoing_kernel(left, left_pair, right, right_pair, right_far, right_near, outs, rights):
    *kept, pair, sent = outs
    for k, blocks in enumerate((right, right_pair, right_far, right_near)):
        rights[k] = jnp.concatenate(blocks, 1)
    lefts = jnp.concatenate([jnp.concatenate(left, 1), jnp.concatenate(left_pair, 1)], 0)
    size = lefts.shape[0] // 2
    here = lax.axis_index("row") ^ lax.axis_index("col")
    for place in range(4):
        terms = dot(lefts, rights[here ^ place], NT).astype(jnp.bfloat16)
        if place % 2:
            sent[0, place // 2, 0] = terms[:size]
            sent[1, place // 2, 0] = terms[size:]
        else:
            kept[place // 2][0] = terms[:size]
            pair[place // 2, 0] = terms[size:]


def incoming_kernel(left, left_core, left_pair, left_pair_core, right, right_pair, outs, lefts):
    *kept, pair, cross = outs
    for k in range(2):
        lefts[2 * k] = jnp.concatenate([left[k], left_pair[k]], 0)
        lefts[2 * k + 1] = jnp.concatenate([left_core[k], left_pair_core[k]], 0)
    rights = jnp.concatenate([jnp.concatenate(right, 1), jnp.concatenate(right_pair, 1)], 0)
    size = rights.shape[1] // 2
    here = lax.axis_index("row") ^ lax.axis_index("col")
    for place in range(4):
        terms = dot(lefts[here ^ place], rights, TN).astype(jnp.bfloat16)
        for k in range(2):
            block = terms[:, k * size : (k + 1) * size]
            if place == 0:
                kept[k][0] = block
            else:
                (pair, cross.at[0], cross.at[1])[place - 1][k, 0] = block


def pieces_kernel(kernel, count, *refs):
    blocks = [ref[(0,) * (len(ref.shape) - 2)] for ref in refs[:count]]
    kernel(*[blocks[k : k + 2] for k in range(0, count, 2)], refs[count:-1], refs[-1])


def params(limit=VMEM):
    return pltpu.CompilerParams(
        vmem_limit_bytes=limit, dimension_semantics=("arbitrary",), fuse_transposed_lhs_in_matmul=True
    )


def part(array, index):
    return pl.BlockSpec((1,) + array.shape[1:], lambda *_: (index,) + (0,) * (array.ndim - 1))


def whole(array):
    return pl.BlockSpec(array.shape, lambda *_: (0,) * array.ndim)


def tile_spec(tile):
    return pl.BlockSpec((STEP,) + tile.shape[1:], lambda r: (r, 0, 0))


def chunk_spec(shape):
    lead = shape[:-2]
    return pl.BlockSpec(lead + (STEP, shape[-1]), lambda r: (0,) * len(lead) + (r, 0))


def cost(flops, nbytes, special=0):
    return pl.CostEstimate(
        flops=int(flops * TOLD), bytes_accessed=int(nbytes * TOLD), transcendentals=int(special * TOLD)
    )


def part_outs(pair, sizes, apart):
    tile = pair.shape[:2]
    own = [(size,) + tile for size in sizes]
    both_sides = [(2,) + shape for shape in own]
    shapes = ([shape for shape in own for _ in range(2)] if apart else both_sides) + both_sides
    return [jax.ShapeDtypeStruct(shape, jnp.bfloat16) for shape in shapes], [chunk_spec(shape) for shape in shapes]


def part_scratch(pair, w_in, sizes):
    width = 2 * sum(sizes)
    return [
        pltpu.VMEM((w_in.shape[2], w_in.shape[1]), jnp.float32),
        pltpu.VMEM((4 * width, w_in.shape[1]), jnp.bfloat16),
        pltpu.VMEM((w_in.shape[1], w_in.shape[1]), jnp.bfloat16),
        pltpu.VMEM((2, width * STEP, pair.shape[1]), jnp.float32),
    ]


def finish_scratch(pair, w_out):
    return [
        pltpu.VMEM((w_out.shape[1] * STEP, pair.shape[1]), jnp.float32),
        pltpu.VMEM((2 * w_out.shape[1], 2 * w_out.shape[2]), jnp.bfloat16),
    ]


def first_call(chain, block_mask, pair, w_in, w_gate, gain_in):
    outs, specs = part_outs(pair, OUT_SIZES, True)
    gate, *result = pl.pallas_call(
        functools.partial(first_kernel, OUT_SIZES),
        grid=(pair.shape[0] // STEP,),
        in_specs=[SMEM_SPEC, SMEM_SPEC, tile_spec(pair), part(w_in, 0), part(w_gate, 0), whole(gain_in)],
        out_specs=[tile_spec(pair)] + specs,
        out_shape=[jax.ShapeDtypeStruct(pair.shape, pair.dtype)] + outs,
        scratch_shapes=part_scratch(pair, w_in, OUT_SIZES),
        compiler_params=params(FIRST_VMEM),
        cost_estimate=cost(2e9, 8 << 20, 4 << 20),
        name="project",
    )(chain, block_mask, pair, w_in, w_gate, gain_in)
    return gate, result


def finish_call(pair, gate, products, w_out, gain_wide):
    return pl.pallas_call(
        finish_kernel,
        grid=(pair.shape[0] // STEP,),
        in_specs=[tile_spec(pair), tile_spec(gate), part(w_out, 1), whole(gain_wide)]
        + [chunk_spec(p.shape) for p in products],
        out_specs=tile_spec(pair),
        out_shape=jax.ShapeDtypeStruct(pair.shape, pair.dtype),
        scratch_shapes=finish_scratch(pair, w_out),
        compiler_params=params(),
        cost_estimate=cost(1e9, 14 << 20, 4 << 20),
        name="finish",
    )(pair, gate, w_out, gain_wide, *products)


def middle_call(chain, block_mask, pair, gate, products, w_out, gain_wide, w_in, w_gate, gain_in):
    outs, specs = part_outs(pair, IN_SIZES, False)
    middle, gate, *result = pl.pallas_call(
        functools.partial(middle_kernel, IN_SIZES, len(products)),
        grid=(pair.shape[0] // STEP,),
        in_specs=[SMEM_SPEC, SMEM_SPEC, tile_spec(pair), tile_spec(gate), part(w_out, 0)]
        + [whole(gain_wide), part(w_in, 1), part(w_gate, 1), whole(gain_in)]
        + [chunk_spec(p.shape) for p in products],
        out_specs=[tile_spec(pair)] * 2 + specs,
        out_shape=[jax.ShapeDtypeStruct(pair.shape, pair.dtype)] * 2 + outs,
        scratch_shapes=finish_scratch(pair, w_out) + part_scratch(pair, w_in, IN_SIZES),
        compiler_params=params(),
        cost_estimate=cost(3e9, 18 << 20, 8 << 20),
        name="middle",
    )(chain, block_mask, pair, gate, w_out, gain_wide, w_in, w_gate, gain_in, *products)
    return middle, gate, result


def product_call(kernel, operands, channels, leads, scratch, name):
    pieces = [piece for operand in operands for piece in operand]
    size = pieces[0][0].shape[-1]

    def piece_spec(array, lead, first):
        return pl.BlockSpec((1,) * (len(lead) + 1) + (size, size), lambda c: lead + (first + c, 0, 0))

    def out_spec(lead):
        return pl.BlockSpec(lead + (1, size, size), lambda c: (0,) * len(lead) + (c, 0, 0))

    return pl.pallas_call(
        functools.partial(pieces_kernel, kernel, len(pieces)),
        grid=(channels,),
        in_specs=[piece_spec(*piece) for piece in pieces],
        out_specs=[out_spec(lead) for lead in leads],
        out_shape=[jax.ShapeDtypeStruct(lead + (channels, size, size), jnp.bfloat16) for lead in leads],
        scratch_shapes=[pltpu.VMEM(scratch, jnp.bfloat16)],
        compiler_params=params(PRODUCT_VMEM),
        cost_estimate=cost(channels * 2 * (4 * size) ** 2 * size, channels * size * size * 2 * 20),
        name=name,
    )(*[piece[0] for piece in pieces])


WAYS = {
    "in": ("row", [(0, 1), (3, 2)]),
    "across": ("row", [(1, 2), (2, 1)]),
    "out": ("row", [(1, 0), (2, 3)]),
    "x": ("col", [(c, c ^ 2) for c in range(4)]),
    "core": ("col", [(c, c ^ 1) for c in range(4)]),
}


class Graph:
    def __init__(self, order):
        self.order, self.steps, self.made = order, {}, {}

    def add(self, name, operand, step):
        self.steps[name] = (operand, step)

    def send(self, name, way, operand):
        axis, pairs = WAYS[way]
        self.add(name, operand, lambda array: lax.ppermute(array, axis, pairs))

    def get(self, name):
        if name not in self.made:
            operand, step = self.steps[name]
            waits = [self.get(other) for other in self.order.get(name, ())]
            array = operand()
            if waits:
                array = lax.optimization_barrier((array, *waits))[0]
            self.made[name] = step(array)
        return self.made[name]


def pack(*columns):
    return jnp.stack([jnp.concatenate([column[k] for column in columns]) for k in range(2)])


def both(array, first=0, lead=()):
    return [(array, (k,) + lead, first) for k in range(2)]


def is_inner():
    row = lax.axis_index("row")
    return (row == 1) | (row == 2)


def shared_steps(graph, groups, mine, other):
    inner = is_inner()
    get = graph.get
    first, names = 0, []

    def joined(arrays, axis):
        return arrays[0] if len(arrays) == 1 else jnp.concatenate(arrays, axis)

    for g, size in enumerate(groups):
        chunks = range(first, first + size)
        first += size

        def ready(k, g=g, chunks=chunks):
            return jnp.where(inner, joined([mine(n, k) for n in chunks], 0), get(f"o{g}")[k])

        graph.send(f"o{g}", "out", lambda chunks=chunks: joined([other(n) for n in chunks], 1))
        graph.send(f"b{g}", "x", lambda ready=ready: ready(1))
        graph.add(f"k{g}", lambda ready=ready: ready(0), lambda array: array)
    return [get(kind + str(g)) for kind in ("k", "b") for g in range(len(groups))]


def outgoing(parts):
    count = len(OUT_SIZES)
    graph = Graph(OUT_ORDER)
    get, send = graph.get, graph.send
    for n in range(count):
        send(f"x{n}", "x", lambda n=n: parts[2 * count + n])
    later = lambda n, side: parts[2 * n + side]
    right_of = lambda n: (later(n, 0), get(f"x{n}")[0])
    left_of = lambda n: (later(n, 1), get(f"x{n}")[1])
    first = parts
    zero = OUT_SIZES[0]
    send("i0", "in", lambda: first[0])
    send("a0", "across", lambda: first[0])
    send("i1", "in", lambda: jnp.concatenate([get("x0")[0], first[1]]))
    send("a1", "across", lambda: jnp.concatenate([get("x0")[0], get("i0")]))

    def come(n):
        array, skip = get(f"i{n + 1}"), zero // 2 if n == 1 else OUT_SIZES[n - 1]
        return (array[0, skip:], array[1, skip:])

    def halves(array):
        return (array[: zero // 2], array[zero // 2 :])

    def inward(n):
        before = halves(get("x0")[1]) if n == 1 else left_of(n - 1)
        return pack(before, right_of(n)) if n < count else pack(before)

    def across(n):
        before = halves(get("i1")[:zero]) if n == 1 else come(n - 1)
        return pack(before, right_of(n)) if n < count else pack(before)

    for n in range(1, count + 1):
        send(f"i{n + 1}", "in", lambda n=n: inward(n))
        send(f"a{n + 1}", "across", lambda n=n: across(n))

    def product(n, left):
        size = left.shape[-1]
        if n == 0:
            x_left = lambda array: array[:, : zero // 2].reshape((zero,) + array.shape[2:])
            operands = [
                [(left, (), 0), (get("x0"), (1,), 0)],
                [(get("i1"), (), zero), (x_left(get("i2")), (), 0)],
                [(first[0], (), 0), (get("x0"), (0,), 0)],
                [(get("i0"), (), 0), (get("i1"), (), 0)],
                [(get("a1"), (), zero), (x_left(get("a2")), (), 0)],
                [(get("a0"), (), 0), (get("a1"), (), 0)],
            ]
        else:
            skip = zero // 2 if n == 1 else OUT_SIZES[n - 1]
            operands = [
                [(left, (), 0), (get(f"x{n}"), (1,), 0)],
                both(get(f"i{n + 2}")),
                [(later(n, 0), (), 0), (get(f"x{n}"), (0,), 0)],
                both(get(f"i{n + 1}"), skip),
                both(get(f"a{n + 2}")),
                both(get(f"a{n + 1}"), skip),
            ]
        leads = ((), (), (2,), (2, 2))
        return product_call(outgoing_kernel, operands, left.shape[0], leads, (4, size, 2 * size), "outgoing")

    for n in range(count):
        graph.add(f"p{n}", lambda n=n: later(n, 1), functools.partial(product, n))
        send(f"c{n}", "core", lambda n=n: get(f"p{n}")[3])
    return shared_steps(
        graph,
        OUT_GROUPS,
        lambda n, k: get(f"p{n}")[k] + get(f"c{n}")[0, k],
        lambda n: get(f"p{n}")[2] + get(f"c{n}")[1],
    )


def incoming(parts):
    count = len(IN_SIZES)
    graph = Graph(IN_ORDER)
    get, send = graph.get, graph.send
    for n in range(count):
        send(f"x{n}", "x", lambda n=n: parts[count + n])
    send("i0", "in", lambda: parts[0])
    send("i0x", "in", lambda: get("x0"))
    send("cl0", "core", lambda: parts[0])
    send("clx", "core", lambda: get("x0"))
    send("cp0", "core", lambda: get("i0"))
    send("cpx", "core", lambda: get("i0x"))
    for n in range(1, count):
        graph.add(f"j{n}", lambda n=n: parts[n], lambda own, n=n: jnp.stack([own, get(f"x{n}")], 1))
        send(f"i{n}", "in", lambda n=n: get(f"j{n}"))
        send(f"cl{n}", "core", lambda n=n: get(f"j{n}")[0])
        send(f"cp{n}", "core", lambda n=n: get(f"i{n}")[0])

    def product(n, own):
        size = own.shape[-1]
        if n == 0:
            side = lambda name, name_x, slot: [
                (own if name is None else get(name), (slot,), 0),
                (get(name_x), (slot,), 0),
            ]
            operands = [side(None, "x0", 0), side("cl0", "clx", 0), side("i0", "i0x", 0), side("cp0", "cpx", 0)]
            operands += [side(None, "x0", 1), side("i0", "i0x", 1)]
        else:
            side = lambda array, slot: [(array, (slot, k), 0) for k in range(2)]
            operands = [side(own, 0), both(get(f"cl{n}")), side(get(f"i{n}"), 0), both(get(f"cp{n}"))]
            operands += [side(own, 1), side(get(f"i{n}"), 1)]
        leads = ((), (), (2,), (2, 2))
        return product_call(incoming_kernel, operands, IN_SIZES[n], leads, (4, 2 * size, size), "incoming")

    for n in range(count):
        graph.add(f"p{n}", lambda n=n: get(f"j{n}") if n else parts[0], functools.partial(product, n))
        send(f"a{n}", "across", lambda n=n: get(f"p{n}")[3])
    return shared_steps(
        graph,
        IN_GROUPS,
        lambda n, k: get(f"p{n}")[k] + get(f"a{n}")[1, k],
        lambda n: get(f"p{n}")[2] + get(f"a{n}")[0],
    )


def four_by_four(pair, chain, block_mask, w_in, w_gate, w_out, gain_in, gain_out):
    gain_wide = jnp.broadcast_to(gain_out[:, :, None, None], gain_out.shape + (1, pair.shape[1]))
    gate, parts = first_call(chain, block_mask, pair, w_in, w_gate, gain_in)
    products = outgoing(parts)
    middle, gate, parts = middle_call(
        chain, block_mask, pair, gate, products, w_out, gain_wide[0], w_in, w_gate, gain_in
    )
    products = incoming(parts)
    return finish_call(middle, gate, products, w_out, gain_wide[1])


def solution(mesh):
    four = mesh.shape["row"] == 4 and mesh.shape["col"] == 4
    return jax.shard_map(
        four_by_four if four else any_mesh,
        mesh=mesh,
        in_specs=(
            P(("group", "row"), "col", None),
            P("group"),
            P("group", None),
            P(),
            P(),
            P(),
            P(),
            P(),
        ),
        out_specs=P(("group", "row"), "col", None),
        check_vma=False,
    )
```

```python
import functools

import jax
import jax.numpy as jnp
from jax import lax
from jax.experimental import pallas as pl
from jax.experimental.pallas import tpu as pltpu
from jax.sharding import PartitionSpec as P

BLOCK = 128
EPS = 1e-05
OUT_SIZES = (8, 8, 8, 4, 4)
IN_SIZES = (8, 8, 8, 4, 4)
OUT_GROUPS = (1, 1, 1, 1, 1)
IN_GROUPS = (1, 1, 1, 1, 1)
OUT_ORDER = {'i1': ('i0',), 'i2': ('i1',), 'i3': ('i2',), 'i4': ('i3',), 'i5': ('i4',), 'i6': ('i5',), 'a1': ('a0',), 'a2': ('a1',), 'a3': ('a2',), 'a4': ('a3',), 'a5': ('a4', 'p1'), 'a6': ('a5',), 'x2': ('x1', 'a1'), 'x3': ('x2',), 'x4': ('x3',), 'o2': ('o1',), 'x1': ('a0',), 'p2': ('o0',), 'p3': ('o1',), 'p4': ('o2',)}
IN_ORDER = {'i0x': ('i0',), 'i3': ('i2',), 'i4': ('i3',), 'a1': ('a0', 'i1'), 'a3': ('a2',), 'o2': ('o1',), 'o3': ('o2',), 'o4': ('o3',), 'x1': ('i0',), 'x2': ('i0x',), 'c4': ('c3',)}
STEP = 16
TOLD = 0.05
TOGETHER = 2
FIRST_VMEM = 61 * 1024 * 1024
VMEM = 28 * 1024 * 1024
PRODUCT_VMEM = 10 * 1024 * 1024


def broadcast(block, axis, owner):
    block = jnp.where(lax.axis_index(axis) == owner, block, jnp.zeros_like(block))
    return lax.psum(block, axis)


def layer_norm(values, gain):
    mean = jnp.mean(values, -1, keepdims=True)
    centred = values - mean
    spread = jnp.mean(centred * centred, -1, keepdims=True)
    return centred * lax.rsqrt(spread + EPS) * gain


def project(pair, tile_mask, w_in, w_gate, gain_in):
    normed = layer_norm(pair.astype(jnp.float32), gain_in).astype(jnp.bfloat16)
    hidden = jnp.dot(normed, w_in, preferred_element_type=jnp.float32)
    width = w_in.shape[1] // 4
    masked = tile_mask[..., None]
    left = (masked * jax.nn.sigmoid(hidden[..., width : 2 * width]) * hidden[..., :width]).astype(
        jnp.bfloat16
    )
    right = (
        masked * jax.nn.sigmoid(hidden[..., 3 * width :]) * hidden[..., 2 * width : 3 * width]
    ).astype(jnp.bfloat16)
    gate = jax.nn.sigmoid(jnp.dot(normed, w_gate, preferred_element_type=jnp.float32))
    return (left, right, gate)


def finish(pair, product, gate, w_out, gain_out):
    update = layer_norm(product, gain_out).astype(jnp.bfloat16)
    return (
        pair.astype(jnp.float32) + gate * jnp.dot(update, w_out, preferred_element_type=jnp.float32)
    ).astype(jnp.bfloat16)


def any_mesh(pair, chain, block_mask, w_in, w_gate, w_out, gain_in, gain_out):
    tile_rows = pair.shape[0]
    tile_cols = pair.shape[1]
    block_count = chain.shape[0]
    ratio = lax.axis_size("row") // lax.axis_size("col")
    row_index = lax.axis_index("row")
    col_index = lax.axis_index("col")
    same = chain[:, None] == chain[None, :]
    blocks = jnp.where(same | (block_mask == 1), 1.0, 0.0).astype(jnp.float32)
    labels = jnp.arange(block_count, dtype=jnp.int32)
    row_blocks = (row_index * tile_rows + jnp.arange(tile_rows, dtype=jnp.int32)) // BLOCK
    col_blocks = (col_index * tile_cols + jnp.arange(tile_cols, dtype=jnp.int32)) // BLOCK
    row_onehot = jnp.where(row_blocks[:, None] == labels[None, :], 1.0, 0.0).astype(jnp.float32)
    col_onehot = jnp.where(col_blocks[:, None] == labels[None, :], 1.0, 0.0).astype(jnp.float32)
    tile_mask = jnp.dot(jnp.dot(row_onehot, blocks), col_onehot.T)
    left, right, gate = project(pair, tile_mask, w_in[0], w_gate[0], gain_in[0])
    partial_terms = jnp.einsum(
        "ikc,jkc->ijc",
        left,
        lax.all_gather(right, "row", axis=0, tiled=True),
        preferred_element_type=jnp.float32,
    )
    product = lax.psum_scatter(
        partial_terms.astype(jnp.bfloat16), "col", scatter_dimension=1, tiled=True
    ).astype(jnp.float32)
    middle = finish(pair, product, gate, w_out[0], gain_out[0])
    left, right, gate = project(middle, tile_mask, w_in[1], w_gate[1], gain_in[1])
    left_cols = lax.all_gather(left, "row", axis=0, tiled=True)
    start_col = row_index % ratio * tile_rows
    left_slice = lax.dynamic_slice_in_dim(left_cols, start_col, tile_rows, 1)
    left_mine = broadcast(left_slice, "col", row_index // ratio)
    product = jnp.einsum(
        "kic,kjc->ijc",
        left_mine,
        lax.all_gather(right, "row", axis=0, tiled=True),
        preferred_element_type=jnp.float32,
    )
    return finish(middle, product, gate, w_out[1], gain_out[1])


NN = (((1,), (0,)), ((), ()))
NT = (((1,), (1,)), ((), ()))
TN = (((0,), (0,)), ((), ()))
SMEM_SPEC = pl.BlockSpec(memory_space=pltpu.SMEM)


def dot(a, b, dims=NN):
    return lax.dot_general(a, b, dims, preferred_element_type=jnp.float32)


def norm_rows(rows, gain):
    channels = rows.shape[-1]
    place = lax.broadcasted_iota(jnp.int32, (channels, channels), 0)
    same = place == lax.broadcasted_iota(jnp.int32, (channels, channels), 1)
    centre = jnp.where(same, 1.0 - 1.0 / channels, -1.0 / channels).astype(jnp.bfloat16)
    mean_of = jnp.full((channels, channels), 1.0 / channels, jnp.bfloat16)
    centred = dot(rows, centre)
    spread = dot((centred * centred).astype(jnp.bfloat16), mean_of)
    return (centred * lax.rsqrt(spread + EPS) * gain).astype(jnp.bfloat16)


def tile_mask(chain_ref, block_mask_ref):
    row, col = lax.axis_index("row"), lax.axis_index("col")
    seen = (chain_ref[row] == chain_ref[col]) | (block_mask_ref[row, col] == 1)
    return jnp.where(seen, 1.0, 0.0).astype(jnp.float32)


def pick_weights(w_ref, w_gate_ref, mask, turned, picked, picked_gate):
    @pl.when(pl.program_id(0) == 0)
    def _():
        turned[...] = w_ref[0].astype(jnp.float32).T
        half = turned.shape[0] // 8
        x = lax.axis_index("col") // 2
        rows = []
        for kind in range(4):
            for other in (x, 1 - x):
                some = turned[pl.ds(pl.multiple_of((2 * kind + other) * half, 8), half), :]
                rows.append(some * (0.5 if kind % 2 else 0.5 * mask))
        picked[...] = jnp.concatenate(rows, 0).astype(jnp.bfloat16)
        picked_gate[...] = (w_gate_ref[0].astype(jnp.float32) * 0.5).astype(jnp.bfloat16)


def project_part(normed, picked, scratch, sides, sizes):
    hidden = dot(picked[...], normed, NT)
    width = picked.shape[0] // 4
    cols = normed.shape[0] // STEP
    for side, refs in enumerate(sides):
        values = hidden[2 * side * width : (2 * side + 1) * width]
        gates = hidden[(2 * side + 1) * width : (2 * side + 2) * width]
        kept = (jnp.tanh(gates) + 1.0) * values
        for row in range(STEP):
            scratch[side, pl.ds(row, width, stride=STEP), :] = kept[:, row * cols : (row + 1) * cols]
        done = 0
        for ref, size in zip(refs, sizes * 2):
            rows = scratch[side, done * STEP : (done + size) * STEP, :]
            ref[...] = rows.astype(jnp.bfloat16).reshape(ref.shape)
            done += size


def split_sides(outs, count, apart):
    lefts, rights = [], []
    for n in range(count):
        if apart:
            rights.append(outs[2 * n])
            lefts.append(outs[2 * n + 1])
        else:
            lefts.append(outs[n].at[0])
            rights.append(outs[n].at[1])
    for ref in outs[-count:]:
        lefts.append(ref.at[1 if apart else 0])
        rights.append(ref.at[0 if apart else 1])
    return lefts, rights


def project_all(rows, gain, gate_ref, picked, picked_gate, scratch, outs, sizes, apart):
    normed = norm_rows(rows, gain)
    project_part(normed, picked, scratch, split_sides(outs, len(sizes), apart), sizes)
    gate = 0.5 * jnp.tanh(dot(normed, picked_gate[...])) + 0.5
    gate_ref[...] = gate.astype(gate_ref.dtype).reshape(gate_ref.shape)


def first_kernel(sizes, chain_ref, block_mask_ref, pair_ref, w_ref, w_gate_ref, gain_ref, gate_ref, *rest):
    *outs, turned, picked, picked_gate, scratch = rest
    pick_weights(w_ref, w_gate_ref, tile_mask(chain_ref, block_mask_ref), turned, picked, picked_gate)
    rows = pair_ref[...].reshape(-1, pair_ref.shape[-1])
    project_all(rows, gain_ref[0:1], gate_ref, picked, picked_gate, scratch, outs, sizes, True)


def finish_rows(pair_ref, gate_ref, product_refs, w_out_ref, gain_ref, scratch, twice, out_ref):
    width = w_out_ref.shape[1]
    half = width // 2
    cols = pair_ref.shape[1]
    x = lax.axis_index("col") // 2
    mine, others = pl.multiple_of(x * half, half), pl.multiple_of((1 - x) * half, half)

    @pl.when(pl.program_id(0) == 0)
    def _():
        w_out = jnp.concatenate([w_out_ref[0, pl.ds(mine, half)], w_out_ref[0, pl.ds(others, half)]], 0)
        none = jnp.zeros_like(w_out)
        twice[...] = jnp.concatenate(
            [jnp.concatenate([w_out, none], 1), jnp.concatenate([none, w_out], 1)], 0
        )

    gain = jnp.concatenate([gain_ref[pl.ds(mine, half)], gain_ref[pl.ds(others, half)]], 0)
    product = jnp.concatenate([ref[...] for ref in product_refs], 0).astype(jnp.float32)
    mean = jnp.sum(product, 0, keepdims=True) * (1.0 / width)
    centred = product - mean
    spread = jnp.sum(centred * centred, 0, keepdims=True) * (1.0 / width)
    update = centred * lax.rsqrt(spread + EPS) * gain
    scratch[...] = update.reshape(width * STEP, cols)
    for row in range(0, STEP, 2):
        two = jnp.concatenate(
            [scratch[pl.ds(row, width, stride=STEP), :], scratch[pl.ds(row + 1, width, stride=STEP), :]], 0
        )
        changes = dot(two.astype(jnp.bfloat16), twice[...], TN)
        for k in range(2):
            change = changes[:, k * pair_ref.shape[2] : (k + 1) * pair_ref.shape[2]]
            gate = gate_ref[row + k].astype(jnp.float32)
            old = pair_ref[row + k].astype(jnp.float32)
            out_ref[row + k] = (old + gate * change).astype(jnp.bfloat16)


def finish_kernel(pair_ref, gate_ref, w_out_ref, gain_ref, *rest):
    *product_refs, out_ref, scratch, twice = rest
    finish_rows(pair_ref, gate_ref, product_refs, w_out_ref, gain_ref, scratch, twice, out_ref)


def middle_kernel(
    sizes,
    count,
    chain_ref,
    block_mask_ref,
    pair_ref,
    gate_ref,
    w_out_ref,
    gain_out_ref,
    w_ref,
    w_gate_ref,
    gain_in_ref,
    *rest,
):
    product_refs, (out_ref, next_ref, *outs) = rest[:count], rest[count:]
    *outs, update, twice, turned, picked, picked_gate, scratch = outs
    pick_weights(w_ref, w_gate_ref, tile_mask(chain_ref, block_mask_ref), turned, picked, picked_gate)
    finish_rows(pair_ref, gate_ref, product_refs, w_out_ref, gain_out_ref, update, twice, out_ref)
    rows = out_ref[...].reshape(-1, out_ref.shape[-1])
    project_all(rows, gain_in_ref[1:2], next_ref, picked, picked_gate, scratch, outs, sizes, False)


def outgoing_kernel(left, left_pair, right, right_pair, right_far, right_near, outs, rights):
    *kept, pair, sent = outs
    for k, blocks in enumerate((right, right_pair, right_far, right_near)):
        rights[k] = jnp.concatenate(blocks, 1)
    lefts = jnp.concatenate([jnp.concatenate(left, 1), jnp.concatenate(left_pair, 1)], 0)
    size = lefts.shape[0] // 2
    here = lax.axis_index("row") ^ lax.axis_index("col")
    for place in range(4):
        terms = dot(lefts, rights[here ^ place], NT).astype(jnp.bfloat16)
        if place % 2:
            sent[0, place // 2, 0] = terms[:size]
            sent[1, place // 2, 0] = terms[size:]
        else:
            kept[place // 2][0] = terms[:size]
            pair[place // 2, 0] = terms[size:]


def incoming_kernel(left, left_core, left_pair, left_pair_core, right, right_pair, outs, lefts):
    *kept, pair, cross = outs
    for k in range(2):
        lefts[2 * k] = jnp.concatenate([left[k], left_pair[k]], 0)
        lefts[2 * k + 1] = jnp.concatenate([left_core[k], left_pair_core[k]], 0)
    rights = jnp.concatenate([jnp.concatenate(right, 1), jnp.concatenate(right_pair, 1)], 0)
    size = rights.shape[1] // 2
    here = lax.axis_index("row") ^ lax.axis_index("col")
    for place in range(4):
        terms = dot(lefts[here ^ place], rights, TN).astype(jnp.bfloat16)
        for k in range(2):
            block = terms[:, k * size : (k + 1) * size]
            if place == 0:
                kept[k][0] = block
            else:
                (pair, cross.at[0], cross.at[1])[place - 1][k, 0] = block


def pieces_kernel(kernel, count, *refs):
    for channel in range(TOGETHER):
        blocks = [ref[(0,) * (len(ref.shape) - 3) + (channel,)] for ref in refs[:count]]
        outs = [ref.at[(slice(None),) * (len(ref.shape) - 3) + (pl.ds(channel, 1),)] for ref in refs[count:-1]]
        kernel(*[blocks[k : k + 2] for k in range(0, count, 2)], outs, refs[-1])


def params(limit=VMEM):
    return pltpu.CompilerParams(
        vmem_limit_bytes=limit, dimension_semantics=("arbitrary",), fuse_transposed_lhs_in_matmul=True
    )


def part(array, index):
    return pl.BlockSpec((1,) + array.shape[1:], lambda *_: (index,) + (0,) * (array.ndim - 1))


def whole(array):
    return pl.BlockSpec(array.shape, lambda *_: (0,) * array.ndim)


def tile_spec(tile):
    return pl.BlockSpec((STEP,) + tile.shape[1:], lambda r: (r, 0, 0))


def chunk_spec(shape):
    lead = shape[:-2]
    return pl.BlockSpec(lead + (STEP, shape[-1]), lambda r: (0,) * len(lead) + (r, 0))


def cost(flops, nbytes, special=0):
    return pl.CostEstimate(
        flops=int(flops * TOLD), bytes_accessed=int(nbytes * TOLD), transcendentals=int(special * TOLD)
    )


def part_outs(pair, sizes, apart):
    tile = pair.shape[:2]
    own = [(size,) + tile for size in sizes]
    both_sides = [(2,) + shape for shape in own]
    shapes = ([shape for shape in own for _ in range(2)] if apart else both_sides) + both_sides
    return [jax.ShapeDtypeStruct(shape, jnp.bfloat16) for shape in shapes], [chunk_spec(shape) for shape in shapes]


def part_scratch(pair, w_in, sizes):
    width = 2 * sum(sizes)
    return [
        pltpu.VMEM((w_in.shape[2], w_in.shape[1]), jnp.float32),
        pltpu.VMEM((4 * width, w_in.shape[1]), jnp.bfloat16),
        pltpu.VMEM((w_in.shape[1], w_in.shape[1]), jnp.bfloat16),
        pltpu.VMEM((2, width * STEP, pair.shape[1]), jnp.float32),
    ]


def finish_scratch(pair, w_out):
    return [
        pltpu.VMEM((w_out.shape[1] * STEP, pair.shape[1]), jnp.float32),
        pltpu.VMEM((2 * w_out.shape[1], 2 * w_out.shape[2]), jnp.bfloat16),
    ]


def first_call(chain, block_mask, pair, w_in, w_gate, gain_in):
    outs, specs = part_outs(pair, OUT_SIZES, True)
    gate, *result = pl.pallas_call(
        functools.partial(first_kernel, OUT_SIZES),
        grid=(pair.shape[0] // STEP,),
        in_specs=[SMEM_SPEC, SMEM_SPEC, tile_spec(pair), part(w_in, 0), part(w_gate, 0), whole(gain_in)],
        out_specs=[tile_spec(pair)] + specs,
        out_shape=[jax.ShapeDtypeStruct(pair.shape, pair.dtype)] + outs,
        scratch_shapes=part_scratch(pair, w_in, OUT_SIZES),
        compiler_params=params(FIRST_VMEM),
        cost_estimate=cost(2e9, 8 << 20, 4 << 20),
        name="project",
    )(chain, block_mask, pair, w_in, w_gate, gain_in)
    return gate, result


def finish_call(pair, gate, products, w_out, gain_wide):
    return pl.pallas_call(
        finish_kernel,
        grid=(pair.shape[0] // STEP,),
        in_specs=[tile_spec(pair), tile_spec(gate), part(w_out, 1), whole(gain_wide)]
        + [chunk_spec(p.shape) for p in products],
        out_specs=tile_spec(pair),
        out_shape=jax.ShapeDtypeStruct(pair.shape, pair.dtype),
        scratch_shapes=finish_scratch(pair, w_out),
        compiler_params=params(),
        cost_estimate=cost(1e9, 14 << 20, 4 << 20),
        name="finish",
    )(pair, gate, w_out, gain_wide, *products)


def middle_call(chain, block_mask, pair, gate, products, w_out, gain_wide, w_in, w_gate, gain_in):
    outs, specs = part_outs(pair, IN_SIZES, False)
    middle, gate, *result = pl.pallas_call(
        functools.partial(middle_kernel, IN_SIZES, len(products)),
        grid=(pair.shape[0] // STEP,),
        in_specs=[SMEM_SPEC, SMEM_SPEC, tile_spec(pair), tile_spec(gate), part(w_out, 0)]
        + [whole(gain_wide), part(w_in, 1), part(w_gate, 1), whole(gain_in)]
        + [chunk_spec(p.shape) for p in products],
        out_specs=[tile_spec(pair)] * 2 + specs,
        out_shape=[jax.ShapeDtypeStruct(pair.shape, pair.dtype)] * 2 + outs,
        scratch_shapes=finish_scratch(pair, w_out) + part_scratch(pair, w_in, IN_SIZES),
        compiler_params=params(),
        cost_estimate=cost(3e9, 18 << 20, 8 << 20),
        name="middle",
    )(chain, block_mask, pair, gate, w_out, gain_wide, w_in, w_gate, gain_in, *products)
    return middle, gate, result


def product_call(kernel, operands, channels, leads, scratch, name):
    pieces = [piece for operand in operands for piece in operand]
    size = pieces[0][0].shape[-1]

    def piece_spec(array, lead, first):
        return pl.BlockSpec(
            (1,) * len(lead) + (TOGETHER, size, size), lambda c: lead + (first // TOGETHER + c, 0, 0)
        )

    def out_spec(lead):
        return pl.BlockSpec(lead + (TOGETHER, size, size), lambda c: (0,) * len(lead) + (c, 0, 0))

    return pl.pallas_call(
        functools.partial(pieces_kernel, kernel, len(pieces)),
        grid=(channels // TOGETHER,),
        in_specs=[piece_spec(*piece) for piece in pieces],
        out_specs=[out_spec(lead) for lead in leads],
        out_shape=[jax.ShapeDtypeStruct(lead + (channels, size, size), jnp.bfloat16) for lead in leads],
        scratch_shapes=[pltpu.VMEM(scratch, jnp.bfloat16)],
        compiler_params=params(PRODUCT_VMEM),
        cost_estimate=cost(channels * 2 * (4 * size) ** 2 * size, channels * size * size * 2 * 20),
        name=name,
    )(*[piece[0] for piece in pieces])


WAYS = {
    "in": ("row", [(0, 1), (3, 2)]),
    "across": ("row", [(1, 2), (2, 1)]),
    "out": ("row", [(1, 0), (2, 3)]),
    "x": ("col", [(c, c ^ 2) for c in range(4)]),
    "core": ("col", [(c, c ^ 1) for c in range(4)]),
}


class Graph:
    def __init__(self, order):
        self.order, self.steps, self.made = order, {}, {}

    def add(self, name, operand, step):
        self.steps[name] = (operand, step)

    def send(self, name, way, operand):
        axis, pairs = WAYS[way]
        self.add(name, operand, lambda array: lax.ppermute(array, axis, pairs))

    def get(self, name):
        if name not in self.made:
            operand, step = self.steps[name]
            waits = [self.get(other) for other in self.order.get(name, ())]
            array = operand()
            if waits:
                array = lax.optimization_barrier((array, *waits))[0]
            self.made[name] = step(array)
        return self.made[name]


def pack(*columns):
    return jnp.stack([jnp.concatenate([column[k] for column in columns]) for k in range(2)])


def both(array, first=0, lead=()):
    return [(array, (k,) + lead, first) for k in range(2)]


def is_inner():
    row = lax.axis_index("row")
    return (row == 1) | (row == 2)


def shared_steps(graph, groups, mine, other):
    inner = is_inner()
    get = graph.get
    first, names = 0, []

    def joined(arrays, axis):
        return arrays[0] if len(arrays) == 1 else jnp.concatenate(arrays, axis)

    for g, size in enumerate(groups):
        chunks = range(first, first + size)
        first += size

        def ready(k, g=g, chunks=chunks):
            return jnp.where(inner, joined([mine(n, k) for n in chunks], 0), get(f"o{g}")[k])

        graph.send(f"o{g}", "out", lambda chunks=chunks: joined([other(n) for n in chunks], 1))
        graph.send(f"b{g}", "x", lambda ready=ready: ready(1))
        graph.add(f"k{g}", lambda ready=ready: ready(0), lambda array: array)
    return [get(kind + str(g)) for kind in ("k", "b") for g in range(len(groups))]


def outgoing(parts):
    count = len(OUT_SIZES)
    graph = Graph(OUT_ORDER)
    get, send = graph.get, graph.send
    for n in range(count):
        send(f"x{n}", "x", lambda n=n: parts[2 * count + n])
    later = lambda n, side: parts[2 * n + side]
    right_of = lambda n: (later(n, 0), get(f"x{n}")[0])
    left_of = lambda n: (later(n, 1), get(f"x{n}")[1])
    first = parts
    zero = OUT_SIZES[0]
    send("i0", "in", lambda: first[0])
    send("a0", "across", lambda: first[0])
    send("i1", "in", lambda: jnp.concatenate([get("x0")[0], first[1]]))
    send("a1", "across", lambda: jnp.concatenate([get("x0")[0], get("i0")]))

    def come(n):
        array, skip = get(f"i{n + 1}"), zero // 2 if n == 1 else OUT_SIZES[n - 1]
        return (array[0, skip:], array[1, skip:])

    def halves(array):
        return (array[: zero // 2], array[zero // 2 :])

    def inward(n):
        before = halves(get("x0")[1]) if n == 1 else left_of(n - 1)
        return pack(before, right_of(n)) if n < count else pack(before)

    def across(n):
        before = halves(get("i1")[:zero]) if n == 1 else come(n - 1)
        return pack(before, right_of(n)) if n < count else pack(before)

    for n in range(1, count + 1):
        send(f"i{n + 1}", "in", lambda n=n: inward(n))
        send(f"a{n + 1}", "across", lambda n=n: across(n))

    def product(n, left):
        size = left.shape[-1]
        if n == 0:
            x_left = lambda array: array[:, : zero // 2].reshape((zero,) + array.shape[2:])
            operands = [
                [(left, (), 0), (get("x0"), (1,), 0)],
                [(get("i1"), (), zero), (x_left(get("i2")), (), 0)],
                [(first[0], (), 0), (get("x0"), (0,), 0)],
                [(get("i0"), (), 0), (get("i1"), (), 0)],
                [(get("a1"), (), zero), (x_left(get("a2")), (), 0)],
                [(get("a0"), (), 0), (get("a1"), (), 0)],
            ]
        else:
            skip = zero // 2 if n == 1 else OUT_SIZES[n - 1]
            operands = [
                [(left, (), 0), (get(f"x{n}"), (1,), 0)],
                both(get(f"i{n + 2}")),
                [(later(n, 0), (), 0), (get(f"x{n}"), (0,), 0)],
                both(get(f"i{n + 1}"), skip),
                both(get(f"a{n + 2}")),
                both(get(f"a{n + 1}"), skip),
            ]
        leads = ((), (), (2,), (2, 2))
        return product_call(outgoing_kernel, operands, left.shape[0], leads, (4, size, 2 * size), "outgoing")

    for n in range(count):
        graph.add(f"p{n}", lambda n=n: later(n, 1), functools.partial(product, n))
        send(f"c{n}", "core", lambda n=n: get(f"p{n}")[3])
    return shared_steps(
        graph,
        OUT_GROUPS,
        lambda n, k: get(f"p{n}")[k] + get(f"c{n}")[0, k],
        lambda n: get(f"p{n}")[2] + get(f"c{n}")[1],
    )


def incoming(parts):
    count = len(IN_SIZES)
    graph = Graph(IN_ORDER)
    get, send = graph.get, graph.send
    for n in range(count):
        send(f"x{n}", "x", lambda n=n: parts[count + n])
    send("i0", "in", lambda: parts[0])
    send("i0x", "in", lambda: get("x0"))
    send("cl0", "core", lambda: parts[0])
    send("clx", "core", lambda: get("x0"))
    send("cp0", "core", lambda: get("i0"))
    send("cpx", "core", lambda: get("i0x"))
    for n in range(1, count):
        graph.add(f"j{n}", lambda n=n: parts[n], lambda own, n=n: jnp.stack([own, get(f"x{n}")], 1))
        send(f"i{n}", "in", lambda n=n: get(f"j{n}"))
        send(f"cl{n}", "core", lambda n=n: get(f"j{n}")[0])
        send(f"cp{n}", "core", lambda n=n: get(f"i{n}")[0])

    def product(n, own):
        size = own.shape[-1]
        if n == 0:
            side = lambda name, name_x, slot: [
                (own if name is None else get(name), (slot,), 0),
                (get(name_x), (slot,), 0),
            ]
            operands = [side(None, "x0", 0), side("cl0", "clx", 0), side("i0", "i0x", 0), side("cp0", "cpx", 0)]
            operands += [side(None, "x0", 1), side("i0", "i0x", 1)]
        else:
            side = lambda array, slot: [(array, (slot, k), 0) for k in range(2)]
            operands = [side(own, 0), both(get(f"cl{n}")), side(get(f"i{n}"), 0), both(get(f"cp{n}"))]
            operands += [side(own, 1), side(get(f"i{n}"), 1)]
        leads = ((), (), (2,), (2, 2))
        return product_call(incoming_kernel, operands, IN_SIZES[n], leads, (4, 2 * size, size), "incoming")

    for n in range(count):
        graph.add(f"p{n}", lambda n=n: get(f"j{n}") if n else parts[0], functools.partial(product, n))
        send(f"a{n}", "across", lambda n=n: get(f"p{n}")[3])
    return shared_steps(
        graph,
        IN_GROUPS,
        lambda n, k: get(f"p{n}")[k] + get(f"a{n}")[1, k],
        lambda n: get(f"p{n}")[2] + get(f"a{n}")[0],
    )


def four_by_four(pair, chain, block_mask, w_in, w_gate, w_out, gain_in, gain_out):
    gain_wide = jnp.broadcast_to(gain_out[:, :, None, None], gain_out.shape + (1, pair.shape[1]))
    gate, parts = first_call(chain, block_mask, pair, w_in, w_gate, gain_in)
    products = outgoing(parts)
    middle, gate, parts = middle_call(
        chain, block_mask, pair, gate, products, w_out, gain_wide[0], w_in, w_gate, gain_in
    )
    products = incoming(parts)
    return finish_call(middle, gate, products, w_out, gain_wide[1])


def solution(mesh):
    four = mesh.shape["row"] == 4 and mesh.shape["col"] == 4
    return jax.shard_map(
        four_by_four if four else any_mesh,
        mesh=mesh,
        in_specs=(
            P(("group", "row"), "col", None),
            P("group"),
            P("group", None),
            P(),
            P(),
            P(),
            P(),
            P(),
        ),
        out_specs=P(("group", "row"), "col", None),
        check_vma=False,
    )
```

```python
import functools

import jax
import jax.numpy as jnp
from jax import lax
from jax.experimental import pallas as pl
from jax.experimental.pallas import tpu as pltpu
from jax.sharding import PartitionSpec as P

BLOCK = 128
EPS = 1e-05
OUT_SIZES = (8, 8, 8, 4, 4)
IN_SIZES = (8, 8, 8, 4, 4)
OUT_GROUPS = (1, 1, 1, 1, 1)
IN_GROUPS = (1, 1, 1, 1, 1)
OUT_ORDER = {'i1': ('i0',), 'i2': ('i1',), 'i3': ('i2',), 'i4': ('i3',), 'i5': ('i4',), 'i6': ('i5',), 'a1': ('a0',), 'a2': ('a1',), 'a3': ('a2',), 'a4': ('a3',), 'a5': ('a4', 'p1'), 'a6': ('a5',), 'x2': ('x1', 'a1'), 'x3': ('x2',), 'x4': ('x3',), 'o2': ('o1',), 'x1': ('a0',), 'p2': ('o0',), 'p3': ('o1',), 'p4': ('o2',)}
IN_ORDER = {'i0x': ('i0',), 'i3': ('i2',), 'i4': ('i3',), 'a1': ('a0', 'i1'), 'a3': ('a2',), 'o2': ('o1',), 'o3': ('o2',), 'o4': ('o3',), 'x1': ('i0',), 'x2': ('i0x',), 'c4': ('c3',)}
STEP = 16
TOLD = 0.05
TOGETHER = 4
FIRST_VMEM = 61 * 1024 * 1024
VMEM = 28 * 1024 * 1024
PRODUCT_VMEM = 10 * 1024 * 1024


def broadcast(block, axis, owner):
    block = jnp.where(lax.axis_index(axis) == owner, block, jnp.zeros_like(block))
    return lax.psum(block, axis)


def layer_norm(values, gain):
    mean = jnp.mean(values, -1, keepdims=True)
    centred = values - mean
    spread = jnp.mean(centred * centred, -1, keepdims=True)
    return centred * lax.rsqrt(spread + EPS) * gain


def project(pair, tile_mask, w_in, w_gate, gain_in):
    normed = layer_norm(pair.astype(jnp.float32), gain_in).astype(jnp.bfloat16)
    hidden = jnp.dot(normed, w_in, preferred_element_type=jnp.float32)
    width = w_in.shape[1] // 4
    masked = tile_mask[..., None]
    left = (masked * jax.nn.sigmoid(hidden[..., width : 2 * width]) * hidden[..., :width]).astype(
        jnp.bfloat16
    )
    right = (
        masked * jax.nn.sigmoid(hidden[..., 3 * width :]) * hidden[..., 2 * width : 3 * width]
    ).astype(jnp.bfloat16)
    gate = jax.nn.sigmoid(jnp.dot(normed, w_gate, preferred_element_type=jnp.float32))
    return (left, right, gate)


def finish(pair, product, gate, w_out, gain_out):
    update = layer_norm(product, gain_out).astype(jnp.bfloat16)
    return (
        pair.astype(jnp.float32) + gate * jnp.dot(update, w_out, preferred_element_type=jnp.float32)
    ).astype(jnp.bfloat16)


def any_mesh(pair, chain, block_mask, w_in, w_gate, w_out, gain_in, gain_out):
    tile_rows = pair.shape[0]
    tile_cols = pair.shape[1]
    block_count = chain.shape[0]
    ratio = lax.axis_size("row") // lax.axis_size("col")
    row_index = lax.axis_index("row")
    col_index = lax.axis_index("col")
    same = chain[:, None] == chain[None, :]
    blocks = jnp.where(same | (block_mask == 1), 1.0, 0.0).astype(jnp.float32)
    labels = jnp.arange(block_count, dtype=jnp.int32)
    row_blocks = (row_index * tile_rows + jnp.arange(tile_rows, dtype=jnp.int32)) // BLOCK
    col_blocks = (col_index * tile_cols + jnp.arange(tile_cols, dtype=jnp.int32)) // BLOCK
    row_onehot = jnp.where(row_blocks[:, None] == labels[None, :], 1.0, 0.0).astype(jnp.float32)
    col_onehot = jnp.where(col_blocks[:, None] == labels[None, :], 1.0, 0.0).astype(jnp.float32)
    tile_mask = jnp.dot(jnp.dot(row_onehot, blocks), col_onehot.T)
    left, right, gate = project(pair, tile_mask, w_in[0], w_gate[0], gain_in[0])
    partial_terms = jnp.einsum(
        "ikc,jkc->ijc",
        left,
        lax.all_gather(right, "row", axis=0, tiled=True),
        preferred_element_type=jnp.float32,
    )
    product = lax.psum_scatter(
        partial_terms.astype(jnp.bfloat16), "col", scatter_dimension=1, tiled=True
    ).astype(jnp.float32)
    middle = finish(pair, product, gate, w_out[0], gain_out[0])
    left, right, gate = project(middle, tile_mask, w_in[1], w_gate[1], gain_in[1])
    left_cols = lax.all_gather(left, "row", axis=0, tiled=True)
    start_col = row_index % ratio * tile_rows
    left_slice = lax.dynamic_slice_in_dim(left_cols, start_col, tile_rows, 1)
    left_mine = broadcast(left_slice, "col", row_index // ratio)
    product = jnp.einsum(
        "kic,kjc->ijc",
        left_mine,
        lax.all_gather(right, "row", axis=0, tiled=True),
        preferred_element_type=jnp.float32,
    )
    return finish(middle, product, gate, w_out[1], gain_out[1])


NN = (((1,), (0,)), ((), ()))
NT = (((1,), (1,)), ((), ()))
TN = (((0,), (0,)), ((), ()))
SMEM_SPEC = pl.BlockSpec(memory_space=pltpu.SMEM)


def dot(a, b, dims=NN):
    return lax.dot_general(a, b, dims, preferred_element_type=jnp.float32)


def norm_rows(rows, gain):
    channels = rows.shape[-1]
    place = lax.broadcasted_iota(jnp.int32, (channels, channels), 0)
    same = place == lax.broadcasted_iota(jnp.int32, (channels, channels), 1)
    centre = jnp.where(same, 1.0 - 1.0 / channels, -1.0 / channels).astype(jnp.bfloat16)
    mean_of = jnp.full((channels, channels), 1.0 / channels, jnp.bfloat16)
    centred = dot(rows, centre)
    spread = dot((centred * centred).astype(jnp.bfloat16), mean_of)
    return (centred * lax.rsqrt(spread + EPS) * gain).astype(jnp.bfloat16)


def tile_mask(chain_ref, block_mask_ref):
    row, col = lax.axis_index("row"), lax.axis_index("col")
    seen = (chain_ref[row] == chain_ref[col]) | (block_mask_ref[row, col] == 1)
    return jnp.where(seen, 1.0, 0.0).astype(jnp.float32)


def pick_weights(w_ref, w_gate_ref, mask, turned, picked, picked_gate):
    @pl.when(pl.program_id(0) == 0)
    def _():
        turned[...] = w_ref[0].astype(jnp.float32).T
        half = turned.shape[0] // 8
        x = lax.axis_index("col") // 2
        rows = []
        for kind in range(4):
            for other in (x, 1 - x):
                some = turned[pl.ds(pl.multiple_of((2 * kind + other) * half, 8), half), :]
                rows.append(some * (0.5 if kind % 2 else 0.5 * mask))
        picked[...] = jnp.concatenate(rows, 0).astype(jnp.bfloat16)
        picked_gate[...] = (w_gate_ref[0].astype(jnp.float32) * 0.5).astype(jnp.bfloat16)


def project_part(normed, picked, scratch, sides, sizes):
    hidden = dot(picked[...], normed, NT)
    width = picked.shape[0] // 4
    cols = normed.shape[0] // STEP
    for side, refs in enumerate(sides):
        values = hidden[2 * side * width : (2 * side + 1) * width]
        gates = hidden[(2 * side + 1) * width : (2 * side + 2) * width]
        kept = (jnp.tanh(gates) + 1.0) * values
        for row in range(STEP):
            scratch[side, pl.ds(row, width, stride=STEP), :] = kept[:, row * cols : (row + 1) * cols]
        done = 0
        for ref, size in zip(refs, sizes * 2):
            rows = scratch[side, done * STEP : (done + size) * STEP, :]
            ref[...] = rows.astype(jnp.bfloat16).reshape(ref.shape)
            done += size


def split_sides(outs, count, apart):
    lefts, rights = [], []
    for n in range(count):
        if apart:
            rights.append(outs[2 * n])
            lefts.append(outs[2 * n + 1])
        else:
            lefts.append(outs[n].at[0])
            rights.append(outs[n].at[1])
    for ref in outs[-count:]:
        lefts.append(ref.at[1 if apart else 0])
        rights.append(ref.at[0 if apart else 1])
    return lefts, rights


def project_all(rows, gain, gate_ref, picked, picked_gate, scratch, outs, sizes, apart):
    normed = norm_rows(rows, gain)
    project_part(normed, picked, scratch, split_sides(outs, len(sizes), apart), sizes)
    gate = 0.5 * jnp.tanh(dot(normed, picked_gate[...])) + 0.5
    gate_ref[...] = gate.astype(gate_ref.dtype).reshape(gate_ref.shape)


def first_kernel(sizes, chain_ref, block_mask_ref, pair_ref, w_ref, w_gate_ref, gain_ref, gate_ref, *rest):
    *outs, turned, picked, picked_gate, scratch = rest
    pick_weights(w_ref, w_gate_ref, tile_mask(chain_ref, block_mask_ref), turned, picked, picked_gate)
    rows = pair_ref[...].reshape(-1, pair_ref.shape[-1])
    project_all(rows, gain_ref[0:1], gate_ref, picked, picked_gate, scratch, outs, sizes, True)


def finish_rows(pair_ref, gate_ref, product_refs, w_out_ref, gain_ref, scratch, twice, out_ref):
    width = w_out_ref.shape[1]
    half = width // 2
    cols = pair_ref.shape[1]
    x = lax.axis_index("col") // 2
    mine, others = pl.multiple_of(x * half, half), pl.multiple_of((1 - x) * half, half)

    @pl.when(pl.program_id(0) == 0)
    def _():
        w_out = jnp.concatenate([w_out_ref[0, pl.ds(mine, half)], w_out_ref[0, pl.ds(others, half)]], 0)
        none = jnp.zeros_like(w_out)
        twice[...] = jnp.concatenate(
            [jnp.concatenate([w_out, none], 1), jnp.concatenate([none, w_out], 1)], 0
        )

    gain = jnp.concatenate([gain_ref[pl.ds(mine, half)], gain_ref[pl.ds(others, half)]], 0)
    product = jnp.concatenate([ref[...] for ref in product_refs], 0).astype(jnp.float32)
    mean = jnp.sum(product, 0, keepdims=True) * (1.0 / width)
    centred = product - mean
    spread = jnp.sum(centred * centred, 0, keepdims=True) * (1.0 / width)
    update = centred * lax.rsqrt(spread + EPS) * gain
    scratch[...] = update.reshape(width * STEP, cols)
    for row in range(0, STEP, 2):
        two = jnp.concatenate(
            [scratch[pl.ds(row, width, stride=STEP), :], scratch[pl.ds(row + 1, width, stride=STEP), :]], 0
        )
        changes = dot(two.astype(jnp.bfloat16), twice[...], TN)
        for k in range(2):
            change = changes[:, k * pair_ref.shape[2] : (k + 1) * pair_ref.shape[2]]
            gate = gate_ref[row + k].astype(jnp.float32)
            old = pair_ref[row + k].astype(jnp.float32)
            out_ref[row + k] = (old + gate * change).astype(jnp.bfloat16)


def finish_kernel(pair_ref, gate_ref, w_out_ref, gain_ref, *rest):
    *product_refs, out_ref, scratch, twice = rest
    finish_rows(pair_ref, gate_ref, product_refs, w_out_ref, gain_ref, scratch, twice, out_ref)


def middle_kernel(
    sizes,
    count,
    chain_ref,
    block_mask_ref,
    pair_ref,
    gate_ref,
    w_out_ref,
    gain_out_ref,
    w_ref,
    w_gate_ref,
    gain_in_ref,
    *rest,
):
    product_refs, (out_ref, next_ref, *outs) = rest[:count], rest[count:]
    *outs, update, twice, turned, picked, picked_gate, scratch = outs
    pick_weights(w_ref, w_gate_ref, tile_mask(chain_ref, block_mask_ref), turned, picked, picked_gate)
    finish_rows(pair_ref, gate_ref, product_refs, w_out_ref, gain_out_ref, update, twice, out_ref)
    rows = out_ref[...].reshape(-1, out_ref.shape[-1])
    project_all(rows, gain_in_ref[1:2], next_ref, picked, picked_gate, scratch, outs, sizes, False)


def outgoing_kernel(left, left_pair, right, right_pair, right_far, right_near, outs, rights):
    *kept, pair, sent = outs
    for k, blocks in enumerate((right, right_pair, right_far, right_near)):
        rights[k] = jnp.concatenate(blocks, 1)
    lefts = jnp.concatenate([jnp.concatenate(left, 1), jnp.concatenate(left_pair, 1)], 0)
    size = lefts.shape[0] // 2
    here = lax.axis_index("row") ^ lax.axis_index("col")
    for place in range(4):
        terms = dot(lefts, rights[here ^ place], NT).astype(jnp.bfloat16)
        if place % 2:
            sent[0, place // 2, 0] = terms[:size]
            sent[1, place // 2, 0] = terms[size:]
        else:
            kept[place // 2][0] = terms[:size]
            pair[place // 2, 0] = terms[size:]


def incoming_kernel(left, left_core, left_pair, left_pair_core, right, right_pair, outs, lefts):
    *kept, pair, cross = outs
    for k in range(2):
        lefts[2 * k] = jnp.concatenate([left[k], left_pair[k]], 0)
        lefts[2 * k + 1] = jnp.concatenate([left_core[k], left_pair_core[k]], 0)
    rights = jnp.concatenate([jnp.concatenate(right, 1), jnp.concatenate(right_pair, 1)], 0)
    size = rights.shape[1] // 2
    here = lax.axis_index("row") ^ lax.axis_index("col")
    for place in range(4):
        terms = dot(lefts[here ^ place], rights, TN).astype(jnp.bfloat16)
        for k in range(2):
            block = terms[:, k * size : (k + 1) * size]
            if place == 0:
                kept[k][0] = block
            else:
                (pair, cross.at[0], cross.at[1])[place - 1][k, 0] = block


def pieces_kernel(kernel, count, *refs):
    for channel in range(TOGETHER):
        blocks = [ref[(0,) * (len(ref.shape) - 3) + (channel,)] for ref in refs[:count]]
        outs = [ref.at[(slice(None),) * (len(ref.shape) - 3) + (pl.ds(channel, 1),)] for ref in refs[count:-1]]
        kernel(*[blocks[k : k + 2] for k in range(0, count, 2)], outs, refs[-1])


def params(limit=VMEM):
    return pltpu.CompilerParams(
        vmem_limit_bytes=limit, dimension_semantics=("arbitrary",), fuse_transposed_lhs_in_matmul=True
    )


def part(array, index):
    return pl.BlockSpec((1,) + array.shape[1:], lambda *_: (index,) + (0,) * (array.ndim - 1))


def whole(array):
    return pl.BlockSpec(array.shape, lambda *_: (0,) * array.ndim)


def tile_spec(tile):
    return pl.BlockSpec((STEP,) + tile.shape[1:], lambda r: (r, 0, 0))


def chunk_spec(shape):
    lead = shape[:-2]
    return pl.BlockSpec(lead + (STEP, shape[-1]), lambda r: (0,) * len(lead) + (r, 0))


def cost(flops, nbytes, special=0):
    return pl.CostEstimate(
        flops=int(flops * TOLD), bytes_accessed=int(nbytes * TOLD), transcendentals=int(special * TOLD)
    )


def part_outs(pair, sizes, apart):
    tile = pair.shape[:2]
    own = [(size,) + tile for size in sizes]
    both_sides = [(2,) + shape for shape in own]
    shapes = ([shape for shape in own for _ in range(2)] if apart else both_sides) + both_sides
    return [jax.ShapeDtypeStruct(shape, jnp.bfloat16) for shape in shapes], [chunk_spec(shape) for shape in shapes]


def part_scratch(pair, w_in, sizes):
    width = 2 * sum(sizes)
    return [
        pltpu.VMEM((w_in.shape[2], w_in.shape[1]), jnp.float32),
        pltpu.VMEM((4 * width, w_in.shape[1]), jnp.bfloat16),
        pltpu.VMEM((w_in.shape[1], w_in.shape[1]), jnp.bfloat16),
        pltpu.VMEM((2, width * STEP, pair.shape[1]), jnp.float32),
    ]


def finish_scratch(pair, w_out):
    return [
        pltpu.VMEM((w_out.shape[1] * STEP, pair.shape[1]), jnp.float32),
        pltpu.VMEM((2 * w_out.shape[1], 2 * w_out.shape[2]), jnp.bfloat16),
    ]


def first_call(chain, block_mask, pair, w_in, w_gate, gain_in):
    outs, specs = part_outs(pair, OUT_SIZES, True)
    gate, *result = pl.pallas_call(
        functools.partial(first_kernel, OUT_SIZES),
        grid=(pair.shape[0] // STEP,),
        in_specs=[SMEM_SPEC, SMEM_SPEC, tile_spec(pair), part(w_in, 0), part(w_gate, 0), whole(gain_in)],
        out_specs=[tile_spec(pair)] + specs,
        out_shape=[jax.ShapeDtypeStruct(pair.shape, pair.dtype)] + outs,
        scratch_shapes=part_scratch(pair, w_in, OUT_SIZES),
        compiler_params=params(FIRST_VMEM),
        cost_estimate=cost(2e9, 8 << 20, 4 << 20),
        name="project",
    )(chain, block_mask, pair, w_in, w_gate, gain_in)
    return gate, result


def finish_call(pair, gate, products, w_out, gain_wide):
    return pl.pallas_call(
        finish_kernel,
        grid=(pair.shape[0] // STEP,),
        in_specs=[tile_spec(pair), tile_spec(gate), part(w_out, 1), whole(gain_wide)]
        + [chunk_spec(p.shape) for p in products],
        out_specs=tile_spec(pair),
        out_shape=jax.ShapeDtypeStruct(pair.shape, pair.dtype),
        scratch_shapes=finish_scratch(pair, w_out),
        compiler_params=params(),
        cost_estimate=cost(1e9, 14 << 20, 4 << 20),
        name="finish",
    )(pair, gate, w_out, gain_wide, *products)


def middle_call(chain, block_mask, pair, gate, products, w_out, gain_wide, w_in, w_gate, gain_in):
    outs, specs = part_outs(pair, IN_SIZES, False)
    middle, gate, *result = pl.pallas_call(
        functools.partial(middle_kernel, IN_SIZES, len(products)),
        grid=(pair.shape[0] // STEP,),
        in_specs=[SMEM_SPEC, SMEM_SPEC, tile_spec(pair), tile_spec(gate), part(w_out, 0)]
        + [whole(gain_wide), part(w_in, 1), part(w_gate, 1), whole(gain_in)]
        + [chunk_spec(p.shape) for p in products],
        out_specs=[tile_spec(pair)] * 2 + specs,
        out_shape=[jax.ShapeDtypeStruct(pair.shape, pair.dtype)] * 2 + outs,
        scratch_shapes=finish_scratch(pair, w_out) + part_scratch(pair, w_in, IN_SIZES),
        compiler_params=params(),
        cost_estimate=cost(3e9, 18 << 20, 8 << 20),
        name="middle",
    )(chain, block_mask, pair, gate, w_out, gain_wide, w_in, w_gate, gain_in, *products)
    return middle, gate, result


def product_call(kernel, operands, channels, leads, scratch, name):
    pieces = [piece for operand in operands for piece in operand]
    size = pieces[0][0].shape[-1]

    def piece_spec(array, lead, first):
        return pl.BlockSpec(
            (1,) * len(lead) + (TOGETHER, size, size), lambda c: lead + (first // TOGETHER + c, 0, 0)
        )

    def out_spec(lead):
        return pl.BlockSpec(lead + (TOGETHER, size, size), lambda c: (0,) * len(lead) + (c, 0, 0))

    return pl.pallas_call(
        functools.partial(pieces_kernel, kernel, len(pieces)),
        grid=(channels // TOGETHER,),
        in_specs=[piece_spec(*piece) for piece in pieces],
        out_specs=[out_spec(lead) for lead in leads],
        out_shape=[jax.ShapeDtypeStruct(lead + (channels, size, size), jnp.bfloat16) for lead in leads],
        scratch_shapes=[pltpu.VMEM(scratch, jnp.bfloat16)],
        compiler_params=params(PRODUCT_VMEM),
        cost_estimate=cost(channels * 2 * (4 * size) ** 2 * size, channels * size * size * 2 * 20),
        name=name,
    )(*[piece[0] for piece in pieces])


WAYS = {
    "in": ("row", [(0, 1), (3, 2)]),
    "across": ("row", [(1, 2), (2, 1)]),
    "out": ("row", [(1, 0), (2, 3)]),
    "x": ("col", [(c, c ^ 2) for c in range(4)]),
    "core": ("col", [(c, c ^ 1) for c in range(4)]),
}


class Graph:
    def __init__(self, order):
        self.order, self.steps, self.made = order, {}, {}

    def add(self, name, operand, step):
        self.steps[name] = (operand, step)

    def send(self, name, way, operand):
        axis, pairs = WAYS[way]
        self.add(name, operand, lambda array: lax.ppermute(array, axis, pairs))

    def get(self, name):
        if name not in self.made:
            operand, step = self.steps[name]
            waits = [self.get(other) for other in self.order.get(name, ())]
            array = operand()
            if waits:
                array = lax.optimization_barrier((array, *waits))[0]
            self.made[name] = step(array)
        return self.made[name]


def pack(*columns):
    return jnp.stack([jnp.concatenate([column[k] for column in columns]) for k in range(2)])


def both(array, first=0, lead=()):
    return [(array, (k,) + lead, first) for k in range(2)]


def is_inner():
    row = lax.axis_index("row")
    return (row == 1) | (row == 2)


def shared_steps(graph, groups, mine, other):
    inner = is_inner()
    get = graph.get
    first, names = 0, []

    def joined(arrays, axis):
        return arrays[0] if len(arrays) == 1 else jnp.concatenate(arrays, axis)

    for g, size in enumerate(groups):
        chunks = range(first, first + size)
        first += size

        def ready(k, g=g, chunks=chunks):
            return jnp.where(inner, joined([mine(n, k) for n in chunks], 0), get(f"o{g}")[k])

        graph.send(f"o{g}", "out", lambda chunks=chunks: joined([other(n) for n in chunks], 1))
        graph.send(f"b{g}", "x", lambda ready=ready: ready(1))
        graph.add(f"k{g}", lambda ready=ready: ready(0), lambda array: array)
    return [get(kind + str(g)) for kind in ("k", "b") for g in range(len(groups))]


def outgoing(parts):
    count = len(OUT_SIZES)
    graph = Graph(OUT_ORDER)
    get, send = graph.get, graph.send
    for n in range(count):
        send(f"x{n}", "x", lambda n=n: parts[2 * count + n])
    later = lambda n, side: parts[2 * n + side]
    right_of = lambda n: (later(n, 0), get(f"x{n}")[0])
    left_of = lambda n: (later(n, 1), get(f"x{n}")[1])
    first = parts
    zero = OUT_SIZES[0]
    send("i0", "in", lambda: first[0])
    send("a0", "across", lambda: first[0])
    send("i1", "in", lambda: jnp.concatenate([get("x0")[0], first[1]]))
    send("a1", "across", lambda: jnp.concatenate([get("x0")[0], get("i0")]))

    def come(n):
        array, skip = get(f"i{n + 1}"), zero // 2 if n == 1 else OUT_SIZES[n - 1]
        return (array[0, skip:], array[1, skip:])

    def halves(array):
        return (array[: zero // 2], array[zero // 2 :])

    def inward(n):
        before = halves(get("x0")[1]) if n == 1 else left_of(n - 1)
        return pack(before, right_of(n)) if n < count else pack(before)

    def across(n):
        before = halves(get("i1")[:zero]) if n == 1 else come(n - 1)
        return pack(before, right_of(n)) if n < count else pack(before)

    for n in range(1, count + 1):
        send(f"i{n + 1}", "in", lambda n=n: inward(n))
        send(f"a{n + 1}", "across", lambda n=n: across(n))

    def product(n, left):
        size = left.shape[-1]
        if n == 0:
            x_left = lambda array: array[:, : zero // 2].reshape((zero,) + array.shape[2:])
            operands = [
                [(left, (), 0), (get("x0"), (1,), 0)],
                [(get("i1"), (), zero), (x_left(get("i2")), (), 0)],
                [(first[0], (), 0), (get("x0"), (0,), 0)],
                [(get("i0"), (), 0), (get("i1"), (), 0)],
                [(get("a1"), (), zero), (x_left(get("a2")), (), 0)],
                [(get("a0"), (), 0), (get("a1"), (), 0)],
            ]
        else:
            skip = zero // 2 if n == 1 else OUT_SIZES[n - 1]
            operands = [
                [(left, (), 0), (get(f"x{n}"), (1,), 0)],
                both(get(f"i{n + 2}")),
                [(later(n, 0), (), 0), (get(f"x{n}"), (0,), 0)],
                both(get(f"i{n + 1}"), skip),
                both(get(f"a{n + 2}")),
                both(get(f"a{n + 1}"), skip),
            ]
        leads = ((), (), (2,), (2, 2))
        return product_call(outgoing_kernel, operands, left.shape[0], leads, (4, size, 2 * size), "outgoing")

    for n in range(count):
        graph.add(f"p{n}", lambda n=n: later(n, 1), functools.partial(product, n))
        send(f"c{n}", "core", lambda n=n: get(f"p{n}")[3])
    return shared_steps(
        graph,
        OUT_GROUPS,
        lambda n, k: get(f"p{n}")[k] + get(f"c{n}")[0, k],
        lambda n: get(f"p{n}")[2] + get(f"c{n}")[1],
    )


def incoming(parts):
    count = len(IN_SIZES)
    graph = Graph(IN_ORDER)
    get, send = graph.get, graph.send
    for n in range(count):
        send(f"x{n}", "x", lambda n=n: parts[count + n])
    send("i0", "in", lambda: parts[0])
    send("i0x", "in", lambda: get("x0"))
    send("cl0", "core", lambda: parts[0])
    send("clx", "core", lambda: get("x0"))
    send("cp0", "core", lambda: get("i0"))
    send("cpx", "core", lambda: get("i0x"))
    for n in range(1, count):
        graph.add(f"j{n}", lambda n=n: parts[n], lambda own, n=n: jnp.stack([own, get(f"x{n}")], 1))
        send(f"i{n}", "in", lambda n=n: get(f"j{n}"))
        send(f"cl{n}", "core", lambda n=n: get(f"j{n}")[0])
        send(f"cp{n}", "core", lambda n=n: get(f"i{n}")[0])

    def product(n, own):
        size = own.shape[-1]
        if n == 0:
            side = lambda name, name_x, slot: [
                (own if name is None else get(name), (slot,), 0),
                (get(name_x), (slot,), 0),
            ]
            operands = [side(None, "x0", 0), side("cl0", "clx", 0), side("i0", "i0x", 0), side("cp0", "cpx", 0)]
            operands += [side(None, "x0", 1), side("i0", "i0x", 1)]
        else:
            side = lambda array, slot: [(array, (slot, k), 0) for k in range(2)]
            operands = [side(own, 0), both(get(f"cl{n}")), side(get(f"i{n}"), 0), both(get(f"cp{n}"))]
            operands += [side(own, 1), side(get(f"i{n}"), 1)]
        leads = ((), (), (2,), (2, 2))
        return product_call(incoming_kernel, operands, IN_SIZES[n], leads, (4, 2 * size, size), "incoming")

    for n in range(count):
        graph.add(f"p{n}", lambda n=n: get(f"j{n}") if n else parts[0], functools.partial(product, n))
        send(f"a{n}", "across", lambda n=n: get(f"p{n}")[3])
    return shared_steps(
        graph,
        IN_GROUPS,
        lambda n, k: get(f"p{n}")[k] + get(f"a{n}")[1, k],
        lambda n: get(f"p{n}")[2] + get(f"a{n}")[0],
    )


def four_by_four(pair, chain, block_mask, w_in, w_gate, w_out, gain_in, gain_out):
    gain_wide = jnp.broadcast_to(gain_out[:, :, None, None], gain_out.shape + (1, pair.shape[1]))
    gate, parts = first_call(chain, block_mask, pair, w_in, w_gate, gain_in)
    products = outgoing(parts)
    middle, gate, parts = middle_call(
        chain, block_mask, pair, gate, products, w_out, gain_wide[0], w_in, w_gate, gain_in
    )
    products = incoming(parts)
    return finish_call(middle, gate, products, w_out, gain_wide[1])


def solution(mesh):
    four = mesh.shape["row"] == 4 and mesh.shape["col"] == 4
    return jax.shard_map(
        four_by_four if four else any_mesh,
        mesh=mesh,
        in_specs=(
            P(("group", "row"), "col", None),
            P("group"),
            P("group", None),
            P(),
            P(),
            P(),
            P(),
            P(),
        ),
        out_specs=P(("group", "row"), "col", None),
        check_vma=False,
    )
```
